32 devices in a mesh: dp: 8 (over z, y), mp: 4 (over x, core).
Axes of the slice: x: 2, y: 2, z: 4, core: 2. Of those that a mesh axis runs over, the one named last changes fastest.
Arguments:
- weights: bfloat16 [14336, 8, 128], P('mp'), may hold values from -0.1875 to 0.1875
- hidden: bfloat16 [2048, 14336], P('dp', 'mp'), may hold values from -6 to 6
- cotangent: bfloat16 [2048, 8192], P('dp', 'mp'), may hold values from -6 to 6
- sketch: float32 [128, 8192], P(None, ('dp', 'mp')), may hold values from -0.046875 to 0.046875
- projection: float32 [128, 4, 3584], P(None, 'mp', 'dp'), may hold values from -0.046875 to 0.046875
- pattern: int32 [112, 8], P('mp'), may hold values from 0 to 63, as said below
Outputs:
- input_grad: bfloat16 [2048, 14336], P('dp', 'mp')
- direction: float32 [4, 3584, 8, 128], P('mp', 'dp')
The draws below stay inside these ranges and needn't reach their ends.
Inputs may be any that keep to these rules, and one draw needn't show every extreme that they name: `pattern`: each block row names 8 different column blocks.
All inputs are finite; a program needn't handle non-finite values.
Results may differ from the reference program's by a relative error of at most 0.001.
Values may be sent and summed in bfloat16 or wider, within the bound.
No kernel may reach another device: no remote copies, remote signals or barrier semaphores. Data moves between devices by JAX's collectives and lax.ppermute only.
A program may use at most 192 MiB of HBM per device.

```python
import math
import jax
import jax.numpy as jnp
from jax import lax

D = 8192
FFW = 14336
BLK = 128
KB = 8
RANK = 128
NS_STEPS = 5
TOKENS = 2048
HBLK = 112
N_MP = 4


def draw_pattern(key, part):
    row_keys = jax.random.split(key, HBLK)

    def one_row(row_key):
        return jax.random.permutation(row_key, D // BLK)[:KB]
    return jax.vmap(one_row)(row_keys).astype(jnp.int32)


def steps_of(key, dims, cuts, smallest, high):
    def one(position, parts):
        draws = jax.random.uniform(jax.random.fold_in(jax.random.fold_in(key, 6), position), (parts,), jnp.float32, smallest / len(cuts), high / len(cuts))
        return jnp.repeat(jnp.exp(draws), dims[position] // parts).reshape((-1,) + (1,) * (len(dims) - position - 1))

    loudness = one(*cuts[0])
    for cut in cuts[1:]:
        loudness = loudness * one(*cut)
    return loudness


def bell_draw(key, shape, width, bound, cuts=(), kind=jnp.bfloat16):
    level = steps_of(key, shape, cuts, -0.22, 0.18) if cuts else 1.0
    entries = jax.random.normal(key, shape, jnp.float32) * width * level
    return jnp.minimum(jnp.maximum(entries, -bound), bound).astype(kind)


def setup_inputs(seed: int = 0) -> dict:
    seeds = jax.random.split(jax.random.key(seed), 7)
    return {
        "weights": bell_draw(seeds[0], (FFW, KB, BLK), (KB * BLK) ** -0.5, 0.1875, ((0, 4),)),
        "hidden": bell_draw(seeds[1], (TOKENS, FFW), 1.0, 6.0, ((0, 8), (1, 4))),
        "cotangent": bell_draw(seeds[2], (TOKENS, D), 1.0, 6.0, ((0, 8), (1, 4))),
        "sketch": bell_draw(seeds[3], (RANK, D), 0.003, 0.046875, ((1, 32),), jnp.float32),
        "projection": bell_draw(seeds[4], (RANK, N_MP, FFW // N_MP), FFW ** -0.5, 0.046875, ((1, 4), (2, 8)), jnp.float32),
        "pattern": draw_pattern(jax.random.fold_in(seeds[6], 71), 0),
    }


shift_eps = 0.0001

def matmul(operand_a, operand_b):
    return jnp.dot(operand_a.astype(jnp.float32), operand_b.astype(jnp.float32), precision=lax.Precision.HIGHEST, preferred_element_type=jnp.float32)

def root_factor(gram):
    identity = jnp.eye(gram.shape[0], dtype=jnp.float32)
    shifted = gram + shift_eps * identity
    frobenius = jnp.sqrt(jnp.sum(shifted * shifted))
    root_iter = shifted / frobenius
    inverse_iter = identity
    for iteration in range(NS_STEPS):
        middle = 0.5 * (3.0 * identity - matmul(inverse_iter, root_iter))
        root_iter = matmul(root_iter, middle)
        inverse_iter = matmul(middle, inverse_iter)
    shifted_root = 0.5 * jnp.sqrt(frobenius) * (root_iter + root_iter.T) + math.sqrt(shift_eps) * identity
    factor = jnp.linalg.cholesky(shifted_root)
    solved = jax.scipy.linalg.cho_solve((factor, True), inverse_iter.T)
    return -solved.T / (math.sqrt(shift_eps) * jnp.sqrt(frobenius))

def reference(weights, hidden, cotangent, sketch, projection, pattern):
    all_tokens = hidden.shape[0]
    cot_blocks = cotangent.reshape(all_tokens, D // BLK, BLK)
    proj_full = projection.reshape(RANK, FFW)
    highest = lax.Precision.HIGHEST

    def grad_row(carry, index):
        cols_row = pattern[index]
        chosen = jnp.take(cot_blocks, cols_row, axis=1).astype(jnp.float32)
        hid_row = lax.dynamic_slice_in_dim(hidden, index * BLK, BLK, 1).astype(jnp.float32)
        weight_row = lax.dynamic_slice_in_dim(weights, index * BLK, BLK, 0).astype(jnp.float32)
        grad_block = jnp.einsum('ti,tkn->ikn', hid_row, chosen, precision=highest) / all_tokens
        back_row = jnp.einsum('tkn,ikn->ti', chosen, weight_row, precision=highest).astype(jnp.bfloat16)
        proj_row = lax.dynamic_slice_in_dim(proj_full, index * BLK, BLK, 1)
        contrib = jnp.einsum('mi,ikn->mkn', proj_row, grad_block, precision=highest)
        carry = carry.at[:, cols_row, :].add(contrib)
        return (carry, (grad_block, back_row))
    start = jnp.zeros((RANK, D // BLK, BLK), jnp.float32)
    compressed, (grads, backs) = lax.scan(grad_row, start, jnp.arange(HBLK, dtype=jnp.int32))
    input_grad = jnp.transpose(backs, (1, 0, 2)).reshape(all_tokens, FFW)
    stacked = jnp.concatenate([sketch, compressed.reshape(RANK, D)], axis=0)
    gram = matmul(stacked, stacked.T)
    mixing = root_factor(gram)
    stacked_blocks = stacked.reshape(2 * RANK, D // BLK, BLK)

    def direction_row(index):
        grad_block = grads[index]
        selected = jnp.take(stacked_blocks, pattern[index], axis=1)
        projected = jnp.einsum('ikn,mkn->im', grad_block, selected, precision=highest)
        mixed = matmul(projected, mixing)
        return grad_block / math.sqrt(shift_eps) + jnp.einsum('im,mkn->ikn', mixed, selected, precision=highest)
    direction = lax.map(direction_row, jnp.arange(HBLK, dtype=jnp.int32))
    return (input_grad, direction.reshape(N_MP, FFW // N_MP, KB, BLK))
```

```python
import functools
import math

import jax
import jax.numpy as jnp
from jax import lax
from jax.experimental import pallas as pl
from jax.experimental.pallas import tpu as pltpu
from jax.sharding import PartitionSpec as P

NS_STEPS = 5
SHIFT_EPS = 0.0001
PROJ_SCALE = 1024.0

BF = jnp.bfloat16
F16 = jnp.float16
F32 = jnp.float32
HIGHEST = lax.Precision.HIGHEST
VMEM = pl.BlockSpec(memory_space=pltpu.VMEM)
ANY = pl.BlockSpec(memory_space=pl.ANY)


def params(mib=48):
    return pltpu.CompilerParams(vmem_limit_bytes=mib * 1024 * 1024)


def dot(a, b):
    return jnp.dot(a, b, preferred_element_type=F32)


def dot_nt(a, b):
    return lax.dot_general(a, b, (((1,), (1,)), ((), ())), preferred_element_type=F32)


def split2(value):
    high = value.astype(BF)
    return high, (value - high.astype(F32)).astype(BF)


def split2_xla(value):
    high = lax.reduce_precision(value, exponent_bits=8, mantissa_bits=7)
    return high.astype(BF), (value - high).astype(BF)


def load_shards(shard_refs, held, sems):
    copies = [
        pltpu.make_async_copy(ref, held.at[i], sems.at[i]) for i, ref in enumerate(shard_refs)
    ]
    for copy in copies:
        copy.start()
    for copy in copies:
        copy.wait()


def column_block(held, base, block, per_shard, block_size):
    shard = block // per_shard
    offset = pl.multiple_of((block - shard * per_shard) * block_size, block_size)
    return held[base + shard, :, pl.ds(offset, block_size)]


def compress_kernel(n_shards, per_shard, scale, pat, *refs):
    shards = refs[:n_shards]
    hid_ref, ph_ref, pl_ref, out_ref, held, sems = refs[n_shards:]
    row = pl.program_id(0)
    blk = out_ref.shape[1]

    @pl.when(row == 0)
    def _():
        load_shards(shards, held, sems)
        out_ref[...] = jnp.zeros_like(out_ref)

    hid = hid_ref[...]
    q = dot(ph_ref[...], hid) + dot(pl_ref[...], hid)
    left = jnp.concatenate(split2(q * scale), axis=0)
    slots = 8
    for j in range(0, slots, 2):
        c0, c1 = pat[row * slots + j], pat[row * slots + j + 1]
        chosen = jnp.concatenate(
            [column_block(held, 0, c, per_shard, blk) for c in (c0, c1)], axis=1
        )
        part = dot(left, chosen)
        part = part[:blk] + part[blk:]
        out_ref[c0] += part[:, :blk]
        out_ref[c1] += part[:, blk:]


def grad_kernel(n_shards, per_shard, blk, pat, *refs):
    shards = refs[: 2 * n_shards]
    own_ref, got_ref, out_ref, top_ref, held, sems = refs[2 * n_shards :]
    row = pl.program_id(0)

    @pl.when(row == 0)
    def _():
        load_shards(shards, held, sems)
        top_ref[...] = jnp.zeros_like(top_ref)

    own, got = own_ref[...].astype(BF), got_ref[...].astype(BF)
    slots = 8
    top = top_ref[...]
    for j in range(0, slots, 2):
        cs = (pat[row * slots + j], pat[row * slots + j + 1])
        part = None
        for base, hid in ((0, own), (n_shards, got)):
            chosen = jnp.concatenate(
                [column_block(held, base, c, per_shard, blk) for c in cs], axis=1
            )
            term = dot(hid, chosen)
            part = term if part is None else part + term
        out_ref[:, j * blk : (j + 2) * blk] = part
        size = jnp.abs(part)
        for i in range(0, part.shape[0], 8):
            top = jnp.maximum(top, size[i : i + 8])
    top_ref[...] = top


def input_grad_kernel(n_shards, per_shard, blk, pat, *refs):
    shards = refs[:n_shards]
    w_ref, out_ref, held, sems = refs[n_shards:]
    row = pl.program_id(0)

    @pl.when(row == 0)
    def _():
        load_shards(shards, held, sems)

    slots = 8
    chosen = jnp.concatenate(
        [column_block(held, 0, pat[row * slots + j], per_shard, blk) for j in range(slots)], axis=1
    )
    out_ref[...] = dot_nt(chosen, w_ref[...]).astype(BF)


def sketch_gram_kernel(sh_ref, sl_ref, out_ref):
    out_ref[...] = jnp.zeros_like(out_ref)
    for s in range(sh_ref.shape[0]):
        high, low = sh_ref[s], sl_ref[s]
        out_ref[...] += dot_nt(high, high) + (dot_nt(high, low) + dot_nt(low, high))


def cross_gram_kernel(ch_ref, cl_ref, sh_ref, sl_ref, out_ref):
    rank = ch_ref.shape[1]
    per = ch_ref.shape[0] // sh_ref.shape[0]
    with_sketch = jnp.zeros((rank, rank), F32)
    with_self = jnp.zeros((rank, rank), F32)
    for s in range(sh_ref.shape[0]):
        high = jnp.concatenate([ch_ref[per * s + b] for b in range(per)], axis=1)
        low = jnp.concatenate([cl_ref[per * s + b] for b in range(per)], axis=1)
        sh, sl = sh_ref[s], sl_ref[s]
        with_sketch += dot_nt(high, sh) + (dot_nt(high, sl) + dot_nt(low, sh))
        with_self += dot_nt(high, high) + (dot_nt(high, low) + dot_nt(low, high))
    out_ref[:, :rank] = with_sketch
    out_ref[:, rank:] = with_self


def mixing_kernel(ss_ref, cross_ref, out_ref):
    rank = ss_ref.shape[0]
    size = 2 * rank
    sqrt_eps = math.sqrt(SHIFT_EPS)

    def mm(a, b):
        return jnp.dot(a, b, precision=HIGHEST, preferred_element_type=F32)

    cross = cross_ref[...]
    gram = jnp.concatenate(
        [jnp.concatenate([ss_ref[...], cross[:, :rank].T], axis=1), cross], axis=0
    )
    rows = lax.broadcasted_iota(jnp.int32, (size, size), 0)
    cols = lax.broadcasted_iota(jnp.int32, (size, size), 1)
    identity = jnp.where(rows == cols, 1.0, 0.0).astype(F32)
    shifted = gram + SHIFT_EPS * identity
    frobenius = jnp.sqrt(jnp.sum(shifted * shifted, keepdims=True))
    root = shifted / frobenius
    inverse = identity
    for step in range(NS_STEPS):
        product = root if step == 0 else mm(inverse, root)
        middle = 0.5 * (3.0 * identity - product)
        root = mm(root, middle)
        inverse = middle if step == 0 else mm(middle, inverse)
    sqrt_fro = jnp.sqrt(frobenius)
    half = 0.5 * sqrt_fro * (root + root.T) + sqrt_eps * identity
    guess = inverse / (sqrt_fro + sqrt_eps * 1.5**NS_STEPS)

    def residual(x):
        r = identity - mm(half, x)
        return r, jnp.max(jnp.abs(r))

    def keep_going(state):
        return jnp.logical_and(state[3] < 48, state[2] > 2e-6)

    def improve(state):
        x, r, _, count = state
        x = x + mm(x, r)
        r, size = residual(x)
        return x, r, size, count + 1

    r, top = residual(guess)
    x, r, _, _ = lax.while_loop(keep_going, improve, (guess, r, top, jnp.int32(0)))
    x = x + mm(x, r)
    out_ref[...] = -mm(inverse, x) / (sqrt_eps * sqrt_fro)


def gathered(held_sk, held_cp, c_sk, c_cp, blk, per):
    shard = c_sk // per
    offset = pl.multiple_of((c_sk - shard * per) * blk, blk)
    return held_sk[shard, :, pl.ds(offset, blk)], held_cp[c_cp]


def project_kernel(per, pat_sk, pat_cp, g_ref, skh, skl, cph, cpl, out_ref):
    row = pl.program_id(0)
    blk = cph.shape[1]
    slots = 8
    rows = g_ref.shape[0]
    total = jnp.zeros(out_ref.shape, F32)
    for k in range(slots):
        c_sk, c_cp = pat_sk[row * slots + k], pat_cp[row * slots + k]
        high = jnp.concatenate(gathered(skh, cph, c_sk, c_cp, blk, per), axis=0)
        low = jnp.concatenate(gathered(skl, cpl, c_sk, c_cp, blk, per), axis=0)
        g = g_ref[:, k * blk : (k + 1) * blk]
        gh = g.astype(BF).astype(F32)
        both = dot_nt(jnp.concatenate([gh, g - gh], axis=0).astype(BF), high)
        total += both[:rows] + both[rows:] + dot_nt(g.astype(BF), low)
    out_ref[...] = total


def direction_kernel(per, pat_sk, pat_cp, g_ref, p_ref, m_ref, skh, skl, cph, cpl, out_ref):
    row = pl.program_id(0)
    blk = cph.shape[1]
    slots = 8
    rows = g_ref.shape[0]
    mixed = jnp.dot(p_ref[...], m_ref[...], precision=HIGHEST, preferred_element_type=F32)
    mixed_high = mixed.astype(BF).astype(F32)
    stacked = jnp.concatenate([mixed_high, mixed - mixed_high], axis=0).astype(BF)
    mixed_bf = mixed.astype(BF)
    for k in range(slots):
        c_sk, c_cp = pat_sk[row * slots + k], pat_cp[row * slots + k]
        high = jnp.concatenate(gathered(skh, cph, c_sk, c_cp, blk, per), axis=0)
        low = jnp.concatenate(gathered(skl, cpl, c_sk, c_cp, blk, per), axis=0)
        both = dot(stacked, high)
        corr = both[:rows] + both[rows:] + dot(mixed_bf, low)
        out_ref[:, k, :] = g_ref[:, k * blk : (k + 1) * blk] * (1.0 / math.sqrt(SHIFT_EPS)) + corr


def cost(flops, moved):
    return pl.CostEstimate(flops=int(flops), bytes_accessed=int(moved), transcendentals=0)


def per_device(weights, hidden, cotangent, sketch, projection, pattern):
    tok_rows = hidden.shape[0]
    mp_rows, slots, blk = weights.shape
    block_rows = mp_rows // blk
    n_dp, n_mp = lax.axis_size("dp"), lax.axis_size("mp")
    dev_rows = mp_rows // n_dp
    all_tokens = tok_rows * n_dp
    rank = sketch.shape[0]
    shard_cols = cotangent.shape[1]
    per_shard = shard_cols // blk
    col_blocks = per_shard * n_mp
    outer = n_dp // 2
    dp, mp = lax.axis_index("dp"), lax.axis_index("mp")
    side = dp % 2

    def swap(x, axis, bit):
        size = lax.axis_size(axis)
        return lax.ppermute(x, axis, [(i, i ^ bit) for i in range(size)])

    x_half = swap(cotangent, "mp", 2)
    y_own = swap(cotangent, "dp", 1)
    own = [cotangent, swap(cotangent, "mp", 1), x_half, swap(x_half, "mp", 1)]
    pattern_rel = jnp.bitwise_xor(pattern, mp * per_shard)

    proj16 = (projection.reshape(rank, dev_rows) * PROJ_SCALE).astype(F16)
    proj_all = lax.all_to_all(
        jnp.broadcast_to(proj16[None], (n_dp, rank, dev_rows)), "dp", 0, 0
    )
    proj_all = proj_all.transpose(1, 0, 2).reshape(rank, mp_rows).astype(F32)
    proj_high, proj_low = split2_xla(proj_all)
    sketch_all = lax.all_gather(sketch.astype(F16), ("dp", "mp"), axis=0, tiled=False)
    width = sketch_all.shape[2]
    if width < blk:
        sketch_all = sketch_all.reshape(col_blocks, blk // width, rank, width)
        sketch_all = sketch_all.transpose(0, 2, 1, 3).reshape(col_blocks, rank, blk)
    sk_high, sk_low = split2_xla(sketch_all.astype(F32))

    hid_t = hidden.T
    hid_parts = hid_t.reshape(outer, 2, dev_rows, tok_rows)
    hid_own = lax.dynamic_index_in_dim(hid_parts, side, 1, keepdims=False)
    hid_send = lax.dynamic_index_in_dim(hid_parts, 1 - side, 1, keepdims=False)

    scratch = lambda n: [
        pltpu.VMEM((n, tok_rows, shard_cols), BF),
        pltpu.SemaphoreType.DMA((n,)),
    ]
    pat_all = pattern_rel.reshape(-1)
    partial_c = pl.pallas_call(
        functools.partial(
            compress_kernel, n_mp, per_shard, 1.0 / (PROJ_SCALE * all_tokens)
        ),
        grid_spec=pltpu.PrefetchScalarGridSpec(
            num_scalar_prefetch=1,
            grid=(block_rows,),
            in_specs=[ANY] * n_mp
            + [
                pl.BlockSpec((blk, tok_rows), lambda i, pat: (i, 0)),
                pl.BlockSpec((rank, blk), lambda i, pat: (0, i)),
                pl.BlockSpec((rank, blk), lambda i, pat: (0, i)),
            ],
            out_specs=pl.BlockSpec((col_blocks, rank, blk), lambda i, pat: (0, 0, 0)),
            scratch_shapes=scratch(n_mp),
        ),
        out_shape=jax.ShapeDtypeStruct((col_blocks, rank, blk), F32),
        compiler_params=params(),
        cost_estimate=cost(4 * mp_rows * slots * blk * tok_rows, 12 << 20),
        name="compress",
    )(pat_all, *own, hid_t, proj_high, proj_low)

    quarters = partial_c.reshape(n_mp, per_shard, rank, blk)
    keep = jnp.stack([quarters[0], quarters[2]])
    sent = swap(jnp.stack([quarters[1], quarters[3]]).astype(F16), "mp", 1)
    keep = keep + sent.astype(F32)
    quarter = keep[0] + swap(keep[1].astype(F16), "mp", 2).astype(F32)
    pieces = quarter.astype(F16).reshape(n_dp, per_shard * rank // n_dp, blk)
    pieces = lax.all_to_all(pieces, "dp", 0, 0)
    piece = jnp.sum(pieces.astype(F32), axis=0).astype(F16)
    quarter16 = lax.all_to_all(jnp.broadcast_to(piece[None], pieces.shape), "dp", 0, 0)
    quarter16 = quarter16.reshape(per_shard, rank, blk)

    sk_per = sk_high.shape[2] // blk
    sk_quarter = col_blocks // sk_per // n_mp
    qh, ql = split2_xla(quarter16.astype(F32))
    cross = pl.pallas_call(
        cross_gram_kernel,
        in_specs=[VMEM] * 4,
        out_specs=VMEM,
        out_shape=jax.ShapeDtypeStruct((rank, 2 * rank), F32),
        compiler_params=params(),
        name="cross_gram",
    )(
        qh,
        ql,
        lax.dynamic_slice_in_dim(sk_high, mp * sk_quarter, sk_quarter, 0),
        lax.dynamic_slice_in_dim(sk_low, mp * sk_quarter, sk_quarter, 0),
    )
    sketch_gram = pl.pallas_call(
        sketch_gram_kernel,
        in_specs=[VMEM] * 2,
        out_specs=VMEM,
        out_shape=jax.ShapeDtypeStruct((rank, rank), F32),
        compiler_params=params(),
        cost_estimate=cost(6 * rank * rank * col_blocks * blk, 4 << 20),
        name="sketch_gram",
    )(sk_high, sk_low)
    cross = cross + swap(cross, "mp", 2)
    cross = cross + swap(cross, "mp", 1)
    mixing = pl.pallas_call(
        mixing_kernel,
        in_specs=[VMEM] * 2,
        out_specs=VMEM,
        out_shape=jax.ShapeDtypeStruct((2 * rank, 2 * rank), F32),
        compiler_params=params(),
        cost_estimate=cost(30 * 12 * (2 * rank) ** 3, 1 << 20),
        name="mixing",
    )(sketch_gram, cross)

    far = swap(quarter16, "mp", 2)
    near = swap(jnp.stack([quarter16, far]), "mp", 1)
    comp16 = jnp.stack([quarter16, near[0], far, near[1]]).reshape(col_blocks, rank, blk)
    cp_high, cp_low = split2_xla(comp16.astype(F32))

    y_x = swap(y_own, "mp", 2)
    y_group = [y_own, swap(y_own, "mp", 1), y_x, swap(y_x, "mp", 1)]
    hid_send, _ = lax.optimization_barrier((hid_send, y_own))
    hid_got = swap(hid_send, "dp", 1)
    group = math.gcd(dev_rows, blk)
    per_dev = dev_rows // group
    half_rows = outer * dev_rows
    hid_type = BF if group % 16 == 0 else F32
    group_start = (
        (2 * jnp.arange(outer, dtype=jnp.int32) + side)[:, None] * dev_rows
        + group * jnp.arange(per_dev, dtype=jnp.int32)[None, :]
    )
    pat_half = jnp.take(pattern_rel, (group_start // blk).reshape(-1), axis=0).reshape(-1)
    grad_half, top = pl.pallas_call(
        functools.partial(grad_kernel, n_mp, per_shard, blk),
        grid_spec=pltpu.PrefetchScalarGridSpec(
            num_scalar_prefetch=1,
            grid=(outer * per_dev,),
            in_specs=[ANY] * (2 * n_mp)
            + [pl.BlockSpec((group, tok_rows), lambda i, pat: (i, 0))] * 2,
            out_specs=[
                pl.BlockSpec((group, slots * blk), lambda i, pat: (i, 0)),
                pl.BlockSpec((8, 2 * blk), lambda i, pat: (0, 0)),
            ],
            scratch_shapes=scratch(2 * n_mp),
        ),
        out_shape=[
            jax.ShapeDtypeStruct((half_rows, slots * blk), F32),
            jax.ShapeDtypeStruct((8, 2 * blk), F32),
        ],
        compiler_params=params(),
        cost_estimate=cost(4 * half_rows * slots * blk * tok_rows, 18 << 20),
        name="pair_grad",
    )(
        pat_half,
        *own,
        *y_group,
        hid_own.reshape(half_rows, tok_rows).astype(hid_type),
        hid_got.reshape(half_rows, tok_rows).astype(hid_type),
    )
    biggest = jnp.maximum(jnp.max(top), 1e-30)
    scale = 16384.0 / biggest
    packed = (grad_half * scale).astype(F16).reshape(outer, dev_rows, slots * blk)
    lanes = [[2 * i + s for i in range(outer)] for s in range(2)]
    packed = lax.all_to_all(packed, "dp", 0, 0, axis_index_groups=lanes)
    unscale = lax.all_to_all(
        jnp.broadcast_to(biggest / (16384.0 * all_tokens), (outer, 8, 128)),
        "dp", 0, 0, axis_index_groups=lanes,
    )
    grad = jnp.sum(packed.astype(F32) * unscale[:, :1, :1], axis=0)

    input_grad = pl.pallas_call(
        functools.partial(input_grad_kernel, n_mp, per_shard, blk),
        grid_spec=pltpu.PrefetchScalarGridSpec(
            num_scalar_prefetch=1,
            grid=(block_rows,),
            in_specs=[ANY] * n_mp + [pl.BlockSpec((blk, slots * blk), lambda i, pat: (i, 0))],
            out_specs=pl.BlockSpec((tok_rows, blk), lambda i, pat: (0, i)),
            scratch_shapes=scratch(n_mp),
        ),
        out_shape=jax.ShapeDtypeStruct((tok_rows, mp_rows), BF),
        compiler_params=params(),
        cost_estimate=cost(2 * mp_rows * slots * blk * tok_rows, 14 << 20),
        name="input_grad",
    )(pat_all, *own, weights.reshape(mp_rows, slots * blk))

    my_start = dp * dev_rows + group * jnp.arange(per_dev, dtype=jnp.int32)
    pat_abs = jnp.take(pattern, my_start // blk, axis=0).reshape(-1)
    pat_rel = jnp.bitwise_xor(pat_abs, mp * per_shard)
    projected = pl.pallas_call(
        functools.partial(project_kernel, sk_per),
        grid_spec=pltpu.PrefetchScalarGridSpec(
            num_scalar_prefetch=2,
            grid=(per_dev,),
            in_specs=[pl.BlockSpec((group, slots * blk), lambda i, a, b: (i, 0))] + [VMEM] * 4,
            out_specs=pl.BlockSpec((group, 2 * rank), lambda i, a, b: (i, 0)),
        ),
        out_shape=jax.ShapeDtypeStruct((dev_rows, 2 * rank), F32),
        compiler_params=params(),
        cost_estimate=cost(6 * dev_rows * slots * blk * 2 * rank, 12 << 20),
        name="project",
    )(pat_abs, pat_rel, grad, sk_high, sk_low, cp_high, cp_low)
    direction = pl.pallas_call(
        functools.partial(direction_kernel, sk_per),
        grid_spec=pltpu.PrefetchScalarGridSpec(
            num_scalar_prefetch=2,
            grid=(per_dev,),
            in_specs=[
                pl.BlockSpec((group, slots * blk), lambda i, a, b: (i, 0)),
                pl.BlockSpec((group, 2 * rank), lambda i, a, b: (i, 0)),
            ]
            + [VMEM] * 5,
            out_specs=pl.BlockSpec((group, slots, blk), lambda i, a, b: (i, 0, 0)),
        ),
        out_shape=jax.ShapeDtypeStruct((dev_rows, slots, blk), F32),
        compiler_params=params(),
        cost_estimate=cost(6 * dev_rows * slots * blk * 2 * rank, 14 << 20),
        name="direction",
    )(pat_abs, pat_rel, grad, projected, mixing, sk_high, sk_low, cp_high, cp_low)
    return (input_grad, direction.reshape(1, dev_rows, slots, blk))


def solution(mesh):
    return jax.shard_map(
        per_device,
        mesh=mesh,
        in_specs=(
            P("mp", None, None),
            P("dp", "mp"),
            P("dp", "mp"),
            P(None, ("dp", "mp")),
            P(None, "mp", "dp"),
            P("mp", None),
        ),
        out_specs=(P("dp", "mp"), P("mp", "dp", None, None)),
        check_vma=False,
    )
```

```python
import functools
import math

import jax
import jax.numpy as jnp
from jax import lax
from jax.experimental import pallas as pl
from jax.experimental.pallas import tpu as pltpu
from jax.sharding import PartitionSpec as P

NS_STEPS = 5
SHIFT_EPS = 0.0001
PROJ_SCALE = 1024.0
SLOTS = 8

BF = jnp.bfloat16
F16 = jnp.float16
F32 = jnp.float32
HIGHEST = lax.Precision.HIGHEST
VMEM = pl.BlockSpec(memory_space=pltpu.VMEM)
ANY = pl.BlockSpec(memory_space=pl.ANY)


SMALL = pl.CostEstimate(flops=1, bytes_accessed=1, transcendentals=0)


def params(mib=48):
    return pltpu.CompilerParams(vmem_limit_bytes=mib * 1024 * 1024)


def dot(a, b):
    return jnp.dot(a, b, preferred_element_type=F32)


def dot_nt(a, b):
    return lax.dot_general(a, b, (((1,), (1,)), ((), ())), preferred_element_type=F32)


def split2(value):
    high = value.astype(BF)
    return high, (value - high.astype(F32)).astype(BF)


def split2_xla(value):
    high = lax.reduce_precision(value, exponent_bits=8, mantissa_bits=7)
    return high.astype(BF), (value - high).astype(BF)


def load_all(pairs, sems):
    copies = [pltpu.make_async_copy(src, dst, sems.at[i]) for i, (src, dst) in enumerate(pairs)]
    for copy in copies:
        copy.start()
    for copy in copies:
        copy.wait()


def column_block(held, block, per_shard, size):
    shard = block // per_shard
    offset = pl.multiple_of((block - shard * per_shard) * size, size)
    return held[shard, :, pl.ds(offset, size)]


def compress_kernel(n_shards, per_shard, scale, per_step, pat, *refs):
    shards = refs[:n_shards]
    hid_ref, proj_ref, out_ref, held, sems = refs[n_shards:]
    blk = out_ref.shape[1]

    @pl.when(pl.program_id(0) == 0)
    def _():
        load_all([(ref, held.at[i]) for i, ref in enumerate(shards)], sems)
        out_ref[...] = jnp.zeros_like(out_ref)

    for u in range(per_step):
        row = pl.program_id(0) * per_step + u
        span = slice(u * blk, (u + 1) * blk)
        hid = hid_ref[span, :]
        ph, pl_ = split2(proj_ref[:, span])
        left = jnp.concatenate(split2((dot(ph, hid) + dot(pl_, hid)) * scale), axis=0)
        cols = [pat[row * SLOTS + j] for j in range(SLOTS)]
        parts = []
        for j in range(0, SLOTS, 2):
            chosen = jnp.concatenate(
                [column_block(held, c, per_shard, blk) for c in cols[j : j + 2]], axis=1
            )
            part = dot(left, chosen)
            parts.append(part[:blk] + part[blk:])
        sums = [
            out_ref[c] + parts[j // 2][:, (j % 2) * blk : (j % 2 + 1) * blk]
            for j, c in enumerate(cols)
        ]
        for c, total in zip(cols, sums):
            out_ref[c] = total


def grad_kernel(n_shards, per_shard, blk, window, n_windows, starts, pat, *refs):
    shards = refs[: 2 * n_shards]
    own_ref, got_ref, out_ref, top_ref, held, sems = refs[2 * n_shards :]
    toks = own_ref.shape[1]

    @pl.when(pl.program_id(0) == 0)
    def _():
        load_all(
            [
                (ref, held.at[i % n_shards, pl.ds(i // n_shards * toks, toks)])
                for i, ref in enumerate(shards)
            ],
            sems,
        )
        top_ref[...] = jnp.zeros_like(top_ref)

    top = top_ref[...]
    for w in range(n_windows):
        index = pl.program_id(0) * n_windows + w
        rows = pl.ds(pl.multiple_of(starts[index], window // 2 if window >= 32 else 8), window)
        hid = jnp.concatenate([own_ref[rows, :], got_ref[rows, :]], axis=1).astype(BF)
        for j in range(0, SLOTS, 2):
            chosen = jnp.concatenate(
                [column_block(held, pat[index * SLOTS + j + i], per_shard, blk) for i in (0, 1)],
                axis=1,
            )
            part = dot(hid, chosen)
            out_ref[rows, j * blk : (j + 2) * blk] = part
            size = jnp.abs(part)
            for i in range(0, window, 8):
                top = jnp.maximum(top, size[i : i + 8])
    top_ref[...] = top


def input_grad_kernel(n_shards, per_shard, blk, per_step, pat, *refs):
    shards = refs[:n_shards]
    w_ref, out_ref, held, sems = refs[n_shards:]

    @pl.when(pl.program_id(0) == 0)
    def _():
        load_all([(ref, held.at[i]) for i, ref in enumerate(shards)], sems)

    for u in range(per_step):
        row = pl.program_id(0) * per_step + u
        chosen = jnp.concatenate(
            [column_block(held, pat[row * SLOTS + j], per_shard, blk) for j in range(SLOTS)], axis=1
        )
        span = slice(u * blk, (u + 1) * blk)
        out_ref[:, span] = dot_nt(chosen, w_ref[span, :]).astype(BF)


def sketch_gram_kernel(sh_ref, sl_ref, out_ref):
    out_ref[...] = jnp.zeros_like(out_ref)
    for s in range(sh_ref.shape[0]):
        high, low = sh_ref[s], sl_ref[s]
        out_ref[...] += dot_nt(high, high) + (dot_nt(high, low) + dot_nt(low, high))


def cross_gram_kernel(ch_ref, cl_ref, sh_ref, sl_ref, out_ref):
    rank = ch_ref.shape[1]
    per = ch_ref.shape[0] // sh_ref.shape[0]
    with_sketch = jnp.zeros((rank, rank), F32)
    with_self = jnp.zeros((rank, rank), F32)
    for s in range(sh_ref.shape[0]):
        high = jnp.concatenate([ch_ref[per * s + b] for b in range(per)], axis=1)
        low = jnp.concatenate([cl_ref[per * s + b] for b in range(per)], axis=1)
        sh, sl = sh_ref[s], sl_ref[s]
        with_sketch += dot_nt(high, sh) + (dot_nt(high, sl) + dot_nt(low, sh))
        with_self += dot_nt(high, high) + (dot_nt(high, low) + dot_nt(low, high))
    out_ref[:, :rank] = with_sketch
    out_ref[:, rank:] = with_self


def mixing_kernel(ss_ref, cross_ref, out_ref):
    rank = ss_ref.shape[0]
    size = 2 * rank
    sqrt_eps = math.sqrt(SHIFT_EPS)

    def mm(a, b):
        return jnp.dot(a, b, precision=HIGHEST, preferred_element_type=F32)

    cross = cross_ref[...]
    gram = jnp.concatenate(
        [jnp.concatenate([ss_ref[...], cross[:, :rank].T], axis=1), cross], axis=0
    )
    rows = lax.broadcasted_iota(jnp.int32, (size, size), 0)
    cols = lax.broadcasted_iota(jnp.int32, (size, size), 1)
    identity = jnp.where(rows == cols, 1.0, 0.0).astype(F32)
    shifted = gram + SHIFT_EPS * identity
    frobenius = jnp.sqrt(jnp.sum(shifted * shifted, keepdims=True))
    root = shifted / frobenius
    inverse = identity
    for step in range(NS_STEPS):
        product = root if step == 0 else mm(inverse, root)
        middle = 0.5 * (3.0 * identity - product)
        root = mm(root, middle)
        inverse = middle if step == 0 else mm(middle, inverse)
    sqrt_fro = jnp.sqrt(frobenius)
    half = 0.5 * sqrt_fro * (root + root.T) + sqrt_eps * identity
    guess = inverse / (sqrt_fro + sqrt_eps * 1.5**NS_STEPS)

    def residual(x):
        r = identity - mm(half, x)
        return r, jnp.max(jnp.abs(r))

    def keep_going(state):
        return jnp.logical_and(state[3] < 48, state[2] > 2e-6)

    def improve(state):
        x, r, _, count = state
        x = x + mm(x, r)
        r, size = residual(x)
        return x, r, size, count + 1

    r, top = residual(guess)
    x, r, _, _ = lax.while_loop(keep_going, improve, (guess, r, top, jnp.int32(0)))
    x = x + mm(x, r)
    out_ref[...] = -mm(inverse, x) / (sqrt_eps * sqrt_fro)


def direction_kernel(per, window, n_windows, starts, pat_sk, pat_cp, *refs):
    g_ref, m_ref, skh, skl = refs[:4]
    parts, (out_ref, cph, cpl, sems) = refs[4:-4], refs[-4:]
    blk = cph.shape[2]
    half = len(parts) // 2
    pairs, at = [], 0
    for i in range(half):
        size = parts[i].shape[0]
        pairs += [(parts[i], cph.at[pl.ds(at, size)]), (parts[half + i], cpl.at[pl.ds(at, size)])]
        at += size
    load_all(pairs, sems)

    def gathered(sk, cp, c_sk, c_cp):
        shard = c_sk // per
        offset = pl.multiple_of((c_sk - shard * per) * blk, blk)
        return jnp.concatenate([sk[shard, :, pl.ds(offset, blk)], cp[c_cp]], axis=0)

    for w in range(n_windows):
        rows = pl.ds(pl.multiple_of(starts[w], window // 2 if window >= 32 else 8), window)
        cols = [(pat_sk[w * SLOTS + k], pat_cp[w * SLOTS + k]) for k in range(SLOTS)]
        g = g_ref[rows, :]
        g_high = g.astype(BF).astype(F32)
        g_both = jnp.concatenate([g_high, g - g_high], axis=0).astype(BF)
        high = [gathered(skh, cph, *c) for c in cols]
        low = [gathered(skl, cpl, *c) for c in cols]
        both = dot_nt(g_both, jnp.concatenate(high, axis=1))
        projected = both[:window] + both[window:]
        projected += dot_nt(g_high.astype(BF), jnp.concatenate(low, axis=1))
        mixed = jnp.dot(projected, m_ref[...], precision=HIGHEST, preferred_element_type=F32)
        mixed_high = mixed.astype(BF).astype(F32)
        mixed_both = jnp.concatenate([mixed_high, mixed - mixed_high], axis=0).astype(BF)
        for k in range(0, SLOTS, 2):
            both = dot(mixed_both, jnp.concatenate(high[k : k + 2], axis=1))
            corr = both[:window] + both[window:]
            corr += dot(mixed_high.astype(BF), jnp.concatenate(low[k : k + 2], axis=1))
            corr += g[:, k * blk : (k + 2) * blk] * (1.0 / math.sqrt(SHIFT_EPS))
            out_ref[rows, k, :] = corr[:, :blk]
            out_ref[rows, k + 1, :] = corr[:, blk:]


def windows_of(start, dev_rows, blk):
    group = math.gcd(dev_rows, blk)
    if dev_rows % blk == blk // 2 and dev_rows > blk:
        whole = dev_rows // blk
        odd = (start // group) % 2
        later = odd * group + blk * jnp.arange(whole, dtype=jnp.int32)
        first = jnp.where(odd == 1, 0, dev_rows - blk)
        first_row = jnp.where(odd == 1, start, start + dev_rows - group)
        starts = jnp.concatenate([first[None], later])
        inside = jnp.concatenate([first_row[None], start + later])
        return blk, starts.astype(jnp.int32), (inside // blk).astype(jnp.int32)
    starts = group * jnp.arange(dev_rows // group, dtype=jnp.int32)
    return group, starts, (start + starts) // blk


def per_device(weights, hidden, cotangent, sketch, projection, pattern):
    tok_rows = hidden.shape[0]
    mp_rows, slots, blk = weights.shape
    block_rows = mp_rows // blk
    n_dp, n_mp = lax.axis_size("dp"), lax.axis_size("mp")
    dev_rows = mp_rows // n_dp
    all_tokens = tok_rows * n_dp
    rank = sketch.shape[0]
    shard_cols = cotangent.shape[1]
    per_shard = shard_cols // blk
    col_blocks = per_shard * n_mp
    outer = n_dp // 2
    per_step = 4 if block_rows % 4 == 0 else 1
    dp, mp = lax.axis_index("dp"), lax.axis_index("mp")
    side = dp % 2

    def swap(x, axis, bit):
        size = lax.axis_size(axis)
        return lax.ppermute(x, axis, [(i, i ^ bit) for i in range(size)])

    def after(x, *others):
        return lax.optimization_barrier((x, *others))[0]

    def over_dp(x):
        return lax.all_to_all(jnp.broadcast_to(x[None], (n_dp, *x.shape)), "dp", 0, 0)

    x_half = swap(cotangent, "mp", 2)
    y_own = swap(cotangent, "dp", 1)
    core_half = swap(cotangent, "mp", 1)
    y_x = swap(y_own, "mp", 2)
    own = [cotangent, core_half, x_half, swap(x_half, "mp", 1)]
    pattern_rel = jnp.bitwise_xor(pattern, mp * per_shard)

    proj16 = (projection.reshape(rank, dev_rows) * PROJ_SCALE).astype(F16)
    proj_all = over_dp(after(proj16, core_half))
    proj_all = proj_all.transpose(1, 0, 2).reshape(rank, mp_rows).astype(F32)

    hid_t = hidden.T
    hid_parts = hid_t.reshape(outer, 2, dev_rows, tok_rows)
    hid_own = lax.dynamic_index_in_dim(hid_parts, side, 1, keepdims=False)
    hid_send = lax.dynamic_index_in_dim(hid_parts, 1 - side, 1, keepdims=False)
    hid_got = swap(after(hid_send, y_own), "dp", 1)

    pat_all = pattern_rel.reshape(-1)
    partial_c = pl.pallas_call(
        functools.partial(
            compress_kernel, n_mp, per_shard, 1.0 / (PROJ_SCALE * all_tokens), per_step
        ),
        grid_spec=pltpu.PrefetchScalarGridSpec(
            num_scalar_prefetch=1,
            grid=(block_rows // per_step,),
            in_specs=[ANY] * n_mp
            + [
                pl.BlockSpec((per_step * blk, tok_rows), lambda i, pat: (i, 0)),
                pl.BlockSpec((rank, per_step * blk), lambda i, pat: (0, i)),
            ],
            out_specs=pl.BlockSpec((col_blocks, rank, blk), lambda i, pat: (0, 0, 0)),
            scratch_shapes=[
                pltpu.VMEM((n_mp, tok_rows, shard_cols), BF),
                pltpu.SemaphoreType.DMA((n_mp,)),
            ],
        ),
        out_shape=jax.ShapeDtypeStruct((col_blocks, rank, blk), F32),
        compiler_params=params(),
        cost_estimate=SMALL,
        name="compress",
    )(pat_all, *own, hid_t, proj_all)

    quarters = partial_c.reshape(n_mp, per_shard, rank, blk)
    sent = swap(jnp.stack([quarters[1], quarters[3]]).astype(F16), "mp", 1)
    far_half = (quarters[2] + sent[1].astype(F32)).astype(F16)
    quarter = (quarters[0] + sent[0].astype(F32)) + swap(far_half, "mp", 2).astype(F32)
    pieces = quarter.astype(F16).reshape(n_dp, per_shard * rank // n_dp, blk)
    pieces = lax.all_to_all(pieces, "dp", 0, 0)
    piece = jnp.sum(pieces.astype(F32), axis=0).astype(F16)
    quarter16 = over_dp(piece).reshape(per_shard, rank, blk)

    sk_own = over_dp(after(sketch.astype(F16), sent))
    sk_far = swap(sk_own, "mp", 2)
    sk_near = swap(jnp.stack([sk_own, sk_far]), "mp", 1)
    sk_rel = jnp.stack([sk_own, sk_near[0], sk_far, sk_near[1]])
    sk_abs = jnp.take(sk_rel, jnp.bitwise_xor(jnp.arange(n_mp, dtype=jnp.int32), mp), axis=0)
    width = sketch.shape[1]
    if width < blk:
        sketch_all = sk_abs.reshape(n_mp, col_blocks, blk // width // n_mp, rank, width)
        sketch_all = sketch_all.transpose(1, 3, 2, 0, 4).reshape(col_blocks, rank, blk)
    else:
        sketch_all = sk_abs.swapaxes(0, 1).reshape(n_dp * n_mp, rank, width)
    sk_high, sk_low = split2_xla(sketch_all.astype(F32))

    sk_per = sk_high.shape[2] // blk
    sk_quarter = col_blocks // sk_per // n_mp
    qh, ql = split2_xla(quarter16.astype(F32))
    cross = pl.pallas_call(
        cross_gram_kernel,
        in_specs=[VMEM] * 4,
        out_specs=VMEM,
        out_shape=jax.ShapeDtypeStruct((rank, 2 * rank), F32),
        compiler_params=params(),
        cost_estimate=SMALL,
        name="cross_gram",
    )(
        qh,
        ql,
        lax.dynamic_slice_in_dim(sk_high, mp * sk_quarter, sk_quarter, 0),
        lax.dynamic_slice_in_dim(sk_low, mp * sk_quarter, sk_quarter, 0),
    )
    sketch_gram = pl.pallas_call(
        sketch_gram_kernel,
        in_specs=[VMEM] * 2,
        out_specs=VMEM,
        out_shape=jax.ShapeDtypeStruct((rank, rank), F32),
        compiler_params=params(),
        cost_estimate=SMALL,
        name="sketch_gram",
    )(sk_high, sk_low)
    cross = cross + swap(cross, "mp", 2)
    cross = cross + swap(cross, "mp", 1)
    mixing = pl.pallas_call(
        mixing_kernel,
        in_specs=[VMEM] * 2,
        out_specs=VMEM,
        out_shape=jax.ShapeDtypeStruct((2 * rank, 2 * rank), F32),
        compiler_params=params(),
        cost_estimate=SMALL,
        name="mixing",
    )(sketch_gram, cross)

    far = swap(after(quarter16, cross), "mp", 2)
    near = swap(jnp.stack([quarter16, far]), "mp", 1)
    fh, fl = split2_xla(far.astype(F32))
    nh, nl = split2_xla(near.astype(F32))
    comp_parts = [qh, nh[0], fh, nh[1], ql, nl[0], fl, nl[1]]

    y_group = [y_own, swap(y_own, "mp", 1), y_x, swap(y_x, "mp", 1)]
    half_rows = outer * dev_rows
    devices = 2 * jnp.arange(outer, dtype=jnp.int32) + side
    window, _, _ = windows_of(dp * dev_rows, dev_rows, blk)
    window_starts, window_blocks = jax.vmap(lambda d: windows_of(d * dev_rows, dev_rows, blk)[1:])(
        devices
    )
    n_windows = window_starts.shape[1]
    pat_half = jnp.take(pattern_rel, window_blocks.reshape(-1), axis=0).reshape(-1)
    hid_type = BF if window % 32 == 0 else F32
    grad_half, top = pl.pallas_call(
        functools.partial(grad_kernel, n_mp, per_shard, blk, window, n_windows),
        grid_spec=pltpu.PrefetchScalarGridSpec(
            num_scalar_prefetch=2,
            grid=(outer,),
            in_specs=[ANY] * (2 * n_mp)
            + [pl.BlockSpec((dev_rows, tok_rows), lambda i, a, b: (i, 0))] * 2,
            out_specs=[
                pl.BlockSpec((dev_rows, slots * blk), lambda i, a, b: (i, 0)),
                pl.BlockSpec((8, 2 * blk), lambda i, a, b: (0, 0)),
            ],
            scratch_shapes=[
                pltpu.VMEM((n_mp, 2 * tok_rows, shard_cols), BF),
                pltpu.SemaphoreType.DMA((2 * n_mp,)),
            ],
        ),
        out_shape=[
            jax.ShapeDtypeStruct((half_rows, slots * blk), F32),
            jax.ShapeDtypeStruct((8, 2 * blk), F32),
        ],
        compiler_params=params(),
        cost_estimate=SMALL,
        name="pair_grad",
    )(
        window_starts.reshape(-1),
        pat_half,
        *own,
        *y_group,
        hid_own.reshape(half_rows, tok_rows).astype(hid_type),
        hid_got.reshape(half_rows, tok_rows).astype(hid_type),
    )
    biggest = jnp.maximum(jnp.max(top), 1e-30)
    scale = 16384.0 / biggest
    packed = (grad_half * scale).astype(F16).reshape(outer, dev_rows, slots * blk)
    lanes = [[2 * i + s for i in range(outer)] for s in range(2)]
    unscale = lax.all_to_all(
        jnp.broadcast_to(biggest / (16384.0 * all_tokens), (outer, 8, 128)),
        "dp", 0, 0, axis_index_groups=lanes,
    )
    packed = lax.all_to_all(packed, "dp", 0, 0, axis_index_groups=lanes)
    grad = jnp.sum(packed.astype(F32) * unscale[:, :1, :1], axis=0)

    input_grad = pl.pallas_call(
        functools.partial(input_grad_kernel, n_mp, per_shard, blk, per_step),
        grid_spec=pltpu.PrefetchScalarGridSpec(
            num_scalar_prefetch=1,
            grid=(block_rows // per_step,),
            in_specs=[ANY] * n_mp
            + [pl.BlockSpec((per_step * blk, slots * blk), lambda i, pat: (i, 0))],
            out_specs=pl.BlockSpec((tok_rows, per_step * blk), lambda i, pat: (0, i)),
            scratch_shapes=[
                pltpu.VMEM((n_mp, tok_rows, shard_cols), BF),
                pltpu.SemaphoreType.DMA((n_mp,)),
            ],
        ),
        out_shape=jax.ShapeDtypeStruct((tok_rows, mp_rows), BF),
        compiler_params=params(),
        cost_estimate=SMALL,
        name="input_grad",
    )(pat_all, *own, weights.reshape(mp_rows, slots * blk))

    _, my_starts, my_blocks = windows_of(dp * dev_rows, dev_rows, blk)
    pat_abs = jnp.take(pattern, my_blocks, axis=0).reshape(-1)
    pat_rel = jnp.bitwise_xor(pat_abs, mp * per_shard)
    smem = pl.BlockSpec(memory_space=pltpu.SMEM)
    direction = pl.pallas_call(
        functools.partial(direction_kernel, sk_per, window, n_windows),
        in_specs=[smem] * 3 + [VMEM] * 4 + [ANY] * len(comp_parts),
        out_specs=VMEM,
        out_shape=jax.ShapeDtypeStruct((dev_rows, slots, blk), F32),
        scratch_shapes=[
            pltpu.VMEM((col_blocks, rank, blk), BF),
            pltpu.VMEM((col_blocks, rank, blk), BF),
            pltpu.SemaphoreType.DMA((len(comp_parts),)),
        ],
        compiler_params=params(),
        cost_estimate=SMALL,
        name="direction",
    )(my_starts, pat_abs, pat_rel, grad, mixing, sk_high, sk_low, *comp_parts)
    return (input_grad, direction.reshape(1, dev_rows, slots, blk))


def solution(mesh):
    return jax.shard_map(
        per_device,
        mesh=mesh,
        in_specs=(
            P("mp", None, None),
            P("dp", "mp"),
            P("dp", "mp"),
            P(None, ("dp", "mp")),
            P(None, "mp", "dp"),
            P("mp", None),
        ),
        out_specs=(P("dp", "mp"), P("mp", "dp", None, None)),
        check_vma=False,
    )
```

```python
import functools
import math

import jax
import jax.numpy as jnp
from jax import lax
from jax.experimental import pallas as pl
from jax.experimental.pallas import tpu as pltpu
from jax.sharding import PartitionSpec as P

NS_STEPS = 5
SHIFT_EPS = 0.0001
PROJ_SCALE = 1024.0
SLOTS = 8

BF = jnp.bfloat16
F16 = jnp.float16
F32 = jnp.float32
HIGHEST = lax.Precision.HIGHEST
VMEM = pl.BlockSpec(memory_space=pltpu.VMEM)
ANY = pl.BlockSpec(memory_space=pl.ANY)


SMALL = pl.CostEstimate(flops=1, bytes_accessed=1, transcendentals=0)


def params(mib=48):
    return pltpu.CompilerParams(vmem_limit_bytes=mib * 1024 * 1024)


def dot(a, b):
    return jnp.dot(a, b, preferred_element_type=F32)


def dot_nt(a, b):
    return lax.dot_general(a, b, (((1,), (1,)), ((), ())), preferred_element_type=F32)


def split2(value):
    high = value.astype(BF)
    return high, (value - high.astype(F32)).astype(BF)


def split2_xla(value):
    high = lax.reduce_precision(value, exponent_bits=8, mantissa_bits=7)
    return high.astype(BF), (value - high).astype(BF)


def load_all(pairs, sems):
    copies = [pltpu.make_async_copy(src, dst, sems.at[i]) for i, (src, dst) in enumerate(pairs)]
    for copy in copies:
        copy.start()
    for copy in copies:
        copy.wait()


def column_block(held, block, per_shard, size):
    shard = block // per_shard
    offset = pl.multiple_of((block - shard * per_shard) * size, size)
    return held[shard, :, pl.ds(offset, size)]


def compress_kernel(n_shards, per_shard, scale, per_step, pat, pat_out, *refs):
    shards = refs[:n_shards]
    hid_ref, proj_ref, out_ref, held, sems = refs[n_shards:]
    blk = out_ref.shape[1]

    @pl.when(pl.program_id(0) == 0)
    def _():
        load_all([(ref, held.at[i]) for i, ref in enumerate(shards)], sems)
        out_ref[...] = jnp.zeros_like(out_ref)

    for u in range(per_step):
        row = pl.program_id(0) * per_step + u
        span = slice(u * blk, (u + 1) * blk)
        hid = hid_ref[span, :]
        ph, pl_ = split2(proj_ref[:, span])
        left = jnp.concatenate(split2((dot(ph, hid) + dot(pl_, hid)) * scale), axis=0)
        cols = [pat[row * SLOTS + j] for j in range(SLOTS)]
        parts = []
        for j in range(0, SLOTS, 2):
            chosen = jnp.concatenate(
                [column_block(held, c, per_shard, blk) for c in cols[j : j + 2]], axis=1
            )
            part = dot(left, chosen)
            parts.append(part[:blk] + part[blk:])
        outs = [pat_out[row * SLOTS + j] for j in range(SLOTS)]
        sums = [
            out_ref[c] + parts[j // 2][:, (j % 2) * blk : (j % 2 + 1) * blk]
            for j, c in enumerate(outs)
        ]
        for c, total in zip(outs, sums):
            out_ref[c] = total


def grad_kernel(n_shards, per_shard, blk, window, n_windows, starts, pat, scale, *refs):
    shards = refs[: 2 * n_shards]
    own_ref, got_ref, out_ref, held, sems = refs[2 * n_shards :]
    toks = own_ref.shape[1]

    @pl.when(pl.program_id(0) == 0)
    def _():
        load_all(
            [
                (ref, held.at[i % n_shards, pl.ds(i // n_shards * toks, toks)])
                for i, ref in enumerate(shards)
            ],
            sems,
        )

    for w in range(n_windows):
        index = pl.program_id(0) * n_windows + w
        rows = pl.ds(pl.multiple_of(starts[index], window // 2 if window >= 32 else 8), window)
        hid = jnp.concatenate([own_ref[rows, :], got_ref[rows, :]], axis=1).astype(BF)
        for j in range(0, SLOTS, 2):
            chosen = jnp.concatenate(
                [column_block(held, pat[index * SLOTS + j + i], per_shard, blk) for i in (0, 1)],
                axis=1,
            )
            out_ref[rows, j * blk : (j + 2) * blk] = dot(hid, chosen) * scale[0]


def input_grad_kernel(n_shards, per_shard, blk, per_step, pat, *refs):
    shards = refs[:n_shards]
    w_ref, out_ref, held, sems = refs[n_shards:]

    @pl.when(pl.program_id(0) == 0)
    def _():
        load_all([(ref, held.at[i]) for i, ref in enumerate(shards)], sems)

    for u in range(per_step):
        row = pl.program_id(0) * per_step + u
        chosen = jnp.concatenate(
            [column_block(held, pat[row * SLOTS + j], per_shard, blk) for j in range(SLOTS)], axis=1
        )
        span = slice(u * blk, (u + 1) * blk)
        out_ref[:, span] = dot_nt(chosen, w_ref[span, :]).astype(BF)


def sketch_gram_kernel(sh_ref, sl_ref, out_ref):
    out_ref[...] = jnp.zeros_like(out_ref)
    for s in range(sh_ref.shape[0]):
        high, low = sh_ref[s], sl_ref[s]
        out_ref[...] += dot_nt(high, high) + (dot_nt(high, low) + dot_nt(low, high))


def cross_gram_kernel(ch_ref, cl_ref, sh_ref, sl_ref, out_ref):
    rank = ch_ref.shape[1]
    per = ch_ref.shape[0] // sh_ref.shape[0]
    with_sketch = jnp.zeros((rank, rank), F32)
    with_self = jnp.zeros((rank, rank), F32)
    for s in range(sh_ref.shape[0]):
        high = jnp.concatenate([ch_ref[per * s + b] for b in range(per)], axis=1)
        low = jnp.concatenate([cl_ref[per * s + b] for b in range(per)], axis=1)
        sh, sl = sh_ref[s], sl_ref[s]
        with_sketch += dot_nt(high, sh) + (dot_nt(high, sl) + dot_nt(low, sh))
        with_self += dot_nt(high, high) + (dot_nt(high, low) + dot_nt(low, high))
    out_ref[:, :rank] = with_sketch
    out_ref[:, rank:] = with_self


def mixing_kernel(ss_ref, cross_ref, out_ref):
    rank = ss_ref.shape[0]
    size = 2 * rank
    sqrt_eps = math.sqrt(SHIFT_EPS)

    def mm(a, b):
        return jnp.dot(a, b, precision=HIGHEST, preferred_element_type=F32)

    cross = cross_ref[...]
    gram = jnp.concatenate(
        [jnp.concatenate([ss_ref[...], cross[:, :rank].T], axis=1), cross], axis=0
    )
    rows = lax.broadcasted_iota(jnp.int32, (size, size), 0)
    cols = lax.broadcasted_iota(jnp.int32, (size, size), 1)
    identity = jnp.where(rows == cols, 1.0, 0.0).astype(F32)
    shifted = gram + SHIFT_EPS * identity
    frobenius = jnp.sqrt(jnp.sum(shifted * shifted, keepdims=True))
    root = shifted / frobenius
    inverse = identity
    for step in range(NS_STEPS):
        product = root if step == 0 else mm(inverse, root)
        middle = 0.5 * (3.0 * identity - product)
        root = mm(root, middle)
        inverse = middle if step == 0 else mm(middle, inverse)
    sqrt_fro = jnp.sqrt(frobenius)
    half = 0.5 * sqrt_fro * (root + root.T) + sqrt_eps * identity
    guess = inverse / (sqrt_fro + sqrt_eps * 1.5**NS_STEPS)

    def residual(x):
        r = identity - mm(half, x)
        return r, jnp.max(jnp.abs(r))

    def keep_going(state):
        return jnp.logical_and(state[3] < 48, state[2] > 2e-6)

    def improve(state):
        x, r, _, count = state
        x = x + mm(x, r)
        r, size = residual(x)
        return x, r, size, count + 1

    r, top = residual(guess)
    x, r, _, _ = lax.while_loop(keep_going, improve, (guess, r, top, jnp.int32(0)))
    x = x + mm(x, r)
    out_ref[...] = -mm(inverse, x) / (sqrt_eps * sqrt_fro)


def direction_kernel(per, window, n_windows, starts, pat, *refs):
    g_ref, m_ref, skh, skl = refs[:4]
    parts, (out_ref, cph, cpl, sems) = refs[4:-4], refs[-4:]
    blk = cph.shape[2]
    half = len(parts) // 2
    pairs, at = [], 0
    for i in range(half):
        size = parts[i].shape[0]
        pairs += [(parts[i], cph.at[pl.ds(at, size)]), (parts[half + i], cpl.at[pl.ds(at, size)])]
        at += size
    load_all(pairs, sems)

    def gathered(sk, cp, c):
        shard = c // per
        offset = pl.multiple_of((c - shard * per) * blk, blk)
        return jnp.concatenate([sk[shard, :, pl.ds(offset, blk)], cp[c]], axis=0)

    for w in range(n_windows):
        rows = pl.ds(pl.multiple_of(starts[w], window // 2 if window >= 32 else 8), window)
        cols = [pat[w * SLOTS + k] for k in range(SLOTS)]
        g = g_ref[rows, :]
        g_high = g.astype(BF).astype(F32)
        g_both = jnp.concatenate([g_high, g - g_high], axis=0).astype(BF)
        high = [gathered(skh, cph, c) for c in cols]
        low = [gathered(skl, cpl, c) for c in cols]
        both = dot_nt(g_both, jnp.concatenate(high, axis=1))
        projected = both[:window] + both[window:]
        projected += dot_nt(g_high.astype(BF), jnp.concatenate(low, axis=1))
        mixed = jnp.dot(projected, m_ref[...], precision=HIGHEST, preferred_element_type=F32)
        mixed_high = mixed.astype(BF).astype(F32)
        mixed_both = jnp.concatenate([mixed_high, mixed - mixed_high], axis=0).astype(BF)
        for k in range(0, SLOTS, 2):
            both = dot(mixed_both, jnp.concatenate(high[k : k + 2], axis=1))
            corr = both[:window] + both[window:]
            corr += dot(mixed_high.astype(BF), jnp.concatenate(low[k : k + 2], axis=1))
            corr += g[:, k * blk : (k + 2) * blk] * (1.0 / math.sqrt(SHIFT_EPS))
            out_ref[rows, k, :] = corr[:, :blk]
            out_ref[rows, k + 1, :] = corr[:, blk:]


def windows_of(start, dev_rows, blk):
    group = math.gcd(dev_rows, blk)
    if dev_rows % blk == blk // 2 and dev_rows > blk:
        whole = dev_rows // blk
        odd = (start // group) % 2
        later = odd * group + blk * jnp.arange(whole, dtype=jnp.int32)
        first = jnp.where(odd == 1, 0, dev_rows - blk)
        first_row = jnp.where(odd == 1, start, start + dev_rows - group)
        starts = jnp.concatenate([first[None], later])
        inside = jnp.concatenate([first_row[None], start + later])
        return blk, starts.astype(jnp.int32), (inside // blk).astype(jnp.int32)
    starts = group * jnp.arange(dev_rows // group, dtype=jnp.int32)
    return group, starts, (start + starts) // blk


def per_device(weights, hidden, cotangent, sketch, projection, pattern):
    tok_rows = hidden.shape[0]
    mp_rows, slots, blk = weights.shape
    block_rows = mp_rows // blk
    n_dp, n_mp = lax.axis_size("dp"), lax.axis_size("mp")
    dev_rows = mp_rows // n_dp
    all_tokens = tok_rows * n_dp
    rank = sketch.shape[0]
    shard_cols = cotangent.shape[1]
    per_shard = shard_cols // blk
    col_blocks = per_shard * n_mp
    outer = n_dp // 2
    per_step = 4 if block_rows % 4 == 0 else 1
    dp, mp = lax.axis_index("dp"), lax.axis_index("mp")
    side = dp % 2

    def swap(x, axis, bit):
        size = lax.axis_size(axis)
        return lax.ppermute(x, axis, [(i, i ^ bit) for i in range(size)])

    def after(x, *others):
        return lax.optimization_barrier((x, *others))[0]

    def over_dp(x):
        return lax.all_to_all(jnp.broadcast_to(x[None], (n_dp, *x.shape)), "dp", 0, 0)

    largest = jnp.stack([jnp.max(jnp.abs(hidden)), jnp.max(jnp.abs(cotangent))]).astype(F32)
    largest = lax.pmax(jnp.broadcast_to(largest[:, None], (2, 128)), ("dp", "mp"))
    bound = jnp.maximum(largest[0, 0] * largest[1, 0] * all_tokens, 1e-30)
    grad_scale = 32768.0 / bound

    width = sketch.shape[1]
    proj16 = (projection.reshape(rank, dev_rows) * PROJ_SCALE).astype(F16)
    early = over_dp(jnp.concatenate([sketch.astype(F16), proj16], axis=1))
    proj_all = early[:, :, width:].transpose(1, 0, 2).reshape(rank, mp_rows).astype(F32)
    sk_own = early[:, :, :width]
    hid_t = hidden.T
    hid_parts = hid_t.reshape(outer, 2, dev_rows, tok_rows)
    hid_own = lax.dynamic_index_in_dim(hid_parts, side, 1, keepdims=False)
    hid_send = lax.dynamic_index_in_dim(hid_parts, 1 - side, 1, keepdims=False)
    x_half, y_own, core_half, proj_all, sk_own, hid_t, hid_own, hid_send, weights_2d = (
        lax.optimization_barrier(
            (
                swap(cotangent, "mp", 2),
                swap(cotangent, "dp", 1),
                swap(cotangent, "mp", 1),
                proj_all,
                sk_own,
                hid_t,
                hid_own,
                hid_send,
                weights.reshape(mp_rows, slots * blk),
            )
        )
    )
    own = [cotangent, core_half, x_half, swap(x_half, "mp", 1)]
    y_x = swap(y_own, "mp", 2)
    hid_got = swap(hid_send, "dp", 1)
    pattern_rel = jnp.bitwise_xor(pattern, mp * per_shard)

    def place(block):
        if width < blk:
            return jnp.bitwise_xor(block, mp * per_shard)
        per = width // blk
        shard, rest = block // per, block % per
        near_mp = jnp.bitwise_xor(shard % n_mp, mp)
        return (near_mp * n_dp + shard // n_mp) * per + rest

    pat_all = pattern_rel.reshape(-1)
    partial_c = pl.pallas_call(
        functools.partial(
            compress_kernel, n_mp, per_shard, 1.0 / (PROJ_SCALE * all_tokens), per_step
        ),
        grid_spec=pltpu.PrefetchScalarGridSpec(
            num_scalar_prefetch=2,
            grid=(block_rows // per_step,),
            in_specs=[ANY] * n_mp
            + [
                pl.BlockSpec((per_step * blk, tok_rows), lambda i, a, b: (i, 0)),
                pl.BlockSpec((rank, per_step * blk), lambda i, a, b: (0, i)),
            ],
            out_specs=pl.BlockSpec((col_blocks, rank, blk), lambda i, a, b: (0, 0, 0)),
            scratch_shapes=[
                pltpu.VMEM((n_mp, tok_rows, shard_cols), BF),
                pltpu.SemaphoreType.DMA((n_mp,)),
            ],
        ),
        out_shape=jax.ShapeDtypeStruct((col_blocks, rank, blk), F32),
        compiler_params=params(),
        cost_estimate=SMALL,
        name="compress",
    )(pat_all, place(pattern).reshape(-1), *own, hid_t, proj_all)

    quarters = partial_c.reshape(n_mp, per_shard, rank, blk)
    got_far = swap(quarters[3].astype(F16), "mp", 1)
    got_near = swap(quarters[1].astype(F16), "mp", 1)
    far_half = (quarters[2] + got_far.astype(F32)).astype(F16)
    quarter = (quarters[0] + got_near.astype(F32)) + swap(far_half, "mp", 2).astype(F32)
    pieces = quarter.astype(F16).reshape(n_dp, per_shard * rank // n_dp, blk)
    pieces = lax.all_to_all(pieces, "dp", 0, 0)
    piece = jnp.sum(pieces.astype(F32), axis=0).astype(F16)
    quarter16 = over_dp(piece).reshape(per_shard, rank, blk)

    sk_own = after(sk_own, pieces)
    sk_far = swap(sk_own, "mp", 2)
    sk_parts = [sk_own, swap(sk_own, "mp", 1), sk_far, swap(sk_far, "mp", 1)]
    if width < blk:
        sk_abs = jnp.take(
            jnp.stack(sk_parts), jnp.bitwise_xor(jnp.arange(n_mp, dtype=jnp.int32), mp), axis=0
        )
        sk_abs = sk_abs.reshape(n_mp, col_blocks, blk // width // n_mp, rank, width)
        sk_abs = sk_abs.transpose(1, 3, 2, 0, 4).reshape(n_mp, per_shard, rank, blk)
        sk_parts = [
            lax.dynamic_index_in_dim(sk_abs, jnp.bitwise_xor(mp, i), 0, keepdims=False)
            for i in range(n_mp)
        ]
    oh, ol = split2_xla(sk_parts[0].astype(F32))
    sk_high, sk_low = split2_xla(jnp.concatenate(sk_parts, axis=0).astype(F32))

    sk_per = sk_high.shape[2] // blk
    qh, ql = split2_xla(quarter16.astype(F32))
    cross = pl.pallas_call(
        cross_gram_kernel,
        in_specs=[VMEM] * 4,
        out_specs=VMEM,
        out_shape=jax.ShapeDtypeStruct((rank, 2 * rank), F32),
        compiler_params=params(),
        cost_estimate=SMALL,
        name="cross_gram",
    )(qh, ql, oh, ol)
    sketch_gram = pl.pallas_call(
        sketch_gram_kernel,
        in_specs=[VMEM] * 2,
        out_specs=VMEM,
        out_shape=jax.ShapeDtypeStruct((rank, rank), F32),
        compiler_params=params(),
        cost_estimate=SMALL,
        name="sketch_gram",
    )(sk_high, sk_low)
    cross = cross + swap(cross, "mp", 2)
    cross = cross + swap(cross, "mp", 1)
    mixing = pl.pallas_call(
        mixing_kernel,
        in_specs=[VMEM] * 2,
        out_specs=VMEM,
        out_shape=jax.ShapeDtypeStruct((2 * rank, 2 * rank), F32),
        compiler_params=params(),
        cost_estimate=SMALL,
        name="mixing",
    )(sketch_gram, cross)

    quarter16 = after(quarter16, cross)
    far = swap(quarter16, "mp", 2)
    comp_parts = [quarter16, swap(quarter16, "mp", 1), far, swap(far, "mp", 1)]
    comp_parts = [split2_xla(part.astype(F32)) for part in comp_parts]
    comp_parts = [part[0] for part in comp_parts] + [part[1] for part in comp_parts]

    y_group = [y_own, swap(y_own, "mp", 1), y_x, swap(y_x, "mp", 1)]
    half_rows = outer * dev_rows
    devices = 2 * jnp.arange(outer, dtype=jnp.int32) + side
    window, _, _ = windows_of(dp * dev_rows, dev_rows, blk)
    window_starts, window_blocks = jax.vmap(lambda d: windows_of(d * dev_rows, dev_rows, blk)[1:])(
        devices
    )
    n_windows = window_starts.shape[1]
    pat_half = jnp.take(pattern_rel, window_blocks.reshape(-1), axis=0).reshape(-1)
    hid_type = BF if window % 32 == 0 else F32
    grad_half = pl.pallas_call(
        functools.partial(grad_kernel, n_mp, per_shard, blk, window, n_windows),
        grid_spec=pltpu.PrefetchScalarGridSpec(
            num_scalar_prefetch=3,
            grid=(outer,),
            in_specs=[ANY] * (2 * n_mp)
            + [pl.BlockSpec((dev_rows, tok_rows), lambda i, a, b, c: (i, 0))] * 2,
            out_specs=pl.BlockSpec((dev_rows, slots * blk), lambda i, a, b, c: (i, 0)),
            scratch_shapes=[
                pltpu.VMEM((n_mp, 2 * tok_rows, shard_cols), BF),
                pltpu.SemaphoreType.DMA((2 * n_mp,)),
            ],
        ),
        out_shape=jax.ShapeDtypeStruct((half_rows, slots * blk), F32),
        compiler_params=params(),
        cost_estimate=SMALL,
        name="pair_grad",
    )(
        window_starts.reshape(-1),
        pat_half,
        grad_scale[None],
        *own,
        *y_group,
        hid_own.reshape(half_rows, tok_rows).astype(hid_type),
        hid_got.reshape(half_rows, tok_rows).astype(hid_type),
    )
    grad_half = grad_half.reshape(outer, dev_rows, slots * blk)
    level = dp // 2

    def block_of(index):
        index = jnp.clip(index, 0, outer - 1)
        return lax.dynamic_index_in_dim(grad_half, index, 0, keepdims=False)

    grad = block_of(level)
    if outer <= 4:
        for d in sorted((d for d in range(1 - outer, outer) if d), key=lambda d: -abs(d)):
            perm = [(i, i + 2 * d) for i in range(n_dp) if 0 <= i + 2 * d < n_dp]
            got = lax.ppermute(block_of(level + d).astype(F16), "dp", perm)
            grad = grad + got.astype(F32)
    else:
        lanes = [[2 * i + s for i in range(outer)] for s in range(2)]
        got = lax.all_to_all(grad_half.astype(F16), "dp", 0, 0, axis_index_groups=lanes)
        grad = jnp.sum(got.astype(F32), axis=0)
    grad = grad * (1.0 / (grad_scale * all_tokens))

    input_grad = pl.pallas_call(
        functools.partial(input_grad_kernel, n_mp, per_shard, blk, per_step),
        grid_spec=pltpu.PrefetchScalarGridSpec(
            num_scalar_prefetch=1,
            grid=(block_rows // per_step,),
            in_specs=[ANY] * n_mp
            + [pl.BlockSpec((per_step * blk, slots * blk), lambda i, pat: (i, 0))],
            out_specs=pl.BlockSpec((tok_rows, per_step * blk), lambda i, pat: (0, i)),
            scratch_shapes=[
                pltpu.VMEM((n_mp, tok_rows, shard_cols), BF),
                pltpu.SemaphoreType.DMA((n_mp,)),
            ],
        ),
        out_shape=jax.ShapeDtypeStruct((tok_rows, mp_rows), BF),
        compiler_params=params(),
        cost_estimate=SMALL,
        name="input_grad",
    )(pat_all, *own, after(weights_2d, pieces))

    _, my_starts, my_blocks = windows_of(dp * dev_rows, dev_rows, blk)
    my_pat = jnp.take(place(pattern), my_blocks, axis=0).reshape(-1)
    smem = pl.BlockSpec(memory_space=pltpu.SMEM)
    direction = pl.pallas_call(
        functools.partial(direction_kernel, sk_per, window, n_windows),
        in_specs=[smem] * 2 + [VMEM] * 4 + [ANY] * len(comp_parts),
        out_specs=VMEM,
        out_shape=jax.ShapeDtypeStruct((dev_rows, slots, blk), F32),
        scratch_shapes=[
            pltpu.VMEM((col_blocks, rank, blk), BF),
            pltpu.VMEM((col_blocks, rank, blk), BF),
            pltpu.SemaphoreType.DMA((len(comp_parts),)),
        ],
        compiler_params=params(),
        cost_estimate=SMALL,
        name="direction",
    )(my_starts, my_pat, grad, mixing, sk_high, sk_low, *comp_parts)
    return (input_grad, direction.reshape(1, dev_rows, slots, blk))


def solution(mesh):
    return jax.shard_map(
        per_device,
        mesh=mesh,
        in_specs=(
            P("mp", None, None),
            P("dp", "mp"),
            P("dp", "mp"),
            P(None, ("dp", "mp")),
            P(None, "mp", "dp"),
            P("mp", None),
        ),
        out_specs=(P("dp", "mp"), P("mp", "dp", None, None)),
        check_vma=False,
    )
```

```python
import functools
import math

import jax
import jax.numpy as jnp
from jax import lax
from jax.experimental import pallas as pl
from jax.experimental.pallas import tpu as pltpu
from jax.sharding import PartitionSpec as P

NS_STEPS = 5
SHIFT_EPS = 0.0001
PROJ_SCALE = 1024.0
SLOTS = 8

BF = jnp.bfloat16
F16 = jnp.float16
F32 = jnp.float32
HIGHEST = lax.Precision.HIGHEST
VMEM = pl.BlockSpec(memory_space=pltpu.VMEM)
ANY = pl.BlockSpec(memory_space=pl.ANY)


SMALL = pl.CostEstimate(flops=1, bytes_accessed=1, transcendentals=0)


def params(mib=48):
    return pltpu.CompilerParams(vmem_limit_bytes=mib * 1024 * 1024)


def dot(a, b):
    return jnp.dot(a, b, preferred_element_type=F32)


def dot_nt(a, b):
    return lax.dot_general(a, b, (((1,), (1,)), ((), ())), preferred_element_type=F32)


def split2(value):
    high = value.astype(BF)
    return high, (value - high.astype(F32)).astype(BF)


def split2_xla(value):
    high = lax.reduce_precision(value, exponent_bits=8, mantissa_bits=7)
    return high.astype(BF), (value - high).astype(BF)


def load_all(pairs, sems):
    copies = [pltpu.make_async_copy(src, dst, sems.at[i]) for i, (src, dst) in enumerate(pairs)]
    for copy in copies:
        copy.start()
    for copy in copies:
        copy.wait()


def column_block(held, block, per_shard, size):
    shard = block // per_shard
    offset = pl.multiple_of((block - shard * per_shard) * size, size)
    return held[shard, :, pl.ds(offset, size)]


def compress_kernel(n_shards, per_shard, scale, per_step, pat, pat_out, *refs):
    shards = refs[:n_shards]
    hid_ref, proj_ref, out_ref, held, sems = refs[n_shards:]
    blk = out_ref.shape[1]

    @pl.when(pl.program_id(0) == 0)
    def _():
        load_all([(ref, held.at[i]) for i, ref in enumerate(shards)], sems)
        out_ref[...] = jnp.zeros_like(out_ref)

    for u in range(per_step):
        row = pl.program_id(0) * per_step + u
        span = slice(u * blk, (u + 1) * blk)
        hid = hid_ref[span, :]
        ph, pl_ = split2(proj_ref[span, :].T)
        left = jnp.concatenate(split2((dot(ph, hid) + dot(pl_, hid)) * scale), axis=0)
        cols = [pat[row * SLOTS + j] for j in range(SLOTS)]
        parts = []
        for j in range(0, SLOTS, 2):
            chosen = jnp.concatenate(
                [column_block(held, c, per_shard, blk) for c in cols[j : j + 2]], axis=1
            )
            part = dot(left, chosen)
            parts.append(part[:blk] + part[blk:])
        outs = [pat_out[row * SLOTS + j] for j in range(SLOTS)]
        sums = [
            out_ref[c] + parts[j // 2][:, (j % 2) * blk : (j % 2 + 1) * blk]
            for j, c in enumerate(outs)
        ]
        for c, total in zip(outs, sums):
            out_ref[c] = total


def grad_kernel(n_shards, per_shard, blk, window, n_windows, order, starts, pat, scale, *refs):
    shards = refs[: 2 * n_shards]
    own_ref, got_ref, out_ref, held, sems = refs[2 * n_shards :]
    toks = own_ref.shape[1]

    @pl.when(pl.program_id(0) == 0)
    def _():
        load_all(
            [
                (ref, held.at[i % n_shards, pl.ds(i // n_shards * toks, toks)])
                for i, ref in enumerate(shards)
            ],
            sems,
        )

    for w in range(n_windows):
        index = order[pl.program_id(0)] * n_windows + w
        rows = pl.ds(pl.multiple_of(starts[index], window // 2 if window >= 32 else 8), window)
        hid = jnp.concatenate([own_ref[rows, :], got_ref[rows, :]], axis=1).astype(BF)
        for j in range(0, SLOTS, 2):
            chosen = jnp.concatenate(
                [column_block(held, pat[index * SLOTS + j + i], per_shard, blk) for i in (0, 1)],
                axis=1,
            )
            out_ref[rows, j * blk : (j + 2) * blk] = dot(hid, chosen) * scale[0]


def input_grad_kernel(n_shards, per_shard, blk, per_step, pat, *refs):
    shards = refs[:n_shards]
    w_ref, out_ref, held, sems = refs[n_shards:]

    @pl.when(pl.program_id(0) == 0)
    def _():
        load_all([(ref, held.at[i]) for i, ref in enumerate(shards)], sems)

    for u in range(per_step):
        row = pl.program_id(0) * per_step + u
        chosen = jnp.concatenate(
            [column_block(held, pat[row * SLOTS + j], per_shard, blk) for j in range(SLOTS)], axis=1
        )
        span = slice(u * blk, (u + 1) * blk)
        out_ref[:, span] = dot_nt(chosen, w_ref[span, :]).astype(BF)


def sketch_gram_kernel(sh_ref, sl_ref, out_ref):
    out_ref[...] = jnp.zeros_like(out_ref)
    for s in range(sh_ref.shape[0]):
        high, low = sh_ref[s], sl_ref[s]
        out_ref[...] += dot_nt(high, high) + (dot_nt(high, low) + dot_nt(low, high))


def cross_gram_kernel(ch_ref, cl_ref, sh_ref, sl_ref, out_ref):
    rank = ch_ref.shape[1]
    per = ch_ref.shape[0] // sh_ref.shape[0]
    with_sketch = jnp.zeros((rank, rank), F32)
    with_self = jnp.zeros((rank, rank), F32)
    for s in range(sh_ref.shape[0]):
        high = jnp.concatenate([ch_ref[per * s + b] for b in range(per)], axis=1)
        low = jnp.concatenate([cl_ref[per * s + b] for b in range(per)], axis=1)
        sh, sl = sh_ref[s], sl_ref[s]
        with_sketch += dot_nt(high, sh) + (dot_nt(high, sl) + dot_nt(low, sh))
        with_self += dot_nt(high, high) + (dot_nt(high, low) + dot_nt(low, high))
    out_ref[:, :rank] = with_sketch
    out_ref[:, rank:] = with_self


def mixing_kernel(ss_ref, cross_ref, out_ref):
    rank = ss_ref.shape[0]
    size = 2 * rank
    sqrt_eps = math.sqrt(SHIFT_EPS)

    def mm(a, b):
        return jnp.dot(a, b, precision=HIGHEST, preferred_element_type=F32)

    cross = cross_ref[...]
    gram = jnp.concatenate(
        [jnp.concatenate([ss_ref[...], cross[:, :rank].T], axis=1), cross], axis=0
    )
    rows = lax.broadcasted_iota(jnp.int32, (size, size), 0)
    cols = lax.broadcasted_iota(jnp.int32, (size, size), 1)
    identity = jnp.where(rows == cols, 1.0, 0.0).astype(F32)
    shifted = gram + SHIFT_EPS * identity
    frobenius = jnp.sqrt(jnp.sum(shifted * shifted, keepdims=True))
    root = shifted / frobenius
    inverse = identity
    for step in range(NS_STEPS):
        product = root if step == 0 else mm(inverse, root)
        middle = 0.5 * (3.0 * identity - product)
        root = mm(root, middle)
        inverse = middle if step == 0 else mm(middle, inverse)
    sqrt_fro = jnp.sqrt(frobenius)
    half = 0.5 * sqrt_fro * (root + root.T) + sqrt_eps * identity
    guess = inverse / (sqrt_fro + sqrt_eps * 1.5**NS_STEPS)

    def residual(x):
        r = identity - mm(half, x)
        return r, jnp.max(jnp.abs(r))

    def keep_going(state):
        return jnp.logical_and(state[3] < 48, state[2] > 2e-6)

    def improve(state):
        x, r, _, count = state
        x = x + mm(x, r)
        r, size = residual(x)
        return x, r, size, count + 1

    r, top = residual(guess)
    x, r, _, _ = lax.while_loop(keep_going, improve, (guess, r, top, jnp.int32(0)))
    x = x + mm(x, r)
    out_ref[...] = -mm(inverse, x) / (sqrt_eps * sqrt_fro)


def direction_kernel(per, window, n_windows, starts, pat, *refs):
    g_ref, m_ref, skh, skl = refs[:4]
    parts, (out_ref, cph, cpl, sems) = refs[4:-4], refs[-4:]
    blk = cph.shape[2]
    half = len(parts) // 2
    pairs, at = [], 0
    for i in range(half):
        size = parts[i].shape[0]
        pairs += [(parts[i], cph.at[pl.ds(at, size)]), (parts[half + i], cpl.at[pl.ds(at, size)])]
        at += size
    load_all(pairs, sems)

    def gathered(sk, cp, c):
        shard = c // per
        offset = pl.multiple_of((c - shard * per) * blk, blk)
        return jnp.concatenate([sk[shard, :, pl.ds(offset, blk)], cp[c]], axis=0)

    for w in range(n_windows):
        rows = pl.ds(pl.multiple_of(starts[w], window // 2 if window >= 32 else 8), window)
        cols = [pat[w * SLOTS + k] for k in range(SLOTS)]
        g = g_ref[rows, :]
        g_high = g.astype(BF).astype(F32)
        g_both = jnp.concatenate([g_high, g - g_high], axis=0).astype(BF)
        high = [gathered(skh, cph, c) for c in cols]
        low = [gathered(skl, cpl, c) for c in cols]
        both = dot_nt(g_both, jnp.concatenate(high, axis=1))
        projected = both[:window] + both[window:]
        projected += dot_nt(g_high.astype(BF), jnp.concatenate(low, axis=1))
        mixed = jnp.dot(projected, m_ref[...], precision=HIGHEST, preferred_element_type=F32)
        mixed_high = mixed.astype(BF).astype(F32)
        mixed_both = jnp.concatenate([mixed_high, mixed - mixed_high], axis=0).astype(BF)
        for k in range(0, SLOTS, 2):
            both = dot(mixed_both, jnp.concatenate(high[k : k + 2], axis=1))
            corr = both[:window] + both[window:]
            corr += dot(mixed_high.astype(BF), jnp.concatenate(low[k : k + 2], axis=1))
            corr += g[:, k * blk : (k + 2) * blk] * (1.0 / math.sqrt(SHIFT_EPS))
            out_ref[rows, k, :] = corr[:, :blk]
            out_ref[rows, k + 1, :] = corr[:, blk:]


def windows_of(start, dev_rows, blk):
    group = math.gcd(dev_rows, blk)
    if dev_rows % blk == blk // 2 and dev_rows > blk:
        whole = dev_rows // blk
        odd = (start // group) % 2
        later = odd * group + blk * jnp.arange(whole, dtype=jnp.int32)
        first = jnp.where(odd == 1, 0, dev_rows - blk)
        first_row = jnp.where(odd == 1, start, start + dev_rows - group)
        starts = jnp.concatenate([first[None], later])
        inside = jnp.concatenate([first_row[None], start + later])
        return blk, starts.astype(jnp.int32), (inside // blk).astype(jnp.int32)
    starts = group * jnp.arange(dev_rows // group, dtype=jnp.int32)
    return group, starts, (start + starts) // blk


def per_device(weights, hidden, cotangent, sketch, projection, pattern):
    tok_rows = hidden.shape[0]
    mp_rows, slots, blk = weights.shape
    block_rows = mp_rows // blk
    n_dp, n_mp = lax.axis_size("dp"), lax.axis_size("mp")
    dev_rows = mp_rows // n_dp
    all_tokens = tok_rows * n_dp
    rank = sketch.shape[0]
    shard_cols = cotangent.shape[1]
    per_shard = shard_cols // blk
    col_blocks = per_shard * n_mp
    outer = n_dp // 2
    per_step = 4 if block_rows % 4 == 0 else 1
    dp, mp = lax.axis_index("dp"), lax.axis_index("mp")
    side = dp % 2

    def swap(x, axis, bit):
        size = lax.axis_size(axis)
        return lax.ppermute(x, axis, [(i, i ^ bit) for i in range(size)])

    def after(x, *others):
        return lax.optimization_barrier((x, *others))[0]

    def over_dp(x):
        return lax.all_to_all(jnp.broadcast_to(x[None], (n_dp, *x.shape)), "dp", 0, 0)

    def exponent(x):
        top = jnp.max(jnp.abs(x)).astype(F32)
        return jnp.floor(jnp.log2(jnp.maximum(top, 1e-15))) + 1.0

    width = sketch.shape[1]
    core_half = swap(cotangent, "mp", 1)
    exponents = jnp.stack([exponent(hidden), exponent(cotangent)])
    exponents = jnp.broadcast_to(jnp.repeat(exponents, 8)[:, None], (16, rank))
    proj_t = projection.reshape(rank, dev_rows).T * PROJ_SCALE
    early = jnp.concatenate([proj_t, exponents], axis=0).astype(F16)
    early = over_dp(after(early, core_half))
    proj_all = early[:, :dev_rows].reshape(mp_rows, rank).astype(F32)
    peaks = jnp.max(early[:, dev_rows:].astype(F32), axis=0)
    hid_t = hidden.T
    hid_parts = hid_t.reshape(outer, 2, dev_rows, tok_rows)
    hid_own = lax.dynamic_index_in_dim(hid_parts, side, 1, keepdims=False)
    hid_send = lax.dynamic_index_in_dim(hid_parts, 1 - side, 1, keepdims=False)
    x_half, y_own, core_half, hid_t, hid_own, hid_send, weights_2d, proj_all, peaks = (
        lax.optimization_barrier(
            (
                swap(cotangent, "mp", 2),
                swap(cotangent, "dp", 1),
                core_half,
                hid_t,
                hid_own,
                hid_send,
                weights.reshape(mp_rows, slots * blk),
                proj_all,
                peaks,
            )
        )
    )
    own = [cotangent, core_half, x_half, swap(x_half, "mp", 1)]
    y_x = swap(y_own, "mp", 2)
    y_core = swap(y_own, "mp", 1)
    hid_got = swap(hid_send, "dp", 1)
    for bit in (1, 2):
        peaks = jnp.maximum(peaks, swap(peaks, "mp", bit))
    sk_own = over_dp(after(sketch.astype(F16), x_half))
    pattern_rel = jnp.bitwise_xor(pattern, mp * per_shard)

    def place(block):
        if width < blk:
            return jnp.bitwise_xor(block, mp * per_shard)
        per = width // blk
        shard, rest = block // per, block % per
        near_mp = jnp.bitwise_xor(shard % n_mp, mp)
        return (near_mp * n_dp + shard // n_mp) * per + rest

    pat_all = pattern_rel.reshape(-1)
    partial_c = pl.pallas_call(
        functools.partial(
            compress_kernel, n_mp, per_shard, 1.0 / (PROJ_SCALE * all_tokens), per_step
        ),
        grid_spec=pltpu.PrefetchScalarGridSpec(
            num_scalar_prefetch=2,
            grid=(block_rows // per_step,),
            in_specs=[ANY] * n_mp
            + [
                pl.BlockSpec((per_step * blk, tok_rows), lambda i, a, b: (i, 0)),
                pl.BlockSpec((per_step * blk, rank), lambda i, a, b: (i, 0)),
            ],
            out_specs=pl.BlockSpec((col_blocks, rank, blk), lambda i, a, b: (0, 0, 0)),
            scratch_shapes=[
                pltpu.VMEM((n_mp, tok_rows, shard_cols), BF),
                pltpu.SemaphoreType.DMA((n_mp,)),
            ],
        ),
        out_shape=jax.ShapeDtypeStruct((col_blocks, rank, blk), F32),
        compiler_params=params(),
        cost_estimate=SMALL,
        name="compress",
    )(pat_all, place(pattern).reshape(-1), *own, hid_t, proj_all)

    partial_c, y_x, y_core, hid_got, peaks, sk_own = lax.optimization_barrier(
        (partial_c, y_x, y_core, hid_got, peaks, sk_own)
    )
    y_group = [y_own, y_core, y_x, swap(y_x, "mp", 1)]
    quarters = partial_c.reshape(n_mp, per_shard, rank, blk)
    got_far = swap(quarters[3].astype(F16), "mp", 1)
    got_near = swap(quarters[1].astype(F16), "mp", 1)
    far_half = (quarters[2] + got_far.astype(F32)).astype(F16)
    near_half = quarters[0] + got_near.astype(F32)
    far_half, near_half, y_last = lax.optimization_barrier((far_half, near_half, y_group[3]))
    y_group[3] = y_last
    far_sum = swap(far_half, "mp", 2)

    grad_scale = jnp.exp2(14.0 - peaks[0, 0] - peaks[8, 0] - math.log2(all_tokens))
    half_rows = outer * dev_rows
    devices = 2 * jnp.arange(outer, dtype=jnp.int32) + side
    window, _, _ = windows_of(dp * dev_rows, dev_rows, blk)
    window_starts, window_blocks = jax.vmap(lambda d: windows_of(d * dev_rows, dev_rows, blk)[1:])(
        devices
    )
    n_windows = window_starts.shape[1]
    pat_half = jnp.take(pattern_rel, window_blocks.reshape(-1), axis=0).reshape(-1)
    hid_type = BF if window % 32 == 0 else F32

    def pair_grad(blocks, shards):
        order = jnp.bitwise_xor(jnp.asarray(blocks, jnp.int32), dp // 2)
        out = pl.pallas_call(
            functools.partial(grad_kernel, n_mp, per_shard, blk, window, n_windows),
            grid_spec=pltpu.PrefetchScalarGridSpec(
                num_scalar_prefetch=4,
                grid=(len(blocks),),
                in_specs=[ANY] * (2 * n_mp)
                + [pl.BlockSpec((dev_rows, tok_rows), lambda i, o, a, b, c: (o[i], 0))] * 2,
                out_specs=pl.BlockSpec((dev_rows, slots * blk), lambda i, o, a, b, c: (i, 0)),
                scratch_shapes=[
                    pltpu.VMEM((n_mp, 2 * tok_rows, shard_cols), BF),
                    pltpu.SemaphoreType.DMA((2 * n_mp,)),
                ],
            ),
            out_shape=jax.ShapeDtypeStruct((len(blocks) * dev_rows, slots * blk), F32),
            compiler_params=params(),
            cost_estimate=SMALL,
            name="pair_grad",
        )(
            order,
            window_starts.reshape(-1),
            pat_half,
            grad_scale[None],
            *shards,
            hid_own.reshape(half_rows, tok_rows).astype(hid_type),
            hid_got.reshape(half_rows, tok_rows).astype(hid_type),
        )
        out = out.reshape(len(blocks), dev_rows, slots * blk)
        return {block: out[i] for i, block in enumerate(blocks)}

    crossing = [i for i in range(outer) if i & 2][::-1]
    staying = [i for i in range(outer) if not i & 2][::-1]
    sums = pair_grad(crossing, own + y_group)
    sent = {i: sums[i].astype(F16) for i in crossing if i & 1}
    got = {i: swap(sent[i], "dp", 2) for i in crossing if i & 1}
    sums.update(pair_grad(staying, own[:3] + [after(own[3], *sent.values())] + y_group))
    sent = {i: sums[i].astype(F16) for i in staying if i & 1}
    got.update({i: swap(sent[i], "dp", 2) for i in staying if i & 1})
    far_sum, near_half, _ = lax.optimization_barrier((far_sum, near_half, list(sent.values())))

    quarter = near_half + far_sum.astype(F32)
    pieces = quarter.astype(F16).reshape(n_dp, per_shard * rank // n_dp, blk)
    pieces = lax.all_to_all(pieces, "dp", 0, 0)

    level = 1
    while level < outer:
        if level > 1:
            got = {}
            for i in [i for i in sums if i & level]:
                got[i] = swap(sums[i].astype(F16), "dp", 2 * level)
        for i in got:
            sums[i ^ level] = sums[i ^ level] + got[i].astype(F32)
        sums = {i: part for i, part in sums.items() if not i & level}
        if level == 1 and outer > 2:
            sums[2], pieces = lax.optimization_barrier((sums[2].astype(F16), pieces))
        level *= 2
    grad = sums[0] * (1.0 / (grad_scale * all_tokens))

    input_grad = pl.pallas_call(
        functools.partial(input_grad_kernel, n_mp, per_shard, blk, per_step),
        grid_spec=pltpu.PrefetchScalarGridSpec(
            num_scalar_prefetch=1,
            grid=(block_rows // per_step,),
            in_specs=[ANY] * n_mp
            + [pl.BlockSpec((per_step * blk, slots * blk), lambda i, pat: (i, 0))],
            out_specs=pl.BlockSpec((tok_rows, per_step * blk), lambda i, pat: (0, i)),
            scratch_shapes=[
                pltpu.VMEM((n_mp, tok_rows, shard_cols), BF),
                pltpu.SemaphoreType.DMA((n_mp,)),
            ],
        ),
        out_shape=jax.ShapeDtypeStruct((tok_rows, mp_rows), BF),
        compiler_params=params(),
        cost_estimate=SMALL,
        name="input_grad",
    )(pat_all, *own, after(weights_2d, quarter))
    pieces, input_grad = lax.optimization_barrier((pieces, input_grad))

    piece = jnp.sum(pieces.astype(F32), axis=0).astype(F16)
    quarter16 = over_dp(piece).reshape(per_shard, rank, blk)

    sk_own = after(sk_own, quarter)
    sk_far = swap(sk_own, "mp", 2)
    sk_parts = [sk_own, swap(sk_own, "mp", 1), sk_far, swap(sk_far, "mp", 1)]
    if width < blk:
        sk_abs = jnp.take(
            jnp.stack(sk_parts), jnp.bitwise_xor(jnp.arange(n_mp, dtype=jnp.int32), mp), axis=0
        )
        sk_abs = sk_abs.reshape(n_mp, col_blocks, blk // width // n_mp, rank, width)
        sk_abs = sk_abs.transpose(1, 3, 2, 0, 4).reshape(n_mp, per_shard, rank, blk)
        sk_parts = [
            lax.dynamic_index_in_dim(sk_abs, jnp.bitwise_xor(mp, i), 0, keepdims=False)
            for i in range(n_mp)
        ]
    oh, ol = split2_xla(sk_parts[0].astype(F32))
    sk_high, sk_low = split2_xla(jnp.concatenate(sk_parts, axis=0).astype(F32))

    sk_per = sk_high.shape[2] // blk
    sketch_gram = pl.pallas_call(
        sketch_gram_kernel,
        in_specs=[VMEM] * 2,
        out_specs=VMEM,
        out_shape=jax.ShapeDtypeStruct((rank, rank), F32),
        compiler_params=params(),
        cost_estimate=SMALL,
        name="sketch_gram",
    )(sk_high, sk_low)
    quarter16, sketch_gram, sk_high, sk_low, oh, ol = lax.optimization_barrier(
        (quarter16, sketch_gram, sk_high, sk_low, oh, ol)
    )
    qh, ql = split2_xla(quarter16.astype(F32))
    cross = pl.pallas_call(
        cross_gram_kernel,
        in_specs=[VMEM] * 4,
        out_specs=VMEM,
        out_shape=jax.ShapeDtypeStruct((rank, 2 * rank), F32),
        compiler_params=params(),
        cost_estimate=SMALL,
        name="cross_gram",
    )(qh, ql, oh, ol)
    cross = cross + swap(cross, "mp", 2)
    cross = cross + swap(cross, "mp", 1)
    mixing = pl.pallas_call(
        mixing_kernel,
        in_specs=[VMEM] * 2,
        out_specs=VMEM,
        out_shape=jax.ShapeDtypeStruct((2 * rank, 2 * rank), F32),
        compiler_params=params(),
        cost_estimate=SMALL,
        name="mixing",
    )(sketch_gram, cross)

    quarter16 = after(quarter16, cross)
    far = swap(quarter16, "mp", 2)
    comp_parts = [quarter16, swap(quarter16, "mp", 1), far, swap(far, "mp", 1)]
    comp_parts = [split2_xla(part.astype(F32)) for part in comp_parts]
    comp_parts = [part[0] for part in comp_parts] + [part[1] for part in comp_parts]

    _, my_starts, my_blocks = windows_of(dp * dev_rows, dev_rows, blk)
    my_pat = jnp.take(place(pattern), my_blocks, axis=0).reshape(-1)
    smem = pl.BlockSpec(memory_space=pltpu.SMEM)
    direction = pl.pallas_call(
        functools.partial(direction_kernel, sk_per, window, n_windows),
        in_specs=[smem] * 2 + [VMEM] * 4 + [ANY] * len(comp_parts),
        out_specs=VMEM,
        out_shape=jax.ShapeDtypeStruct((dev_rows, slots, blk), F32),
        scratch_shapes=[
            pltpu.VMEM((col_blocks, rank, blk), BF),
            pltpu.VMEM((col_blocks, rank, blk), BF),
            pltpu.SemaphoreType.DMA((len(comp_parts),)),
        ],
        compiler_params=params(),
        cost_estimate=SMALL,
        name="direction",
    )(my_starts, my_pat, grad, mixing, sk_high, sk_low, *comp_parts)
    return (input_grad, direction.reshape(1, dev_rows, slots, blk))


def solution(mesh):
    return jax.shard_map(
        per_device,
        mesh=mesh,
        in_specs=(
            P("mp", None, None),
            P("dp", "mp"),
            P("dp", "mp"),
            P(None, ("dp", "mp")),
            P(None, "mp", "dp"),
            P("mp", None),
        ),
        out_specs=(P("dp", "mp"), P("mp", "dp", None, None)),
        check_vma=False,
    )
```

```python
import functools
import math

import jax
import jax.numpy as jnp
from jax import lax
from jax.experimental import pallas as pl
from jax.experimental.pallas import tpu as pltpu
from jax.sharding import PartitionSpec as P

NS_STEPS = 5
SHIFT_EPS = 0.0001
PROJ_SCALE = 1024.0
SLOTS = 8

BF = jnp.bfloat16
F16 = jnp.float16
F32 = jnp.float32
HIGHEST = lax.Precision.HIGHEST
VMEM = pl.BlockSpec(memory_space=pltpu.VMEM)
ANY = pl.BlockSpec(memory_space=pl.ANY)


SMALL = pl.CostEstimate(flops=1, bytes_accessed=1, transcendentals=0)


def params(mib=48):
    return pltpu.CompilerParams(vmem_limit_bytes=mib * 1024 * 1024)


def dot(a, b):
    return jnp.dot(a, b, preferred_element_type=F32)


def dot_nt(a, b):
    return lax.dot_general(a, b, (((1,), (1,)), ((), ())), preferred_element_type=F32)


def split2(value):
    high = value.astype(BF)
    return high, (value - high.astype(F32)).astype(BF)


def split2_xla(value):
    high = lax.reduce_precision(value, exponent_bits=8, mantissa_bits=7)
    return high.astype(BF), (value - high).astype(BF)


def load_all(pairs, sems):
    copies = [pltpu.make_async_copy(src, dst, sems.at[i]) for i, (src, dst) in enumerate(pairs)]
    for copy in copies:
        copy.start()
    for copy in copies:
        copy.wait()


def column_block(held, block, per_shard, size):
    shard = block // per_shard
    offset = pl.multiple_of((block - shard * per_shard) * size, size)
    return held[shard, :, pl.ds(offset, size)]


def compress_kernel(n_shards, per_shard, scale, per_step, pat, pat_out, places, *refs):
    shards = refs[:n_shards]
    hid_ref, parts_ref, out_ref, held, proj, sems = refs[n_shards:]
    blk = out_ref.shape[1]
    n_parts, part_rows = parts_ref.shape[:2]

    @pl.when(pl.program_id(0) == 0)
    def _():
        loads = [(ref, held.at[i]) for i, ref in enumerate(shards)]
        for i in range(n_parts):
            rows = pl.ds(pl.multiple_of(places[i] * part_rows, 8), part_rows)
            loads.append((parts_ref.at[i], proj.at[rows]))
        load_all(loads, sems)
        out_ref[...] = jnp.zeros_like(out_ref)

    for u in range(per_step):
        row = pl.program_id(0) * per_step + u
        span = slice(u * blk, (u + 1) * blk)
        hid = hid_ref[span, :]
        ph, pl_ = split2(proj[pl.ds(pl.multiple_of(row * blk, blk), blk), :].T)
        left = jnp.concatenate(split2((dot(ph, hid) + dot(pl_, hid)) * scale), axis=0)
        cols = [pat[row * SLOTS + j] for j in range(SLOTS)]
        parts = []
        for j in range(0, SLOTS, 2):
            chosen = jnp.concatenate(
                [column_block(held, c, per_shard, blk) for c in cols[j : j + 2]], axis=1
            )
            part = dot(left, chosen)
            parts.append(part[:blk] + part[blk:])
        outs = [pat_out[row * SLOTS + j] for j in range(SLOTS)]
        sums = [
            out_ref[c] + parts[j // 2][:, (j % 2) * blk : (j % 2 + 1) * blk]
            for j, c in enumerate(outs)
        ]
        for c, total in zip(outs, sums):
            out_ref[c] = total


def grad_kernel(n_shards, per_shard, blk, window, n_windows, order, starts, pat, *refs):
    shards = refs[: 2 * n_shards]
    own_ref, got_ref, out_ref, top_ref, held, sems = refs[2 * n_shards :]
    toks = own_ref.shape[1]

    @pl.when(pl.program_id(0) == 0)
    def _():
        load_all(
            [
                (ref, held.at[i % n_shards, pl.ds(i // n_shards * toks, toks)])
                for i, ref in enumerate(shards)
            ],
            sems,
        )
        top_ref[...] = jnp.zeros_like(top_ref)

    top = top_ref[...]
    for w in range(n_windows):
        index = order[pl.program_id(0)] * n_windows + w
        rows = pl.ds(pl.multiple_of(starts[index], window // 2 if window >= 32 else 8), window)
        hid = jnp.concatenate([own_ref[rows, :], got_ref[rows, :]], axis=1).astype(BF)
        for j in range(0, SLOTS, 2):
            chosen = jnp.concatenate(
                [column_block(held, pat[index * SLOTS + j + i], per_shard, blk) for i in (0, 1)],
                axis=1,
            )
            part = dot(hid, chosen)
            out_ref[rows, j * blk : (j + 2) * blk] = part
            size = jnp.abs(part)
            for i in range(0, window, 8):
                top = jnp.maximum(top, size[i : i + 8])
    top_ref[...] = top


def input_grad_kernel(n_shards, per_shard, blk, per_step, pat, *refs):
    shards = refs[:n_shards]
    w_ref, out_ref, held, sems = refs[n_shards:]

    @pl.when(pl.program_id(0) == 0)
    def _():
        load_all([(ref, held.at[i]) for i, ref in enumerate(shards)], sems)

    for u in range(per_step):
        row = pl.program_id(0) * per_step + u
        chosen = jnp.concatenate(
            [column_block(held, pat[row * SLOTS + j], per_shard, blk) for j in range(SLOTS)], axis=1
        )
        span = slice(u * blk, (u + 1) * blk)
        out_ref[:, span] = dot_nt(chosen, w_ref[span, :]).astype(BF)


def sketch_gram_kernel(sh_ref, sl_ref, out_ref):
    out_ref[...] = jnp.zeros_like(out_ref)
    for s in range(sh_ref.shape[0]):
        high, low = sh_ref[s], sl_ref[s]
        out_ref[...] += dot_nt(high, high) + (dot_nt(high, low) + dot_nt(low, high))


def cross_gram_kernel(ch_ref, cl_ref, sh_ref, sl_ref, out_ref):
    rank = ch_ref.shape[1]
    per = ch_ref.shape[0] // sh_ref.shape[0]
    with_sketch = jnp.zeros((rank, rank), F32)
    with_self = jnp.zeros((rank, rank), F32)
    for s in range(sh_ref.shape[0]):
        high = jnp.concatenate([ch_ref[per * s + b] for b in range(per)], axis=1)
        low = jnp.concatenate([cl_ref[per * s + b] for b in range(per)], axis=1)
        sh, sl = sh_ref[s], sl_ref[s]
        with_sketch += dot_nt(high, sh) + (dot_nt(high, sl) + dot_nt(low, sh))
        with_self += dot_nt(high, high) + (dot_nt(high, low) + dot_nt(low, high))
    out_ref[:, :rank] = with_sketch
    out_ref[:, rank:] = with_self


def mixing_kernel(ss_ref, cross_ref, out_ref):
    rank = ss_ref.shape[0]
    size = 2 * rank
    sqrt_eps = math.sqrt(SHIFT_EPS)

    def mm(a, b):
        return jnp.dot(a, b, precision=HIGHEST, preferred_element_type=F32)

    cross = cross_ref[...]
    gram = jnp.concatenate(
        [jnp.concatenate([ss_ref[...], cross[:, :rank].T], axis=1), cross], axis=0
    )
    rows = lax.broadcasted_iota(jnp.int32, (size, size), 0)
    cols = lax.broadcasted_iota(jnp.int32, (size, size), 1)
    identity = jnp.where(rows == cols, 1.0, 0.0).astype(F32)
    shifted = gram + SHIFT_EPS * identity
    frobenius = jnp.sqrt(jnp.sum(shifted * shifted, keepdims=True))
    root = shifted / frobenius
    inverse = identity
    for step in range(NS_STEPS):
        product = root if step == 0 else mm(inverse, root)
        middle = 0.5 * (3.0 * identity - product)
        root = mm(root, middle)
        inverse = middle if step == 0 else mm(middle, inverse)
    sqrt_fro = jnp.sqrt(frobenius)
    half = 0.5 * sqrt_fro * (root + root.T) + sqrt_eps * identity
    guess = inverse / (sqrt_fro + sqrt_eps * 1.5**NS_STEPS)

    def residual(x):
        r = identity - mm(half, x)
        return r, jnp.max(jnp.abs(r))

    def keep_going(state):
        return jnp.logical_and(state[3] < 48, state[2] > 2e-6)

    def improve(state):
        x, r, _, count = state
        x = x + mm(x, r)
        r, size = residual(x)
        return x, r, size, count + 1

    r, top = residual(guess)
    x, r, _, _ = lax.while_loop(keep_going, improve, (guess, r, top, jnp.int32(0)))
    x = x + mm(x, r)
    out_ref[...] = -mm(inverse, x) / (sqrt_eps * sqrt_fro)


def direction_kernel(per, window, n_windows, starts, pat, *refs):
    g_ref, m_ref, skh, skl = refs[:4]
    parts, (out_ref, cph, cpl, sems) = refs[4:-4], refs[-4:]
    blk = cph.shape[2]
    half = len(parts) // 2
    pairs, at = [], 0
    for i in range(half):
        size = parts[i].shape[0]
        pairs += [(parts[i], cph.at[pl.ds(at, size)]), (parts[half + i], cpl.at[pl.ds(at, size)])]
        at += size
    load_all(pairs, sems)

    def gathered(sk, cp, c):
        shard = c // per
        offset = pl.multiple_of((c - shard * per) * blk, blk)
        return jnp.concatenate([sk[shard, :, pl.ds(offset, blk)], cp[c]], axis=0)

    for w in range(n_windows):
        rows = pl.ds(pl.multiple_of(starts[w], window // 2 if window >= 32 else 8), window)
        cols = [pat[w * SLOTS + k] for k in range(SLOTS)]
        g = g_ref[rows, :]
        g_high = g.astype(BF).astype(F32)
        g_both = jnp.concatenate([g_high, g - g_high], axis=0).astype(BF)
        high = [gathered(skh, cph, c) for c in cols]
        low = [gathered(skl, cpl, c) for c in cols]
        both = dot_nt(g_both, jnp.concatenate(high, axis=1))
        projected = both[:window] + both[window:]
        projected += dot_nt(g_high.astype(BF), jnp.concatenate(low, axis=1))
        mixed = jnp.dot(projected, m_ref[...], precision=HIGHEST, preferred_element_type=F32)
        mixed_high = mixed.astype(BF).astype(F32)
        mixed_both = jnp.concatenate([mixed_high, mixed - mixed_high], axis=0).astype(BF)
        for k in range(0, SLOTS, 2):
            both = dot(mixed_both, jnp.concatenate(high[k : k + 2], axis=1))
            corr = both[:window] + both[window:]
            corr += dot(mixed_high.astype(BF), jnp.concatenate(low[k : k + 2], axis=1))
            corr += g[:, k * blk : (k + 2) * blk] * (1.0 / math.sqrt(SHIFT_EPS))
            out_ref[rows, k, :] = corr[:, :blk]
            out_ref[rows, k + 1, :] = corr[:, blk:]


def windows_of(start, dev_rows, blk):
    group = math.gcd(dev_rows, blk)
    if dev_rows % blk == blk // 2 and dev_rows > blk:
        whole = dev_rows // blk
        odd = (start // group) % 2
        later = odd * group + blk * jnp.arange(whole, dtype=jnp.int32)
        first = jnp.where(odd == 1, 0, dev_rows - blk)
        first_row = jnp.where(odd == 1, start, start + dev_rows - group)
        starts = jnp.concatenate([first[None], later])
        inside = jnp.concatenate([first_row[None], start + later])
        return blk, starts.astype(jnp.int32), (inside // blk).astype(jnp.int32)
    starts = group * jnp.arange(dev_rows // group, dtype=jnp.int32)
    return group, starts, (start + starts) // blk


def per_device(weights, hidden, cotangent, sketch, projection, pattern):
    tok_rows = hidden.shape[0]
    mp_rows, slots, blk = weights.shape
    block_rows = mp_rows // blk
    n_dp, n_mp = lax.axis_size("dp"), lax.axis_size("mp")
    dev_rows = mp_rows // n_dp
    all_tokens = tok_rows * n_dp
    rank = sketch.shape[0]
    shard_cols = cotangent.shape[1]
    per_shard = shard_cols // blk
    col_blocks = per_shard * n_mp
    outer = n_dp // 2
    per_step = 4 if block_rows % 4 == 0 else 1
    dp, mp = lax.axis_index("dp"), lax.axis_index("mp")
    side = dp % 2

    def swap(x, axis, bit):
        size = lax.axis_size(axis)
        return lax.ppermute(x, axis, [(i, i ^ bit) for i in range(size)])

    def after(x, *others):
        return lax.optimization_barrier((x, *others))[0]

    few = n_dp <= 8

    def over_dp(x):
        if few:
            return jnp.stack([x] + [swap(x, "dp", bits) for bits in range(1, n_dp)])
        return lax.all_to_all(jnp.broadcast_to(x[None], (n_dp, *x.shape)), "dp", 0, 0)

    width = sketch.shape[1]
    core_half = swap(cotangent, "mp", 1)
    proj_t = (projection.reshape(rank, dev_rows).T * PROJ_SCALE).astype(F16)
    proj_all = over_dp(after(proj_t, core_half)).astype(F32)
    if few:
        places = jnp.bitwise_xor(jnp.arange(n_dp, dtype=jnp.int32), dp)
    else:
        proj_all = proj_all.reshape(1, mp_rows, rank)
        places = jnp.zeros((1,), jnp.int32)
    hid_t = hidden.T
    hid_parts = hid_t.reshape(outer, 2, dev_rows, tok_rows)
    hid_own = lax.dynamic_index_in_dim(hid_parts, side, 1, keepdims=False)
    hid_send = lax.dynamic_index_in_dim(hid_parts, 1 - side, 1, keepdims=False)
    x_half, y_own, core_half, hid_t, hid_own, hid_send, weights_2d, proj_all = (
        lax.optimization_barrier(
            (
                swap(cotangent, "mp", 2),
                swap(cotangent, "dp", 1),
                core_half,
                hid_t,
                hid_own,
                hid_send,
                weights.reshape(mp_rows, slots * blk),
                proj_all,
            )
        )
    )
    own = [cotangent, core_half, x_half, swap(x_half, "mp", 1)]
    y_x = swap(y_own, "mp", 2)
    y_core = swap(y_own, "mp", 1)
    hid_got = swap(hid_send, "dp", 1)
    sk_own = over_dp(after(sketch.astype(F16), x_half))
    pattern_rel = jnp.bitwise_xor(pattern, mp * per_shard)

    def place(block):
        if width < blk:
            return jnp.bitwise_xor(block, mp * per_shard)
        per = width // blk
        shard, rest = block // per, block % per
        near_mp = jnp.bitwise_xor(shard % n_mp, mp)
        far_dp = shard // n_mp
        if few:
            far_dp = jnp.bitwise_xor(far_dp, dp)
        return (near_mp * n_dp + far_dp) * per + rest

    pat_all = pattern_rel.reshape(-1)
    partial_c = pl.pallas_call(
        functools.partial(
            compress_kernel, n_mp, per_shard, 1.0 / (PROJ_SCALE * all_tokens), per_step
        ),
        grid_spec=pltpu.PrefetchScalarGridSpec(
            num_scalar_prefetch=3,
            grid=(block_rows // per_step,),
            in_specs=[ANY] * n_mp
            + [pl.BlockSpec((per_step * blk, tok_rows), lambda i, a, b, c: (i, 0)), ANY],
            out_specs=pl.BlockSpec((col_blocks, rank, blk), lambda i, a, b, c: (0, 0, 0)),
            scratch_shapes=[
                pltpu.VMEM((n_mp, tok_rows, shard_cols), BF),
                pltpu.VMEM((mp_rows, rank), F32),
                pltpu.SemaphoreType.DMA((n_mp + len(places),)),
            ],
        ),
        out_shape=jax.ShapeDtypeStruct((col_blocks, rank, blk), F32),
        compiler_params=params(),
        cost_estimate=SMALL,
        name="compress",
    )(pat_all, place(pattern).reshape(-1), places, *own, hid_t, proj_all)

    partial_c, y_x, y_core, hid_got, sk_own = lax.optimization_barrier(
        (partial_c, y_x, y_core, hid_got, sk_own)
    )
    y_group = [y_own, y_core, y_x, swap(y_x, "mp", 1)]
    quarters = partial_c.reshape(n_mp, per_shard, rank, blk)
    got_far = swap(quarters[3].astype(F16), "mp", 1)
    got_near = swap(quarters[1].astype(F16), "mp", 1)
    far_half = (quarters[2] + got_far.astype(F32)).astype(F16)
    near_half = quarters[0] + got_near.astype(F32)
    far_half, near_half, y_last = lax.optimization_barrier((far_half, near_half, y_group[3]))
    y_group[3] = y_last
    far_sum = swap(far_half, "mp", 2)

    half_rows = outer * dev_rows
    devices = 2 * jnp.arange(outer, dtype=jnp.int32) + side
    window, _, _ = windows_of(dp * dev_rows, dev_rows, blk)
    window_starts, window_blocks = jax.vmap(lambda d: windows_of(d * dev_rows, dev_rows, blk)[1:])(
        devices
    )
    n_windows = window_starts.shape[1]
    pat_half = jnp.take(pattern_rel, window_blocks.reshape(-1), axis=0).reshape(-1)
    hid_type = BF if window % 32 == 0 else F32

    def pair_grad(blocks, shards):
        order = jnp.bitwise_xor(jnp.asarray(blocks, jnp.int32), dp // 2)
        out, top = pl.pallas_call(
            functools.partial(grad_kernel, n_mp, per_shard, blk, window, n_windows),
            grid_spec=pltpu.PrefetchScalarGridSpec(
                num_scalar_prefetch=3,
                grid=(len(blocks),),
                in_specs=[ANY] * (2 * n_mp)
                + [pl.BlockSpec((dev_rows, tok_rows), lambda i, o, a, b: (o[i], 0))] * 2,
                out_specs=[
                    pl.BlockSpec((dev_rows, slots * blk), lambda i, o, a, b: (i, 0)),
                    pl.BlockSpec((8, 2 * blk), lambda i, o, a, b: (0, 0)),
                ],
                scratch_shapes=[
                    pltpu.VMEM((n_mp, 2 * tok_rows, shard_cols), BF),
                    pltpu.SemaphoreType.DMA((2 * n_mp,)),
                ],
            ),
            out_shape=[
                jax.ShapeDtypeStruct((len(blocks) * dev_rows, slots * blk), F32),
                jax.ShapeDtypeStruct((8, 2 * blk), F32),
            ],
            compiler_params=params(),
            cost_estimate=SMALL,
            name="pair_grad",
        )(
            order,
            window_starts.reshape(-1),
            pat_half,
            *shards,
            hid_own.reshape(half_rows, tok_rows).astype(hid_type),
            hid_got.reshape(half_rows, tok_rows).astype(hid_type),
        )
        out = out.reshape(len(blocks), dev_rows, slots * blk)
        top = jnp.maximum(jnp.max(top), 1e-30)
        return {block: (out[i], top) for i, block in enumerate(blocks)}

    def pack(part):
        value, top = part
        return (value * (16384.0 / top)).astype(F16), jnp.broadcast_to(top, (8, 128))

    def send(packed, bit):
        top = swap(packed[1], "dp", bit)
        return swap(packed[0], "dp", bit), top

    def add(part, got):
        value, top = part
        far = got[1][0, 0]
        return value + got[0].astype(F32) * (far * (1.0 / 16384.0)), top + far

    crossing = [i for i in range(outer) if i & 2][::-1]
    staying = [i for i in range(outer) if not i & 2][::-1]
    sums = pair_grad(crossing, own + y_group)
    sent = {i: pack(sums[i]) for i in crossing if i & 1}
    got = {i: send(part, 2) for i, part in sent.items()}
    before = [part[0] for part in sent.values()]
    sums.update(pair_grad(staying, own[:3] + [after(own[3], *before)] + y_group))
    sent = {i: pack(sums[i]) for i in staying if i & 1}
    got.update({i: send(part, 2) for i, part in sent.items()})
    before = [part[0] for part in sent.values()]
    far_sum, near_half, _ = lax.optimization_barrier((far_sum, near_half, before))

    quarter = near_half + far_sum.astype(F32)
    pieces = quarter.astype(F16).reshape(n_dp, per_shard * rank // n_dp, blk)
    if few:
        pieces = [pieces[0]] + [swap(pieces[bits], "dp", bits) for bits in range(1, n_dp)]
    else:
        pieces = list(lax.all_to_all(pieces, "dp", 0, 0))

    level = 1
    while level < outer:
        if level > 1:
            got = {i: send(pack(sums[i]), 2 * level) for i in sums if i & level}
        for i in got:
            sums[i ^ level] = add(sums[i ^ level], got[i])
        sums = {i: part for i, part in sums.items() if not i & level}
        if level == 1 and outer > 2:
            crossed, pieces = lax.optimization_barrier((pack(sums[2]), pieces))
            got = {2: send(crossed, 4)}
            if outer > 4:
                got.update({i: send(pack(sums[i]), 4) for i in sums if i & 2 and i > 2})
            for i in got:
                sums[i ^ 2] = add(sums[i ^ 2], got[i]) if outer > 4 else sums[i ^ 2]
            sums = {i: part for i, part in sums.items() if not i & 2}
            level = 2
        level *= 2

    input_grad = pl.pallas_call(
        functools.partial(input_grad_kernel, n_mp, per_shard, blk, per_step),
        grid_spec=pltpu.PrefetchScalarGridSpec(
            num_scalar_prefetch=1,
            grid=(block_rows // per_step,),
            in_specs=[ANY] * n_mp
            + [pl.BlockSpec((per_step * blk, slots * blk), lambda i, pat: (i, 0))],
            out_specs=pl.BlockSpec((tok_rows, per_step * blk), lambda i, pat: (0, i)),
            scratch_shapes=[
                pltpu.VMEM((n_mp, tok_rows, shard_cols), BF),
                pltpu.SemaphoreType.DMA((n_mp,)),
            ],
        ),
        out_shape=jax.ShapeDtypeStruct((tok_rows, mp_rows), BF),
        compiler_params=params(),
        cost_estimate=SMALL,
        name="input_grad",
    )(pat_all, *own, after(weights_2d, quarter))
    pieces, input_grad = lax.optimization_barrier((pieces, input_grad))

    piece = sum(part.astype(F32) for part in pieces).astype(F16)
    quarter16 = over_dp(piece).reshape(per_shard, rank, blk)

    sk_own = after(sk_own, quarter)
    sk_far = swap(sk_own, "mp", 2)
    sk_parts = [sk_own, swap(sk_own, "mp", 1), sk_far, swap(sk_far, "mp", 1)]
    if width < blk:
        sk_abs = jnp.take(
            jnp.stack(sk_parts), jnp.bitwise_xor(jnp.arange(n_mp, dtype=jnp.int32), mp), axis=0
        )
        sk_abs = sk_abs.reshape(n_mp, col_blocks, blk // width // n_mp, rank, width)
        sk_abs = sk_abs.transpose(1, 3, 2, 0, 4).reshape(n_mp, per_shard, rank, blk)
        sk_parts = [
            lax.dynamic_index_in_dim(sk_abs, jnp.bitwise_xor(mp, i), 0, keepdims=False)
            for i in range(n_mp)
        ]
    oh, ol = split2_xla(sk_parts[0].astype(F32))
    sk_high, sk_low = split2_xla(jnp.concatenate(sk_parts, axis=0).astype(F32))

    sk_per = sk_high.shape[2] // blk
    sketch_gram = pl.pallas_call(
        sketch_gram_kernel,
        in_specs=[VMEM] * 2,
        out_specs=VMEM,
        out_shape=jax.ShapeDtypeStruct((rank, rank), F32),
        compiler_params=params(),
        cost_estimate=SMALL,
        name="sketch_gram",
    )(sk_high, sk_low)
    quarter16, sketch_gram, sk_high, sk_low, oh, ol = lax.optimization_barrier(
        (quarter16, sketch_gram, sk_high, sk_low, oh, ol)
    )
    qh, ql = split2_xla(quarter16.astype(F32))
    cross = pl.pallas_call(
        cross_gram_kernel,
        in_specs=[VMEM] * 4,
        out_specs=VMEM,
        out_shape=jax.ShapeDtypeStruct((rank, 2 * rank), F32),
        compiler_params=params(),
        cost_estimate=SMALL,
        name="cross_gram",
    )(qh, ql, oh, ol)
    cross = cross + swap(cross, "mp", 2)
    cross = cross + swap(cross, "mp", 1)
    mixing = pl.pallas_call(
        mixing_kernel,
        in_specs=[VMEM] * 2,
        out_specs=VMEM,
        out_shape=jax.ShapeDtypeStruct((2 * rank, 2 * rank), F32),
        compiler_params=params(),
        cost_estimate=SMALL,
        name="mixing",
    )(sketch_gram, cross)

    quarter16 = after(quarter16, cross)
    far = swap(quarter16, "mp", 2)
    comp_parts = [quarter16, swap(quarter16, "mp", 1), far, swap(far, "mp", 1)]
    comp_parts = [split2_xla(part.astype(F32)) for part in comp_parts]
    comp_parts = [part[0] for part in comp_parts] + [part[1] for part in comp_parts]

    kept, mixing, comp_parts, sk_high, sk_low = lax.optimization_barrier(
        (sums[0], mixing, comp_parts, sk_high, sk_low)
    )
    if outer == 4:
        kept = add(kept, got[2])
    grad = kept[0] * (1.0 / all_tokens)
    _, my_starts, my_blocks = windows_of(dp * dev_rows, dev_rows, blk)
    my_pat = jnp.take(place(pattern), my_blocks, axis=0).reshape(-1)
    smem = pl.BlockSpec(memory_space=pltpu.SMEM)
    direction = pl.pallas_call(
        functools.partial(direction_kernel, sk_per, window, n_windows),
        in_specs=[smem] * 2 + [VMEM] * 4 + [ANY] * len(comp_parts),
        out_specs=VMEM,
        out_shape=jax.ShapeDtypeStruct((dev_rows, slots, blk), F32),
        scratch_shapes=[
            pltpu.VMEM((col_blocks, rank, blk), BF),
            pltpu.VMEM((col_blocks, rank, blk), BF),
            pltpu.SemaphoreType.DMA((len(comp_parts),)),
        ],
        compiler_params=params(),
        cost_estimate=SMALL,
        name="direction",
    )(my_starts, my_pat, grad, mixing, sk_high, sk_low, *comp_parts)
    return (input_grad, direction.reshape(1, dev_rows, slots, blk))


def solution(mesh):
    return jax.shard_map(
        per_device,
        mesh=mesh,
        in_specs=(
            P("mp", None, None),
            P("dp", "mp"),
            P("dp", "mp"),
            P(None, ("dp", "mp")),
            P(None, "mp", "dp"),
            P("mp", None),
        ),
        out_specs=(P("dp", "mp"), P("mp", "dp", None, None)),
        check_vma=False,
    )
```

```python
import functools
import math

import jax
import jax.numpy as jnp
from jax import lax
from jax.experimental import pallas as pl
from jax.experimental.pallas import tpu as pltpu
from jax.sharding import PartitionSpec as P

NS_STEPS = 5
SHIFT_EPS = 0.0001
PROJ_SCALE = 1024.0
SLOTS = 8

BF = jnp.bfloat16
F16 = jnp.float16
F32 = jnp.float32
HIGHEST = lax.Precision.HIGHEST
VMEM = pl.BlockSpec(memory_space=pltpu.VMEM)
ANY = pl.BlockSpec(memory_space=pl.ANY)


SMALL = pl.CostEstimate(flops=1, bytes_accessed=1, transcendentals=0)


def params(mib=48):
    return pltpu.CompilerParams(vmem_limit_bytes=mib * 1024 * 1024)


def dot(a, b):
    return jnp.dot(a, b, preferred_element_type=F32)


def dot_nt(a, b):
    return lax.dot_general(a, b, (((1,), (1,)), ((), ())), preferred_element_type=F32)


def split2(value):
    high = value.astype(BF)
    return high, (value - high.astype(F32)).astype(BF)


def split2_xla(value):
    high = lax.reduce_precision(value, exponent_bits=8, mantissa_bits=7)
    return high.astype(BF), (value - high).astype(BF)


def load_all(pairs, sems):
    copies = [pltpu.make_async_copy(src, dst, sems.at[i]) for i, (src, dst) in enumerate(pairs)]
    for copy in copies:
        copy.start()
    for copy in copies:
        copy.wait()


def column_block(held, block, per_shard, size):
    shard = block // per_shard
    offset = pl.multiple_of((block - shard * per_shard) * size, size)
    return held[shard, :, pl.ds(offset, size)]


def compress_kernel(n_shards, per_shard, scale, per_step, peak_rows, pat, pat_out, *refs):
    shards = refs[:n_shards]
    hid_ref, proj_ref, out_ref, top_ref, held, sems = refs[n_shards:]
    blk = out_ref.shape[1]

    @pl.when(pl.program_id(0) == 0)
    def _():
        load_all([(ref, held.at[i]) for i, ref in enumerate(shards)], sems)
        out_ref[...] = jnp.zeros_like(out_ref)
        top_ref[...] = jnp.zeros_like(top_ref)

    toks = held.shape[1]
    start = jnp.minimum(pl.program_id(0) * peak_rows, toks - peak_rows)
    top = top_ref[...]
    for i in range(n_shards):
        part = jnp.abs(held[i, pl.ds(pl.multiple_of(start, 16), peak_rows), :])
        part = jnp.max(part.reshape(peak_rows // 16, 16, -1), axis=0).astype(F32)
        part = jnp.maximum(part[:8], part[8:])
        for j in range(0, part.shape[1], 128):
            top = jnp.maximum(top, part[:, j : j + 128])
    top_ref[...] = top

    for u in range(per_step):
        row = pl.program_id(0) * per_step + u
        span = slice(u * blk, (u + 1) * blk)
        hid = hid_ref[span, :]
        ph, pl_ = split2(proj_ref[span, :].T)
        left = jnp.concatenate(split2((dot(ph, hid) + dot(pl_, hid)) * scale), axis=0)
        cols = [pat[row * SLOTS + j] for j in range(SLOTS)]
        parts = []
        for j in range(0, SLOTS, 2):
            chosen = jnp.concatenate(
                [column_block(held, c, per_shard, blk) for c in cols[j : j + 2]], axis=1
            )
            part = dot(left, chosen)
            parts.append(part[:blk] + part[blk:])
        outs = [pat_out[row * SLOTS + j] for j in range(SLOTS)]
        sums = [
            out_ref[c] + parts[j // 2][:, (j % 2) * blk : (j % 2 + 1) * blk]
            for j, c in enumerate(outs)
        ]
        for c, total in zip(outs, sums):
            out_ref[c] = total


def grad_kernel(n_shards, per_shard, blk, window, n_windows, order, starts, pat, *refs):
    shards = refs[: 2 * n_shards]
    own_ref, got_ref, out_ref, held, sems = refs[2 * n_shards :]
    toks = own_ref.shape[1]

    @pl.when(pl.program_id(0) == 0)
    def _():
        load_all(
            [
                (ref, held.at[i % n_shards, pl.ds(i // n_shards * toks, toks)])
                for i, ref in enumerate(shards)
            ],
            sems,
        )

    for w in range(n_windows):
        index = order[pl.program_id(0)] * n_windows + w
        rows = pl.ds(pl.multiple_of(starts[index], window // 2 if window >= 32 else 8), window)
        hid = jnp.concatenate([own_ref[rows, :], got_ref[rows, :]], axis=1).astype(BF)
        for j in range(0, SLOTS, 2):
            chosen = jnp.concatenate(
                [column_block(held, pat[index * SLOTS + j + i], per_shard, blk) for i in (0, 1)],
                axis=1,
            )
            out_ref[rows, j * blk : (j + 2) * blk] = dot(hid, chosen)


def input_grad_kernel(n_shards, per_shard, blk, per_step, pat, *refs):
    shards = refs[:n_shards]
    w_ref, out_ref, held, sems = refs[n_shards:]

    @pl.when(pl.program_id(0) == 0)
    def _():
        load_all([(ref, held.at[i]) for i, ref in enumerate(shards)], sems)

    for u in range(per_step):
        row = pl.program_id(0) * per_step + u
        chosen = jnp.concatenate(
            [column_block(held, pat[row * SLOTS + j], per_shard, blk) for j in range(SLOTS)], axis=1
        )
        span = slice(u * blk, (u + 1) * blk)
        out_ref[:, span] = dot_nt(chosen, w_ref[span, :]).astype(BF)


def sketch_gram_kernel(sh_ref, sl_ref, out_ref):
    out_ref[...] = jnp.zeros_like(out_ref)
    for s in range(sh_ref.shape[0]):
        high, low = sh_ref[s], sl_ref[s]
        out_ref[...] += dot_nt(high, high) + (dot_nt(high, low) + dot_nt(low, high))


def cross_gram_kernel(ch_ref, cl_ref, sh_ref, sl_ref, out_ref):
    rank = ch_ref.shape[1]
    per = ch_ref.shape[0] // sh_ref.shape[0]
    with_sketch = jnp.zeros((rank, rank), F32)
    with_self = jnp.zeros((rank, rank), F32)
    for s in range(sh_ref.shape[0]):
        high = jnp.concatenate([ch_ref[per * s + b] for b in range(per)], axis=1)
        low = jnp.concatenate([cl_ref[per * s + b] for b in range(per)], axis=1)
        sh, sl = sh_ref[s], sl_ref[s]
        with_sketch += dot_nt(high, sh) + (dot_nt(high, sl) + dot_nt(low, sh))
        with_self += dot_nt(high, high) + (dot_nt(high, low) + dot_nt(low, high))
    out_ref[:, :rank] = with_sketch
    out_ref[:, rank:] = with_self


def mixing_kernel(ss_ref, cross_ref, out_ref):
    rank = ss_ref.shape[0]
    size = 2 * rank
    sqrt_eps = math.sqrt(SHIFT_EPS)

    def mm(a, b):
        return jnp.dot(a, b, precision=HIGHEST, preferred_element_type=F32)

    cross = cross_ref[...]
    gram = jnp.concatenate(
        [jnp.concatenate([ss_ref[...], cross[:, :rank].T], axis=1), cross], axis=0
    )
    rows = lax.broadcasted_iota(jnp.int32, (size, size), 0)
    cols = lax.broadcasted_iota(jnp.int32, (size, size), 1)
    identity = jnp.where(rows == cols, 1.0, 0.0).astype(F32)
    shifted = gram + SHIFT_EPS * identity
    frobenius = jnp.sqrt(jnp.sum(shifted * shifted, keepdims=True))
    root = shifted / frobenius
    inverse = identity
    for step in range(NS_STEPS):
        product = root if step == 0 else mm(inverse, root)
        middle = 0.5 * (3.0 * identity - product)
        root = mm(root, middle)
        inverse = middle if step == 0 else mm(middle, inverse)
    sqrt_fro = jnp.sqrt(frobenius)
    half = 0.5 * sqrt_fro * (root + root.T) + sqrt_eps * identity
    guess = inverse / (sqrt_fro + sqrt_eps * 1.5**NS_STEPS)

    def residual(x):
        r = identity - mm(half, x)
        return r, jnp.max(jnp.abs(r))

    def keep_going(state):
        return jnp.logical_and(state[3] < 48, state[2] > 2e-6)

    def improve(state):
        x, r, _, count = state
        x = x + mm(x, r)
        r, size = residual(x)
        return x, r, size, count + 1

    r, top = residual(guess)
    x, r, _, _ = lax.while_loop(keep_going, improve, (guess, r, top, jnp.int32(0)))
    x = x + mm(x, r)
    out_ref[...] = -mm(inverse, x) / (sqrt_eps * sqrt_fro)


def direction_kernel(per, window, n_windows, starts, pat, *refs):
    g_ref, m_ref, skh, skl = refs[:4]
    parts, (out_ref, cph, cpl, sems) = refs[4:-4], refs[-4:]
    blk = cph.shape[2]
    half = len(parts) // 2
    pairs, at = [], 0
    for i in range(half):
        size = parts[i].shape[0]
        pairs += [(parts[i], cph.at[pl.ds(at, size)]), (parts[half + i], cpl.at[pl.ds(at, size)])]
        at += size
    load_all(pairs, sems)

    def gathered(sk, cp, c):
        shard = c // per
        offset = pl.multiple_of((c - shard * per) * blk, blk)
        return jnp.concatenate([sk[shard, :, pl.ds(offset, blk)], cp[c]], axis=0)

    for w in range(n_windows):
        rows = pl.ds(pl.multiple_of(starts[w], window // 2 if window >= 32 else 8), window)
        cols = [pat[w * SLOTS + k] for k in range(SLOTS)]
        g = g_ref[rows, :]
        g_high = g.astype(BF).astype(F32)
        g_both = jnp.concatenate([g_high, g - g_high], axis=0).astype(BF)
        high = [gathered(skh, cph, c) for c in cols]
        low = [gathered(skl, cpl, c) for c in cols]
        both = dot_nt(g_both, jnp.concatenate(high, axis=1))
        projected = both[:window] + both[window:]
        projected += dot_nt(g_high.astype(BF), jnp.concatenate(low, axis=1))
        mixed = jnp.dot(projected, m_ref[...], precision=HIGHEST, preferred_element_type=F32)
        mixed_high = mixed.astype(BF).astype(F32)
        mixed_both = jnp.concatenate([mixed_high, mixed - mixed_high], axis=0).astype(BF)
        for k in range(0, SLOTS, 2):
            both = dot(mixed_both, jnp.concatenate(high[k : k + 2], axis=1))
            corr = both[:window] + both[window:]
            corr += dot(mixed_high.astype(BF), jnp.concatenate(low[k : k + 2], axis=1))
            corr += g[:, k * blk : (k + 2) * blk] * (1.0 / math.sqrt(SHIFT_EPS))
            out_ref[rows, k, :] = corr[:, :blk]
            out_ref[rows, k + 1, :] = corr[:, blk:]


def windows_of(start, dev_rows, blk):
    group = math.gcd(dev_rows, blk)
    if dev_rows % blk == blk // 2 and dev_rows > blk:
        whole = dev_rows // blk
        odd = (start // group) % 2
        later = odd * group + blk * jnp.arange(whole, dtype=jnp.int32)
        first = jnp.where(odd == 1, 0, dev_rows - blk)
        first_row = jnp.where(odd == 1, start, start + dev_rows - group)
        starts = jnp.concatenate([first[None], later])
        inside = jnp.concatenate([first_row[None], start + later])
        return blk, starts.astype(jnp.int32), (inside // blk).astype(jnp.int32)
    starts = group * jnp.arange(dev_rows // group, dtype=jnp.int32)
    return group, starts, (start + starts) // blk


def per_device(weights, hidden, cotangent, sketch, projection, pattern):
    tok_rows = hidden.shape[0]
    mp_rows, slots, blk = weights.shape
    block_rows = mp_rows // blk
    n_dp, n_mp = lax.axis_size("dp"), lax.axis_size("mp")
    dev_rows = mp_rows // n_dp
    all_tokens = tok_rows * n_dp
    rank = sketch.shape[0]
    shard_cols = cotangent.shape[1]
    per_shard = shard_cols // blk
    col_blocks = per_shard * n_mp
    outer = n_dp // 2
    per_step = 4 if block_rows % 4 == 0 else 1
    dp, mp = lax.axis_index("dp"), lax.axis_index("mp")
    side = dp % 2

    def swap(x, axis, bit):
        size = lax.axis_size(axis)
        return lax.ppermute(x, axis, [(i, i ^ bit) for i in range(size)])

    def after(x, *others):
        return lax.optimization_barrier((x, *others))[0]

    def over_dp(x):
        return lax.all_to_all(jnp.broadcast_to(x[None], (n_dp, *x.shape)), "dp", 0, 0)

    width = sketch.shape[1]
    core_half = swap(cotangent, "mp", 1)
    hid_t = hidden.T
    hid_parts = hid_t.reshape(outer, 2, dev_rows, tok_rows)
    hid_own = lax.dynamic_index_in_dim(hid_parts, side, 1, keepdims=False)
    hid_send = lax.dynamic_index_in_dim(hid_parts, 1 - side, 1, keepdims=False)
    proj_t = (projection.reshape(rank, dev_rows).T * PROJ_SCALE).astype(F16)
    proj_all = over_dp(after(proj_t, core_half, hid_send)).reshape(mp_rows, rank).astype(F32)
    top_hidden = jnp.max(jnp.abs(hidden)).astype(F32)
    x_half, y_own, core_half, hid_t, hid_own, hid_send, weights_2d, proj_all, top_hidden = (
        lax.optimization_barrier(
            (
                swap(cotangent, "mp", 2),
                swap(cotangent, "dp", 1),
                core_half,
                hid_t,
                hid_own,
                hid_send,
                weights.reshape(mp_rows, slots * blk),
                proj_all,
                top_hidden,
            )
        )
    )
    own = [cotangent, core_half, x_half, swap(x_half, "mp", 1)]
    y_x = swap(y_own, "mp", 2)
    y_core = swap(y_own, "mp", 1)
    hid_got = swap(hid_send, "dp", 1)
    sk_own = over_dp(after(sketch.astype(F16), x_half))
    pattern_rel = jnp.bitwise_xor(pattern, mp * per_shard)

    def place(block):
        if width < blk:
            return jnp.bitwise_xor(block, mp * per_shard)
        per = width // blk
        shard, rest = block // per, block % per
        near_mp = jnp.bitwise_xor(shard % n_mp, mp)
        return (near_mp * n_dp + shard // n_mp) * per + rest

    pat_all = pattern_rel.reshape(-1)
    partial_c, top = pl.pallas_call(
        functools.partial(
            compress_kernel,
            n_mp,
            per_shard,
            1.0 / (PROJ_SCALE * all_tokens),
            per_step,
            -(-tok_rows * per_step // block_rows // 16) * 16,
        ),
        grid_spec=pltpu.PrefetchScalarGridSpec(
            num_scalar_prefetch=2,
            grid=(block_rows // per_step,),
            in_specs=[ANY] * n_mp
            + [
                pl.BlockSpec((per_step * blk, tok_rows), lambda i, a, b: (i, 0)),
                pl.BlockSpec((per_step * blk, rank), lambda i, a, b: (i, 0)),
            ],
            out_specs=[
                pl.BlockSpec((col_blocks, rank, blk), lambda i, a, b: (0, 0, 0)),
                pl.BlockSpec((8, 128), lambda i, a, b: (0, 0)),
            ],
            scratch_shapes=[
                pltpu.VMEM((n_mp, tok_rows, shard_cols), BF),
                pltpu.SemaphoreType.DMA((n_mp,)),
            ],
        ),
        out_shape=[
            jax.ShapeDtypeStruct((col_blocks, rank, blk), F32),
            jax.ShapeDtypeStruct((8, 128), F32),
        ],
        compiler_params=params(),
        cost_estimate=SMALL,
        name="compress",
    )(pat_all, place(pattern).reshape(-1), *own, hid_t, proj_all)

    partial_c, y_x, y_core, hid_got, sk_own, top = lax.optimization_barrier(
        (partial_c, y_x, y_core, hid_got, sk_own, top)
    )
    tops = jnp.concatenate([top, jnp.broadcast_to(top_hidden, top.shape)], axis=0)
    tops = jnp.maximum(tops, swap(tops, "dp", 1))
    if n_dp <= 8:
        others = [swap(tops, "dp", bits) for bits in range(2, n_dp, 2)]
        tops = functools.reduce(jnp.maximum, others, tops)
    else:
        for bit in range(1, n_dp.bit_length() - 1):
            tops = jnp.maximum(tops, swap(tops, "dp", 1 << bit))
    bound = jnp.maximum(jnp.max(tops[:8]) * jnp.max(tops[8:]), 1e-30)
    y_group = [y_own, y_core, y_x, swap(y_x, "mp", 1)]
    quarters = partial_c.reshape(n_mp, per_shard, rank, blk)
    got_far = swap(quarters[3].astype(F16), "mp", 1)
    got_near = swap(quarters[1].astype(F16), "mp", 1)
    far_half = (quarters[2] + got_far.astype(F32)).astype(F16)
    near_half = quarters[0] + got_near.astype(F32)
    far_half, near_half, y_last = lax.optimization_barrier((far_half, near_half, y_group[3]))
    y_group[3] = y_last
    far_sum = swap(far_half, "mp", 2)

    grad_scale = (16384.0 / all_tokens) / bound
    half_rows = outer * dev_rows
    devices = 2 * jnp.arange(outer, dtype=jnp.int32) + side
    window, _, _ = windows_of(dp * dev_rows, dev_rows, blk)
    window_starts, window_blocks = jax.vmap(lambda d: windows_of(d * dev_rows, dev_rows, blk)[1:])(
        devices
    )
    n_windows = window_starts.shape[1]
    pat_half = jnp.take(pattern_rel, window_blocks.reshape(-1), axis=0).reshape(-1)
    hid_type = BF if window % 32 == 0 else F32

    def pair_grad(blocks, shards):
        order = jnp.bitwise_xor(jnp.asarray(blocks, jnp.int32), dp // 2)
        out = pl.pallas_call(
            functools.partial(grad_kernel, n_mp, per_shard, blk, window, n_windows),
            grid_spec=pltpu.PrefetchScalarGridSpec(
                num_scalar_prefetch=3,
                grid=(len(blocks),),
                in_specs=[ANY] * (2 * n_mp)
                + [pl.BlockSpec((dev_rows, tok_rows), lambda i, o, a, b: (o[i], 0))] * 2,
                out_specs=pl.BlockSpec((dev_rows, slots * blk), lambda i, o, a, b: (i, 0)),
                scratch_shapes=[
                    pltpu.VMEM((n_mp, 2 * tok_rows, shard_cols), BF),
                    pltpu.SemaphoreType.DMA((2 * n_mp,)),
                ],
            ),
            out_shape=jax.ShapeDtypeStruct((len(blocks) * dev_rows, slots * blk), F32),
            compiler_params=params(),
            cost_estimate=SMALL,
            name="pair_grad",
        )(
            order,
            window_starts.reshape(-1),
            pat_half,
            *shards,
            hid_own.reshape(half_rows, tok_rows).astype(hid_type),
            hid_got.reshape(half_rows, tok_rows).astype(hid_type),
        )
        out = out.reshape(len(blocks), dev_rows, slots * blk)
        return {block: out[i] for i, block in enumerate(blocks)}

    crossing = [i for i in range(outer) if i & 2][::-1]
    staying = [i for i in range(outer) if not i & 2][::-1]
    sums = pair_grad(crossing, own + y_group)
    sent = {i: (sums[i] * grad_scale).astype(F16) for i in crossing if i & 1}
    got = {i: swap(sent[i], "dp", 2) for i in crossing if i & 1}
    sums.update(pair_grad(staying, own[:3] + [after(own[3], *sent.values())] + y_group))
    sent = {i: (sums[i] * grad_scale).astype(F16) for i in staying if i & 1}
    got.update({i: swap(sent[i], "dp", 2) for i in staying if i & 1})
    far_sum, near_half, _ = lax.optimization_barrier((far_sum, near_half, list(sent.values())))

    quarter = near_half + far_sum.astype(F32)
    pieces = quarter.astype(F16).reshape(n_dp, per_shard * rank // n_dp, blk)
    pieces = lax.all_to_all(pieces, "dp", 0, 0)

    sums = {i: part * grad_scale for i, part in sums.items() if not i & 1}
    level = 1
    while level < outer:
        if level > 1:
            got = {i: swap(sums[i].astype(F16), "dp", 2 * level) for i in sums if i & level}
        if 2 * level < outer:
            for i in got:
                sums[i ^ level] = sums[i ^ level] + got[i].astype(F32)
            sums = {i: part for i, part in sums.items() if not i & level}
        if level == 1 and outer > 2:
            sums[2], pieces = lax.optimization_barrier((sums[2].astype(F16), pieces))
        level *= 2

    input_grad = pl.pallas_call(
        functools.partial(input_grad_kernel, n_mp, per_shard, blk, per_step),
        grid_spec=pltpu.PrefetchScalarGridSpec(
            num_scalar_prefetch=1,
            grid=(block_rows // per_step,),
            in_specs=[ANY] * n_mp
            + [pl.BlockSpec((per_step * blk, slots * blk), lambda i, pat: (i, 0))],
            out_specs=pl.BlockSpec((tok_rows, per_step * blk), lambda i, pat: (0, i)),
            scratch_shapes=[
                pltpu.VMEM((n_mp, tok_rows, shard_cols), BF),
                pltpu.SemaphoreType.DMA((n_mp,)),
            ],
        ),
        out_shape=jax.ShapeDtypeStruct((tok_rows, mp_rows), BF),
        compiler_params=params(),
        cost_estimate=SMALL,
        name="input_grad",
    )(pat_all, *own, after(weights_2d, quarter))
    pieces, input_grad = lax.optimization_barrier((pieces, input_grad))

    piece = jnp.sum(pieces.astype(F32), axis=0).astype(F16)
    quarter16 = over_dp(piece).reshape(per_shard, rank, blk)

    sk_own = after(sk_own, quarter)
    sk_far = swap(sk_own, "mp", 2)
    sk_parts = [sk_own, swap(sk_own, "mp", 1), sk_far, swap(sk_far, "mp", 1)]
    if width < blk:
        sk_abs = jnp.take(
            jnp.stack(sk_parts), jnp.bitwise_xor(jnp.arange(n_mp, dtype=jnp.int32), mp), axis=0
        )
        sk_abs = sk_abs.reshape(n_mp, col_blocks, blk // width // n_mp, rank, width)
        sk_abs = sk_abs.transpose(1, 3, 2, 0, 4).reshape(n_mp, per_shard, rank, blk)
        sk_parts = [
            lax.dynamic_index_in_dim(sk_abs, jnp.bitwise_xor(mp, i), 0, keepdims=False)
            for i in range(n_mp)
        ]
    oh, ol = split2_xla(sk_parts[0].astype(F32))
    sk_high, sk_low = split2_xla(jnp.concatenate(sk_parts, axis=0).astype(F32))

    sk_per = sk_high.shape[2] // blk
    sketch_gram = pl.pallas_call(
        sketch_gram_kernel,
        in_specs=[VMEM] * 2,
        out_specs=VMEM,
        out_shape=jax.ShapeDtypeStruct((rank, rank), F32),
        compiler_params=params(),
        cost_estimate=SMALL,
        name="sketch_gram",
    )(sk_high, sk_low)
    quarter16, sketch_gram, sk_high, sk_low, oh, ol = lax.optimization_barrier(
        (quarter16, sketch_gram, sk_high, sk_low, oh, ol)
    )
    qh, ql = split2_xla(quarter16.astype(F32))
    cross = pl.pallas_call(
        cross_gram_kernel,
        in_specs=[VMEM] * 4,
        out_specs=VMEM,
        out_shape=jax.ShapeDtypeStruct((rank, 2 * rank), F32),
        compiler_params=params(),
        cost_estimate=SMALL,
        name="cross_gram",
    )(qh, ql, oh, ol)
    cross = cross + swap(cross, "mp", 2)
    cross = cross + swap(cross, "mp", 1)
    mixing = pl.pallas_call(
        mixing_kernel,
        in_specs=[VMEM] * 2,
        out_specs=VMEM,
        out_shape=jax.ShapeDtypeStruct((2 * rank, 2 * rank), F32),
        compiler_params=params(),
        cost_estimate=SMALL,
        name="mixing",
    )(sketch_gram, cross)

    quarter16 = after(quarter16, cross)
    far = swap(quarter16, "mp", 2)
    comp_parts = [quarter16, swap(quarter16, "mp", 1), far, swap(far, "mp", 1)]
    comp_parts = [split2_xla(part.astype(F32)) for part in comp_parts]
    comp_parts = [part[0] for part in comp_parts] + [part[1] for part in comp_parts]

    kept, mixing, comp_parts, sk_high, sk_low = lax.optimization_barrier(
        (sums[0], mixing, comp_parts, sk_high, sk_low)
    )
    for part in got.values():
        kept = kept + part.astype(F32)
    grad = kept * (bound / 16384.0)
    _, my_starts, my_blocks = windows_of(dp * dev_rows, dev_rows, blk)
    my_pat = jnp.take(place(pattern), my_blocks, axis=0).reshape(-1)
    smem = pl.BlockSpec(memory_space=pltpu.SMEM)
    direction = pl.pallas_call(
        functools.partial(direction_kernel, sk_per, window, n_windows),
        in_specs=[smem] * 2 + [VMEM] * 4 + [ANY] * len(comp_parts),
        out_specs=VMEM,
        out_shape=jax.ShapeDtypeStruct((dev_rows, slots, blk), F32),
        scratch_shapes=[
            pltpu.VMEM((col_blocks, rank, blk), BF),
            pltpu.VMEM((col_blocks, rank, blk), BF),
            pltpu.SemaphoreType.DMA((len(comp_parts),)),
        ],
        compiler_params=params(),
        cost_estimate=SMALL,
        name="direction",
    )(my_starts, my_pat, grad, mixing, sk_high, sk_low, *comp_parts)
    return (input_grad, direction.reshape(1, dev_rows, slots, blk))


def solution(mesh):
    return jax.shard_map(
        per_device,
        mesh=mesh,
        in_specs=(
            P("mp", None, None),
            P("dp", "mp"),
            P("dp", "mp"),
            P(None, ("dp", "mp")),
            P(None, "mp", "dp"),
            P("mp", None),
        ),
        out_specs=(P("dp", "mp"), P("mp", "dp", None, None)),
        check_vma=False,
    )
```

```python
import functools
import math

import jax
import jax.numpy as jnp
from jax import lax
from jax.experimental import pallas as pl
from jax.experimental.pallas import tpu as pltpu
from jax.sharding import PartitionSpec as P

NS_STEPS = 5
SHIFT_EPS = 0.0001
PROJ_SCALE = 1024.0
SLOTS = 8

BF = jnp.bfloat16
F16 = jnp.float16
F32 = jnp.float32
HIGHEST = lax.Precision.HIGHEST
VMEM = pl.BlockSpec(memory_space=pltpu.VMEM)
ANY = pl.BlockSpec(memory_space=pl.ANY)


SMALL = pl.CostEstimate(flops=1, bytes_accessed=1, transcendentals=0)


def params(mib=48):
    return pltpu.CompilerParams(vmem_limit_bytes=mib * 1024 * 1024)


def dot(a, b):
    return jnp.dot(a, b, preferred_element_type=F32)


def dot_nt(a, b):
    return lax.dot_general(a, b, (((1,), (1,)), ((), ())), preferred_element_type=F32)


def split2(value):
    high = value.astype(BF)
    return high, (value - high.astype(F32)).astype(BF)


def split2_xla(value):
    high = lax.reduce_precision(value, exponent_bits=8, mantissa_bits=7)
    return high.astype(BF), (value - high).astype(BF)


def load_all(pairs, sems):
    copies = [pltpu.make_async_copy(src, dst, sems.at[i]) for i, (src, dst) in enumerate(pairs)]
    for copy in copies:
        copy.start()
    for copy in copies:
        copy.wait()


def column_block(held, block, per_shard, size):
    shard = block // per_shard
    offset = pl.multiple_of((block - shard * per_shard) * size, size)
    return held[shard, :, pl.ds(offset, size)]


def compress_kernel(n_shards, per_shard, scale, per_step, pat, pat_out, *refs):
    shards = refs[:n_shards]
    hid_ref, proj_ref, out_ref, held, sems = refs[n_shards:]
    blk = out_ref.shape[1]

    @pl.when(pl.program_id(0) == 0)
    def _():
        load_all([(ref, held.at[i]) for i, ref in enumerate(shards)], sems)
        out_ref[...] = jnp.zeros_like(out_ref)

    first = pl.program_id(0) * per_step
    lefts = []
    for u in range(per_step):
        span = slice(u * blk, (u + 1) * blk)
        hid = hid_ref[span, :]
        ph, pl_ = split2(proj_ref[span, :].T)
        lefts.append(((dot(ph, hid) + dot(pl_, hid)) * scale).astype(BF))
    parts = []
    for u in range(per_step):
        cols = [pat[(first + u) * SLOTS + j] for j in range(SLOTS)]
        for j in range(0, SLOTS, 2):
            chosen = jnp.concatenate(
                [column_block(held, c, per_shard, blk) for c in cols[j : j + 2]], axis=1
            )
            parts.append(dot(lefts[u], chosen))
    for u in range(per_step):
        outs = [pat_out[(first + u) * SLOTS + j] for j in range(SLOTS)]
        sums = [
            out_ref[c] + parts[(u * SLOTS + j) // 2][:, (j % 2) * blk : (j % 2 + 1) * blk]
            for j, c in enumerate(outs)
        ]
        for c, total in zip(outs, sums):
            out_ref[c] = total


def grad_kernel(n_shards, per_shard, blk, window, n_windows, order, starts, pat, *refs):
    shards = refs[: 2 * n_shards]
    own_ref, got_ref, out_ref, top_ref, held, sems = refs[2 * n_shards :]
    toks = own_ref.shape[1]

    @pl.when(pl.program_id(0) == 0)
    def _():
        load_all(
            [
                (ref, held.at[i % n_shards, pl.ds(i // n_shards * toks, toks)])
                for i, ref in enumerate(shards)
            ],
            sems,
        )
        top_ref[...] = jnp.zeros_like(top_ref)

    top = top_ref[...]
    for w in range(n_windows):
        index = order[pl.program_id(0)] * n_windows + w
        rows = pl.ds(pl.multiple_of(starts[index], window // 2 if window >= 32 else 8), window)
        hid = jnp.concatenate([own_ref[rows, :], got_ref[rows, :]], axis=1).astype(BF)
        for j in range(0, SLOTS, 2):
            chosen = jnp.concatenate(
                [column_block(held, pat[index * SLOTS + j + i], per_shard, blk) for i in (0, 1)],
                axis=1,
            )
            part = dot(hid, chosen)
            out_ref[rows, j * blk : (j + 2) * blk] = part
            size = jnp.abs(part)
            for i in range(0, window, 8):
                top = jnp.maximum(top, size[i : i + 8])
    top_ref[...] = top


def input_grad_kernel(n_shards, per_shard, blk, per_step, pat, *refs):
    shards = refs[:n_shards]
    w_ref, out_ref, held, sems = refs[n_shards:]

    @pl.when(pl.program_id(0) == 0)
    def _():
        load_all([(ref, held.at[i]) for i, ref in enumerate(shards)], sems)

    for u in range(per_step):
        row = pl.program_id(0) * per_step + u
        chosen = jnp.concatenate(
            [column_block(held, pat[row * SLOTS + j], per_shard, blk) for j in range(SLOTS)], axis=1
        )
        span = slice(u * blk, (u + 1) * blk)
        out_ref[:, span] = dot_nt(chosen, w_ref[span, :]).astype(BF)


def sketch_gram_kernel(sh_ref, sl_ref, out_ref):
    out_ref[...] = jnp.zeros_like(out_ref)
    for s in range(sh_ref.shape[0]):
        high, low = sh_ref[s], sl_ref[s]
        out_ref[...] += dot_nt(high, high) + (dot_nt(high, low) + dot_nt(low, high))


def cross_gram_kernel(ch_ref, cl_ref, sh_ref, sl_ref, out_ref):
    rank = ch_ref.shape[1]
    per = ch_ref.shape[0] // sh_ref.shape[0]
    with_sketch = jnp.zeros((rank, rank), F32)
    with_self = jnp.zeros((rank, rank), F32)
    for s in range(sh_ref.shape[0]):
        high = jnp.concatenate([ch_ref[per * s + b] for b in range(per)], axis=1)
        low = jnp.concatenate([cl_ref[per * s + b] for b in range(per)], axis=1)
        sh, sl = sh_ref[s], sl_ref[s]
        with_sketch += dot_nt(high, sh) + (dot_nt(high, sl) + dot_nt(low, sh))
        with_self += dot_nt(high, high) + (dot_nt(high, low) + dot_nt(low, high))
    out_ref[:, :rank] = with_sketch
    out_ref[:, rank:] = with_self


def mixing_kernel(ss_ref, cross_ref, out_ref):
    rank = ss_ref.shape[0]
    size = 2 * rank
    sqrt_eps = math.sqrt(SHIFT_EPS)

    def mm(a, b):
        return jnp.dot(a, b, precision=HIGHEST, preferred_element_type=F32)

    cross = cross_ref[...]
    gram = jnp.concatenate(
        [jnp.concatenate([ss_ref[...], cross[:, :rank].T], axis=1), cross], axis=0
    )
    rows = lax.broadcasted_iota(jnp.int32, (size, size), 0)
    cols = lax.broadcasted_iota(jnp.int32, (size, size), 1)
    identity = jnp.where(rows == cols, 1.0, 0.0).astype(F32)
    shifted = gram + SHIFT_EPS * identity
    frobenius = jnp.sqrt(jnp.sum(shifted * shifted, keepdims=True))
    root = shifted / frobenius
    inverse = identity
    for step in range(NS_STEPS):
        product = root if step == 0 else mm(inverse, root)
        middle = 0.5 * (3.0 * identity - product)
        root = mm(root, middle)
        inverse = middle if step == 0 else mm(middle, inverse)
    sqrt_fro = jnp.sqrt(frobenius)
    half = 0.5 * sqrt_fro * (root + root.T) + sqrt_eps * identity
    guess = inverse / (sqrt_fro + sqrt_eps * 1.5**NS_STEPS)

    def residual(x):
        r = identity - mm(half, x)
        return r, jnp.max(jnp.abs(r))

    def keep_going(state):
        return jnp.logical_and(state[3] < 48, state[2] > 2e-6)

    def improve(state):
        x, r, _, count = state
        x = x + mm(x, r)
        r, size = residual(x)
        return x, r, size, count + 1

    r, top = residual(guess)
    x, r, _, _ = lax.while_loop(keep_going, improve, (guess, r, top, jnp.int32(0)))
    x = x + mm(x, r)
    out_ref[...] = -mm(inverse, x) / (sqrt_eps * sqrt_fro)


def direction_kernel(per, window, n_windows, starts, pat, *refs):
    g_ref, m_ref, skh, skl = refs[:4]
    parts, (out_ref, cph, cpl, sems) = refs[4:-4], refs[-4:]
    blk = cph.shape[2]
    half = len(parts) // 2
    pairs, at = [], 0
    for i in range(half):
        size = parts[i].shape[0]
        pairs += [(parts[i], cph.at[pl.ds(at, size)]), (parts[half + i], cpl.at[pl.ds(at, size)])]
        at += size
    load_all(pairs, sems)

    def gathered(sk, cp, c):
        shard = c // per
        offset = pl.multiple_of((c - shard * per) * blk, blk)
        return jnp.concatenate([sk[shard, :, pl.ds(offset, blk)], cp[c]], axis=0)

    for w in range(n_windows):
        rows = pl.ds(pl.multiple_of(starts[w], window // 2 if window >= 32 else 8), window)
        cols = [pat[w * SLOTS + k] for k in range(SLOTS)]
        g = g_ref[rows, :]
        g_high = g.astype(BF).astype(F32)
        g_both = jnp.concatenate([g_high, g - g_high], axis=0).astype(BF)
        high = [gathered(skh, cph, c) for c in cols]
        low = [gathered(skl, cpl, c) for c in cols]
        both = dot_nt(g_both, jnp.concatenate(high, axis=1))
        projected = both[:window] + both[window:]
        projected += dot_nt(g_high.astype(BF), jnp.concatenate(low, axis=1))
        mixed = jnp.dot(projected, m_ref[...], precision=HIGHEST, preferred_element_type=F32)
        mixed_high = mixed.astype(BF).astype(F32)
        mixed_both = jnp.concatenate([mixed_high, mixed - mixed_high], axis=0).astype(BF)
        for k in range(0, SLOTS, 2):
            both = dot(mixed_both, jnp.concatenate(high[k : k + 2], axis=1))
            corr = both[:window] + both[window:]
            corr += dot(mixed_high.astype(BF), jnp.concatenate(low[k : k + 2], axis=1))
            corr += g[:, k * blk : (k + 2) * blk] * (1.0 / math.sqrt(SHIFT_EPS))
            out_ref[rows, k, :] = corr[:, :blk]
            out_ref[rows, k + 1, :] = corr[:, blk:]


def windows_of(start, dev_rows, blk):
    group = math.gcd(dev_rows, blk)
    if dev_rows % blk == blk // 2 and dev_rows > blk:
        whole = dev_rows // blk
        odd = (start // group) % 2
        later = odd * group + blk * jnp.arange(whole, dtype=jnp.int32)
        first = jnp.where(odd == 1, 0, dev_rows - blk)
        first_row = jnp.where(odd == 1, start, start + dev_rows - group)
        starts = jnp.concatenate([first[None], later])
        inside = jnp.concatenate([first_row[None], start + later])
        return blk, starts.astype(jnp.int32), (inside // blk).astype(jnp.int32)
    starts = group * jnp.arange(dev_rows // group, dtype=jnp.int32)
    return group, starts, (start + starts) // blk


def per_device(weights, hidden, cotangent, sketch, projection, pattern):
    tok_rows = hidden.shape[0]
    mp_rows, slots, blk = weights.shape
    block_rows = mp_rows // blk
    n_dp, n_mp = lax.axis_size("dp"), lax.axis_size("mp")
    dev_rows = mp_rows // n_dp
    all_tokens = tok_rows * n_dp
    rank = sketch.shape[0]
    shard_cols = cotangent.shape[1]
    per_shard = shard_cols // blk
    col_blocks = per_shard * n_mp
    outer = n_dp // 2
    per_step = 4 if block_rows % 4 == 0 else 1
    dp, mp = lax.axis_index("dp"), lax.axis_index("mp")
    side = dp % 2

    def swap(x, axis, bit):
        size = lax.axis_size(axis)
        return lax.ppermute(x, axis, [(i, i ^ bit) for i in range(size)])

    def after(x, *others):
        return lax.optimization_barrier((x, *others))[0]

    def over_dp(x):
        return lax.all_to_all(jnp.broadcast_to(x[None], (n_dp, *x.shape)), "dp", 0, 0)

    width = sketch.shape[1]
    core_half = swap(cotangent, "mp", 1)
    hid_t = hidden.T
    hid_parts = hid_t.reshape(outer, 2, dev_rows, tok_rows)
    hid_own = lax.dynamic_index_in_dim(hid_parts, side, 1, keepdims=False)
    hid_send = lax.dynamic_index_in_dim(hid_parts, 1 - side, 1, keepdims=False)
    proj_t = (projection.reshape(rank, dev_rows).T * PROJ_SCALE).astype(F16)
    x_part, y_part = swap(cotangent, "mp", 2), swap(cotangent, "dp", 1)
    weights_2d = weights.reshape(mp_rows, slots * blk)
    proj_all = over_dp(proj_t).reshape(mp_rows, rank).astype(F32)
    x_half, y_own, core_half, hid_t, hid_own, hid_send, weights_2d, proj_all = (
        lax.optimization_barrier(
            (
                x_part,
                y_part,
                core_half,
                hid_t,
                hid_own,
                hid_send,
                weights_2d,
                proj_all,
            )
        )
    )
    own = [cotangent, core_half, x_half, swap(x_half, "mp", 1)]
    y_x = swap(y_own, "mp", 2)
    y_core = swap(y_own, "mp", 1)
    hid_got = swap(hid_send, "dp", 1)
    pattern_rel = jnp.bitwise_xor(pattern, mp * per_shard)

    def place(block):
        if width < blk:
            return jnp.bitwise_xor(block, mp * per_shard)
        per = width // blk
        shard, rest = block // per, block % per
        near_mp = jnp.bitwise_xor(shard % n_mp, mp)
        return (near_mp * n_dp + shard // n_mp) * per + rest

    pat_all = pattern_rel.reshape(-1)
    partial_c = pl.pallas_call(
        functools.partial(
            compress_kernel,
            n_mp,
            per_shard,
            1.0 / (PROJ_SCALE * all_tokens),
            per_step,
        ),
        grid_spec=pltpu.PrefetchScalarGridSpec(
            num_scalar_prefetch=2,
            grid=(block_rows // per_step,),
            in_specs=[ANY] * n_mp
            + [
                pl.BlockSpec((per_step * blk, tok_rows), lambda i, a, b: (i, 0)),
                pl.BlockSpec((per_step * blk, rank), lambda i, a, b: (i, 0)),
            ],
            out_specs=pl.BlockSpec((col_blocks, rank, blk), lambda i, a, b: (0, 0, 0)),
            scratch_shapes=[
                pltpu.VMEM((n_mp, tok_rows, shard_cols), BF),
                pltpu.SemaphoreType.DMA((n_mp,)),
            ],
        ),
        out_shape=jax.ShapeDtypeStruct((col_blocks, rank, blk), F32),
        compiler_params=params(),
        cost_estimate=SMALL,
        name="compress",
    )(pat_all, place(pattern).reshape(-1), *own, hid_t, proj_all)

    partial_c, y_x, y_core, hid_got = lax.optimization_barrier((partial_c, y_x, y_core, hid_got))
    y_group = [y_own, y_core, y_x, swap(y_x, "mp", 1)]
    quarters = partial_c.reshape(n_mp, per_shard, rank, blk)
    to_far, to_near = quarters[3].astype(F16), quarters[1].astype(F16)
    got_far, got_near = swap(to_far, "mp", 1), swap(to_near, "mp", 1)
    y_group[3] = after(y_group[3], to_far, to_near)

    half_rows = outer * dev_rows
    devices = 2 * jnp.arange(outer, dtype=jnp.int32) + side
    window, _, _ = windows_of(dp * dev_rows, dev_rows, blk)
    window_starts, window_blocks = jax.vmap(lambda d: windows_of(d * dev_rows, dev_rows, blk)[1:])(
        devices
    )
    n_windows = window_starts.shape[1]
    pat_half = jnp.take(pattern_rel, window_blocks.reshape(-1), axis=0).reshape(-1)
    hid_type = BF if window % 32 == 0 else F32

    def pair_grad(blocks, shards):
        order = jnp.bitwise_xor(jnp.asarray(blocks, jnp.int32), dp // 2)
        out, top = pl.pallas_call(
            functools.partial(grad_kernel, n_mp, per_shard, blk, window, n_windows),
            grid_spec=pltpu.PrefetchScalarGridSpec(
                num_scalar_prefetch=3,
                grid=(len(blocks),),
                in_specs=[ANY] * (2 * n_mp)
                + [pl.BlockSpec((dev_rows, tok_rows), lambda i, o, a, b: (o[i], 0))] * 2,
                out_specs=[
                    pl.BlockSpec((dev_rows, slots * blk), lambda i, o, a, b: (i, 0)),
                    pl.BlockSpec((8, 2 * blk), lambda i, o, a, b: (0, 0)),
                ],
                scratch_shapes=[
                    pltpu.VMEM((n_mp, 2 * tok_rows, shard_cols), BF),
                    pltpu.SemaphoreType.DMA((2 * n_mp,)),
                ],
            ),
            out_shape=[
                jax.ShapeDtypeStruct((len(blocks) * dev_rows, slots * blk), F32),
                jax.ShapeDtypeStruct((8, 2 * blk), F32),
            ],
            compiler_params=params(),
            cost_estimate=SMALL,
            name="pair_grad",
        )(
            order,
            window_starts.reshape(-1),
            pat_half,
            *shards,
            hid_own.reshape(half_rows, tok_rows).astype(hid_type),
            hid_got.reshape(half_rows, tok_rows).astype(hid_type),
        )
        out = out.reshape(len(blocks), dev_rows, slots * blk)
        top = jnp.max(top)
        return {block: (out[i], top) for i, block in enumerate(blocks)}

    def pack(part):
        value, top = part
        exponent = 13.0 - jnp.floor(jnp.log2(jnp.maximum(top, 1e-30)))
        below = jnp.broadcast_to(exponent, (16, value.shape[1]))
        return jnp.concatenate([value * jnp.exp2(exponent), below], axis=0).astype(F16)

    def unpack(message, first=0):
        exponent = lax.dynamic_slice(message, (dev_rows + first, 0), (8, 128))[0, 0].astype(F32)
        value = message[:dev_rows].astype(F32) * jnp.exp2(-exponent)
        return value, jnp.exp2(14.0 - exponent)

    def add(part, message, first=0):
        value, top = unpack(message, first)
        return part[0] + value, part[1] + top

    crossing = [i for i in range(outer) if i & 2][::-1]
    staying = [i for i in range(outer) if not i & 2][::-1]
    sums = pair_grad(crossing, own + y_group)
    sent = {i: pack(sums[i]) for i in crossing if i & 1}
    got_far, got_near, *before = lax.optimization_barrier((got_far, got_near, *sent.values()))
    sent = dict(zip(sent, before))
    got = {i: swap(sent[i], "dp", 2) for i in sent}
    far_half = (quarters[2] + got_far.astype(F32)).astype(F16)
    near_half = quarters[0] + got_near.astype(F32)
    far_half, near_half, y_group[3] = lax.optimization_barrier((far_half, near_half, y_group[3]))
    far_sum = swap(far_half, "mp", 2)
    sums.update(pair_grad(staying, own + y_group))
    sent = {i: pack(sums[i]) for i in staying if i & 1}
    got.update({i: swap(sent[i], "dp", 2) for i in staying if i & 1})
    far_sum, near_half, _ = lax.optimization_barrier((far_sum, near_half, list(sent.values())))

    quarter = near_half + far_sum.astype(F32)
    pieces = quarter.astype(F16).reshape(n_dp, per_shard * rank // n_dp, blk)
    pieces = lax.all_to_all(pieces, "dp", 0, 0)

    last = [got.pop(1)]
    level = 1
    while level < outer:
        if level > 1:
            got = {i: swap(pack(sums[i]), "dp", 2 * level) for i in sums if i & level}
        for i in got:
            sums[i ^ level] = add(sums[i ^ level], got[i])
        sums = {i: part for i, part in sums.items() if not i & level}
        if outer == 4:
            crossed, pieces = lax.optimization_barrier((pack(sums[2]), pieces))
            last.append(swap(crossed, "dp", 4))
            break
        level *= 2


    piece = jnp.sum(pieces.astype(F32), axis=0).astype(F16)
    quarter16 = over_dp(piece).reshape(per_shard, rank, blk)

    sk_own = after(lax.all_gather(sketch, "dp"), quarter).astype(F16)
    sk_far = swap(sk_own, "mp", 2)
    sk_parts = [sk_own, swap(sk_own, "mp", 1), sk_far, swap(sk_far, "mp", 1)]
    if width < blk:
        sk_abs = jnp.take(
            jnp.stack(sk_parts), jnp.bitwise_xor(jnp.arange(n_mp, dtype=jnp.int32), mp), axis=0
        )
        sk_abs = sk_abs.reshape(n_mp, col_blocks, blk // width // n_mp, rank, width)
        sk_abs = sk_abs.transpose(1, 3, 2, 0, 4).reshape(n_mp, per_shard, rank, blk)
        sk_parts = [
            lax.dynamic_index_in_dim(sk_abs, jnp.bitwise_xor(mp, i), 0, keepdims=False)
            for i in range(n_mp)
        ]
    oh, ol = split2_xla(sk_parts[0].astype(F32))
    sk_high, sk_low = split2_xla(jnp.concatenate(sk_parts, axis=0).astype(F32))

    sk_per = sk_high.shape[2] // blk
    sketch_gram = pl.pallas_call(
        sketch_gram_kernel,
        in_specs=[VMEM] * 2,
        out_specs=VMEM,
        out_shape=jax.ShapeDtypeStruct((rank, rank), F32),
        compiler_params=params(),
        cost_estimate=SMALL,
        name="sketch_gram",
    )(sk_high, sk_low)
    quarter16, sketch_gram, sk_high, sk_low, oh, ol = lax.optimization_barrier(
        (quarter16, sketch_gram, sk_high, sk_low, oh, ol)
    )
    qh, ql = split2_xla(quarter16.astype(F32))
    cross = pl.pallas_call(
        cross_gram_kernel,
        in_specs=[VMEM] * 4,
        out_specs=VMEM,
        out_shape=jax.ShapeDtypeStruct((rank, 2 * rank), F32),
        compiler_params=params(),
        cost_estimate=SMALL,
        name="cross_gram",
    )(qh, ql, oh, ol)
    cross = cross + swap(cross, "mp", 2)
    cross = cross + swap(cross, "mp", 1)
    input_grad = pl.pallas_call(
        functools.partial(input_grad_kernel, n_mp, per_shard, blk, per_step),
        grid_spec=pltpu.PrefetchScalarGridSpec(
            num_scalar_prefetch=1,
            grid=(block_rows // per_step,),
            in_specs=[ANY] * n_mp
            + [pl.BlockSpec((per_step * blk, slots * blk), lambda i, pat: (i, 0))],
            out_specs=pl.BlockSpec((tok_rows, per_step * blk), lambda i, pat: (0, i)),
            scratch_shapes=[
                pltpu.VMEM((n_mp, tok_rows, shard_cols), BF),
                pltpu.SemaphoreType.DMA((n_mp,)),
            ],
        ),
        out_shape=jax.ShapeDtypeStruct((tok_rows, mp_rows), BF),
        compiler_params=params(),
        cost_estimate=SMALL,
        name="input_grad",
    )(pat_all, *own, after(weights_2d, cross))
    cross, input_grad = lax.optimization_barrier((cross, input_grad))
    mixing = pl.pallas_call(
        mixing_kernel,
        in_specs=[VMEM] * 2,
        out_specs=VMEM,
        out_shape=jax.ShapeDtypeStruct((2 * rank, 2 * rank), F32),
        compiler_params=params(),
        cost_estimate=SMALL,
        name="mixing",
    )(sketch_gram, cross)

    quarter16 = after(quarter16, cross)
    far = swap(quarter16, "mp", 2)
    comp_parts = [quarter16, swap(quarter16, "mp", 1), far, swap(far, "mp", 1)]
    comp_parts = [split2_xla(part.astype(F32)) for part in comp_parts]
    comp_parts = [part[0] for part in comp_parts] + [part[1] for part in comp_parts]

    kept, mixing, first = lax.optimization_barrier((sums[0], mixing, jnp.int32(0)))
    for message in last:
        kept = add(kept, message, first)
    grad = kept[0] * (1.0 / all_tokens)
    _, my_starts, my_blocks = windows_of(dp * dev_rows, dev_rows, blk)
    my_pat = jnp.take(place(pattern), my_blocks, axis=0).reshape(-1)
    smem = pl.BlockSpec(memory_space=pltpu.SMEM)
    direction = pl.pallas_call(
        functools.partial(direction_kernel, sk_per, window, n_windows),
        in_specs=[smem] * 2 + [VMEM] * 4 + [ANY] * len(comp_parts),
        out_specs=VMEM,
        out_shape=jax.ShapeDtypeStruct((dev_rows, slots, blk), F32),
        scratch_shapes=[
            pltpu.VMEM((col_blocks, rank, blk), BF),
            pltpu.VMEM((col_blocks, rank, blk), BF),
            pltpu.SemaphoreType.DMA((len(comp_parts),)),
        ],
        compiler_params=params(),
        cost_estimate=SMALL,
        name="direction",
    )(my_starts, my_pat, grad, mixing, sk_high, sk_low, *comp_parts)
    return (input_grad, direction.reshape(1, dev_rows, slots, blk))


def solution(mesh):
    return jax.shard_map(
        per_device,
        mesh=mesh,
        in_specs=(
            P("mp", None, None),
            P("dp", "mp"),
            P("dp", "mp"),
            P(None, ("dp", "mp")),
            P(None, "mp", "dp"),
            P("mp", None),
        ),
        out_specs=(P("dp", "mp"), P("mp", "dp", None, None)),
        check_vma=False,
    )
```

```python
import functools
import math

import jax
import jax.numpy as jnp
from jax import lax
from jax.experimental import pallas as pl
from jax.experimental.pallas import tpu as pltpu
from jax.sharding import PartitionSpec as P

NS_STEPS = 5
SHIFT_EPS = 0.0001
PROJ_SCALE = 1024.0
SLOTS = 8

BF = jnp.bfloat16
F16 = jnp.float16
F32 = jnp.float32
HIGHEST = lax.Precision.HIGHEST
VMEM = pl.BlockSpec(memory_space=pltpu.VMEM)
ANY = pl.BlockSpec(memory_space=pl.ANY)


SMALL = pl.CostEstimate(flops=1, bytes_accessed=1, transcendentals=0)


def params(mib=48):
    return pltpu.CompilerParams(vmem_limit_bytes=mib * 1024 * 1024)


def dot(a, b):
    return jnp.dot(a, b, preferred_element_type=F32)


def dot_nt(a, b):
    return lax.dot_general(a, b, (((1,), (1,)), ((), ())), preferred_element_type=F32)


def split2(value):
    high = value.astype(BF)
    return high, (value - high.astype(F32)).astype(BF)


def split2_xla(value):
    high = lax.reduce_precision(value, exponent_bits=8, mantissa_bits=7)
    return high.astype(BF), (value - high).astype(BF)


def load_all(pairs, sems):
    copies = [pltpu.make_async_copy(src, dst, sems.at[i]) for i, (src, dst) in enumerate(pairs)]
    for copy in copies:
        copy.start()
    for copy in copies:
        copy.wait()


def column_block(held, block, per_shard, size):
    shard = block // per_shard
    offset = pl.multiple_of((block - shard * per_shard) * size, size)
    return held[shard, :, pl.ds(offset, size)]


def compress_kernel(n_shards, per_shard, scale, per_step, pat, pat_out, places, *refs):
    shards = refs[:n_shards]
    hid_ref, *proj_refs, out_ref, held, proj, sems = refs[n_shards:]
    blk = out_ref.shape[1]

    @pl.when(pl.program_id(0) == 0)
    def _():
        loads = [(ref, held.at[i]) for i, ref in enumerate(shards)]
        for ref in proj_refs:
            part_rows = ref.shape[1]
            for i in range(ref.shape[0]):
                place = places[len(loads) - n_shards]
                rows = pl.ds(pl.multiple_of(place * part_rows, 8), part_rows)
                loads.append((ref.at[i], proj.at[rows]))
        load_all(loads, sems)
        out_ref[...] = jnp.zeros_like(out_ref)

    first = pl.program_id(0) * per_step
    lefts = []
    for u in range(per_step):
        span = slice(u * blk, (u + 1) * blk)
        hid = hid_ref[span, :]
        rows = pl.ds(pl.multiple_of((first + u) * blk, blk), blk)
        ph, pl_ = split2(proj[rows, :].T)
        lefts.append(((dot(ph, hid) + dot(pl_, hid)) * scale).astype(BF))
    parts = []
    for u in range(per_step):
        cols = [pat[(first + u) * SLOTS + j] for j in range(SLOTS)]
        for j in range(0, SLOTS, 2):
            chosen = jnp.concatenate(
                [column_block(held, c, per_shard, blk) for c in cols[j : j + 2]], axis=1
            )
            parts.append(dot(lefts[u], chosen))
    for u in range(per_step):
        outs = [pat_out[(first + u) * SLOTS + j] for j in range(SLOTS)]
        sums = [
            out_ref[c] + parts[(u * SLOTS + j) // 2][:, (j % 2) * blk : (j % 2 + 1) * blk]
            for j, c in enumerate(outs)
        ]
        for c, total in zip(outs, sums):
            out_ref[c] = total


def grad_kernel(n_shards, per_shard, blk, window, n_windows, order, starts, pat, *refs):
    shards = refs[: 2 * n_shards]
    own_ref, got_ref, out_ref, top_ref, held, sems = refs[2 * n_shards :]
    toks = own_ref.shape[1]

    @pl.when(pl.program_id(0) == 0)
    def _():
        load_all(
            [
                (ref, held.at[i % n_shards, pl.ds(i // n_shards * toks, toks)])
                for i, ref in enumerate(shards)
            ],
            sems,
        )
        top_ref[...] = jnp.zeros_like(top_ref)

    top = top_ref[...]
    for w in range(n_windows):
        index = order[pl.program_id(0)] * n_windows + w
        rows = pl.ds(pl.multiple_of(starts[index], window // 2 if window >= 32 else 8), window)
        hid = jnp.concatenate([own_ref[rows, :], got_ref[rows, :]], axis=1).astype(BF)
        for j in range(0, SLOTS, 2):
            chosen = jnp.concatenate(
                [column_block(held, pat[index * SLOTS + j + i], per_shard, blk) for i in (0, 1)],
                axis=1,
            )
            part = dot(hid, chosen)
            out_ref[rows, j * blk : (j + 2) * blk] = part
            size = jnp.abs(part)
            for i in range(0, window, 8):
                top = jnp.maximum(top, size[i : i + 8])
    top_ref[...] = top


def input_grad_kernel(n_shards, per_shard, blk, per_step, pat, *refs):
    shards = refs[:n_shards]
    w_ref, out_ref, held, sems = refs[n_shards:]

    @pl.when(pl.program_id(0) == 0)
    def _():
        load_all([(ref, held.at[i]) for i, ref in enumerate(shards)], sems)

    for u in range(per_step):
        row = pl.program_id(0) * per_step + u
        chosen = jnp.concatenate(
            [column_block(held, pat[row * SLOTS + j], per_shard, blk) for j in range(SLOTS)], axis=1
        )
        span = slice(u * blk, (u + 1) * blk)
        out_ref[:, span] = dot_nt(chosen, w_ref[span, :]).astype(BF)


def sketch_gram_kernel(sh_ref, sl_ref, out_ref):
    out_ref[...] = jnp.zeros_like(out_ref)
    for s in range(sh_ref.shape[0]):
        high, low = sh_ref[s], sl_ref[s]
        out_ref[...] += dot_nt(high, high) + (dot_nt(high, low) + dot_nt(low, high))


def cross_gram_kernel(ch_ref, cl_ref, sh_ref, sl_ref, out_ref):
    rank = ch_ref.shape[1]
    per = ch_ref.shape[0] // sh_ref.shape[0]
    with_sketch = jnp.zeros((rank, rank), F32)
    with_self = jnp.zeros((rank, rank), F32)
    for s in range(sh_ref.shape[0]):
        high = jnp.concatenate([ch_ref[per * s + b] for b in range(per)], axis=1)
        low = jnp.concatenate([cl_ref[per * s + b] for b in range(per)], axis=1)
        sh, sl = sh_ref[s], sl_ref[s]
        with_sketch += dot_nt(high, sh) + (dot_nt(high, sl) + dot_nt(low, sh))
        with_self += dot_nt(high, high) + (dot_nt(high, low) + dot_nt(low, high))
    out_ref[:, :rank] = with_sketch
    out_ref[:, rank:] = with_self


def mixing_kernel(ss_ref, cross_ref, out_ref):
    rank = ss_ref.shape[0]
    size = 2 * rank
    sqrt_eps = math.sqrt(SHIFT_EPS)

    def mm(a, b):
        return jnp.dot(a, b, precision=HIGHEST, preferred_element_type=F32)

    cross = cross_ref[...]
    gram = jnp.concatenate(
        [jnp.concatenate([ss_ref[...], cross[:, :rank].T], axis=1), cross], axis=0
    )
    rows = lax.broadcasted_iota(jnp.int32, (size, size), 0)
    cols = lax.broadcasted_iota(jnp.int32, (size, size), 1)
    identity = jnp.where(rows == cols, 1.0, 0.0).astype(F32)
    shifted = gram + SHIFT_EPS * identity
    frobenius = jnp.sqrt(jnp.sum(shifted * shifted, keepdims=True))
    root = shifted / frobenius
    inverse = identity
    for step in range(NS_STEPS):
        product = root if step == 0 else mm(inverse, root)
        middle = 0.5 * (3.0 * identity - product)
        root = mm(root, middle)
        inverse = middle if step == 0 else mm(middle, inverse)
    sqrt_fro = jnp.sqrt(frobenius)
    half = 0.5 * sqrt_fro * (root + root.T) + sqrt_eps * identity
    guess = inverse / (sqrt_fro + sqrt_eps * 1.5**NS_STEPS)

    def residual(x):
        r = identity - mm(half, x)
        return r, jnp.max(jnp.abs(r))

    def keep_going(state):
        return jnp.logical_and(state[3] < 48, state[2] > 2e-6)

    def improve(state):
        x, r, _, count = state
        x = x + mm(x, r)
        r, size = residual(x)
        return x, r, size, count + 1

    r, top = residual(guess)
    x, r, _, _ = lax.while_loop(keep_going, improve, (guess, r, top, jnp.int32(0)))
    x = x + mm(x, r)
    out_ref[...] = -mm(inverse, x) / (sqrt_eps * sqrt_fro)


def direction_kernel(per, window, n_windows, starts, pat, *refs):
    g_ref, m_ref, skh, skl = refs[:4]
    parts, (out_ref, cph, cpl, sems) = refs[4:-4], refs[-4:]
    blk = cph.shape[2]
    half = len(parts) // 2
    pairs, at = [], 0
    for i in range(half):
        size = parts[i].shape[0]
        pairs += [(parts[i], cph.at[pl.ds(at, size)]), (parts[half + i], cpl.at[pl.ds(at, size)])]
        at += size
    load_all(pairs, sems)

    def gathered(sk, cp, c):
        shard = c // per
        offset = pl.multiple_of((c - shard * per) * blk, blk)
        return jnp.concatenate([sk[shard, :, pl.ds(offset, blk)], cp[c]], axis=0)

    for w in range(n_windows):
        rows = pl.ds(pl.multiple_of(starts[w], window // 2 if window >= 32 else 8), window)
        cols = [pat[w * SLOTS + k] for k in range(SLOTS)]
        g = g_ref[rows, :]
        g_high = g.astype(BF).astype(F32)
        g_both = jnp.concatenate([g_high, g - g_high], axis=0).astype(BF)
        high = [gathered(skh, cph, c) for c in cols]
        low = [gathered(skl, cpl, c) for c in cols]
        both = dot_nt(g_both, jnp.concatenate(high, axis=1))
        projected = both[:window] + both[window:]
        projected += dot_nt(g_high.astype(BF), jnp.concatenate(low, axis=1))
        mixed = jnp.dot(projected, m_ref[...], precision=HIGHEST, preferred_element_type=F32)
        mixed_high = mixed.astype(BF).astype(F32)
        mixed_both = jnp.concatenate([mixed_high, mixed - mixed_high], axis=0).astype(BF)
        for k in range(0, SLOTS, 2):
            both = dot(mixed_both, jnp.concatenate(high[k : k + 2], axis=1))
            corr = both[:window] + both[window:]
            corr += dot(mixed_high.astype(BF), jnp.concatenate(low[k : k + 2], axis=1))
            corr += g[:, k * blk : (k + 2) * blk] * (1.0 / math.sqrt(SHIFT_EPS))
            out_ref[rows, k, :] = corr[:, :blk]
            out_ref[rows, k + 1, :] = corr[:, blk:]


def windows_of(start, dev_rows, blk):
    group = math.gcd(dev_rows, blk)
    if dev_rows % blk == blk // 2 and dev_rows > blk:
        whole = dev_rows // blk
        odd = (start // group) % 2
        later = odd * group + blk * jnp.arange(whole, dtype=jnp.int32)
        first = jnp.where(odd == 1, 0, dev_rows - blk)
        first_row = jnp.where(odd == 1, start, start + dev_rows - group)
        starts = jnp.concatenate([first[None], later])
        inside = jnp.concatenate([first_row[None], start + later])
        return blk, starts.astype(jnp.int32), (inside // blk).astype(jnp.int32)
    starts = group * jnp.arange(dev_rows // group, dtype=jnp.int32)
    return group, starts, (start + starts) // blk


def per_device(weights, hidden, cotangent, sketch, projection, pattern):
    tok_rows = hidden.shape[0]
    mp_rows, slots, blk = weights.shape
    block_rows = mp_rows // blk
    n_dp, n_mp = lax.axis_size("dp"), lax.axis_size("mp")
    dev_rows = mp_rows // n_dp
    all_tokens = tok_rows * n_dp
    rank = sketch.shape[0]
    shard_cols = cotangent.shape[1]
    per_shard = shard_cols // blk
    col_blocks = per_shard * n_mp
    outer = n_dp // 2
    per_step = 4 if block_rows % 4 == 0 else 1
    dp, mp = lax.axis_index("dp"), lax.axis_index("mp")
    side = dp % 2

    def swap(x, axis, bit):
        size = lax.axis_size(axis)
        return lax.ppermute(x, axis, [(i, i ^ bit) for i in range(size)])

    def after(x, *others):
        return lax.optimization_barrier((x, *others))[0]

    def over_dp(x):
        return lax.all_to_all(jnp.broadcast_to(x[None], (n_dp, *x.shape)), "dp", 0, 0)

    width = sketch.shape[1]
    core_half = swap(cotangent, "mp", 1)
    proj_t = (projection.reshape(rank, dev_rows).T * PROJ_SCALE).astype(F16)
    if width < blk:
        sk_rows = sketch.reshape(width, rank)
    else:
        sk_rows = sketch.reshape(rank, width // blk, blk).swapaxes(0, 1).reshape(-1, blk)
    early = jnp.concatenate([proj_t, sk_rows.astype(F16)], axis=0)
    early, order = early[None], jnp.zeros((1,), jnp.int32)
    bits = [1 << i for i in range(1, n_dp.bit_length() - 1)]
    if n_dp > 8:
        early, order, bits = over_dp(early[0]), jnp.arange(n_dp, dtype=jnp.int32), []
    hidden_in, weights_in = hidden, weights
    for bit in bits:
        early = jnp.concatenate([early, swap(early, "dp", bit)], axis=0)
        order = jnp.concatenate([order, jnp.bitwise_xor(order, bit)])
        if bit == 2:
            early, hidden_in, weights_in = lax.optimization_barrier((early, hidden, weights))
    hid_t = hidden_in.T
    hid_parts = hid_t.reshape(outer, 2, dev_rows, tok_rows)
    hid_own = lax.dynamic_index_in_dim(hid_parts, side, 1, keepdims=False)
    hid_send = lax.dynamic_index_in_dim(hid_parts, 1 - side, 1, keepdims=False)
    weights_2d = weights_in.reshape(mp_rows, slots * blk)
    if n_dp <= 8:
        early, hid_own, hid_send, weights_2d = lax.optimization_barrier(
            (early, hid_own, hid_send, weights_2d)
        )
        early = [early, swap(early, "dp", 1)]
        order = jnp.concatenate([order, jnp.bitwise_xor(order, 1)])
        places = jnp.bitwise_xor(order, dp)
        sk_own = jnp.concatenate([part[:, dev_rows:] for part in early], axis=0)
        far = jnp.bitwise_xor(jnp.arange(n_dp, dtype=jnp.int32), dp)
        at = jnp.where(jnp.bitwise_and(far, 1) == 1, n_dp // 2, 0) + far // 2
        sk_own = jnp.take(sk_own, at, axis=0, mode="clip")
        proj_parts = [part[:, :dev_rows].astype(F32) for part in early]
        hid_send = after(hid_send, early[1])
    else:
        sk_own = early[:, dev_rows:]
        proj_parts = [early[:, :dev_rows].reshape(1, mp_rows, rank).astype(F32)]
        places = jnp.zeros((1,), jnp.int32)
    if width < blk:
        sk_own = sk_own.reshape(n_dp, rank, width)
    else:
        sk_own = sk_own.reshape(per_shard, rank, blk)
    x_part, y_part = swap(cotangent, "mp", 2), swap(cotangent, "dp", 1)
    x_half, y_own, core_half, hid_t, hid_own, weights_2d = (
        lax.optimization_barrier(
            (
                x_part,
                y_part,
                core_half,
                hid_t,
                hid_own,
                weights_2d,
            )
        )
    )
    own = [cotangent, core_half, x_half, swap(x_half, "mp", 1)]
    y_x = swap(y_own, "mp", 2)
    y_core = swap(y_own, "mp", 1)
    hid_got = swap(hid_send, "dp", 1)
    pattern_rel = jnp.bitwise_xor(pattern, mp * per_shard)

    def place(block):
        if width < blk:
            return jnp.bitwise_xor(block, mp * per_shard)
        per = width // blk
        shard, rest = block // per, block % per
        near_mp = jnp.bitwise_xor(shard % n_mp, mp)
        return (near_mp * n_dp + shard // n_mp) * per + rest

    pat_all = pattern_rel.reshape(-1)
    partial_c = pl.pallas_call(
        functools.partial(
            compress_kernel,
            n_mp,
            per_shard,
            1.0 / (PROJ_SCALE * all_tokens),
            per_step,
        ),
        grid_spec=pltpu.PrefetchScalarGridSpec(
            num_scalar_prefetch=3,
            grid=(block_rows // per_step,),
            in_specs=[ANY] * n_mp
            + [pl.BlockSpec((per_step * blk, tok_rows), lambda i, a, b, c: (i, 0))]
            + [ANY] * len(proj_parts),
            out_specs=pl.BlockSpec((col_blocks, rank, blk), lambda i, a, b, c: (0, 0, 0)),
            scratch_shapes=[
                pltpu.VMEM((n_mp, tok_rows, shard_cols), BF),
                pltpu.VMEM((mp_rows, rank), F32),
                pltpu.SemaphoreType.DMA((n_mp + len(places),)),
            ],
        ),
        out_shape=jax.ShapeDtypeStruct((col_blocks, rank, blk), F32),
        compiler_params=params(),
        cost_estimate=SMALL,
        name="compress",
    )(pat_all, place(pattern).reshape(-1), places, *own, hid_t, *proj_parts)

    partial_c, y_x, y_core, hid_got = lax.optimization_barrier((partial_c, y_x, y_core, hid_got))
    y_group = [y_own, y_core, y_x, swap(y_x, "mp", 1)]
    quarters = partial_c.reshape(n_mp, per_shard, rank, blk)
    to_far, to_near = quarters[3].astype(F16), quarters[1].astype(F16)
    got_far, got_near = swap(to_far, "mp", 1), swap(to_near, "mp", 1)
    y_group[3] = after(y_group[3], to_far, to_near)

    half_rows = outer * dev_rows
    devices = 2 * jnp.arange(outer, dtype=jnp.int32) + side
    window, _, _ = windows_of(dp * dev_rows, dev_rows, blk)
    window_starts, window_blocks = jax.vmap(lambda d: windows_of(d * dev_rows, dev_rows, blk)[1:])(
        devices
    )
    n_windows = window_starts.shape[1]
    pat_half = jnp.take(pattern_rel, window_blocks.reshape(-1), axis=0).reshape(-1)
    hid_type = BF if window % 32 == 0 else F32

    def pair_grad(blocks, shards):
        order = jnp.bitwise_xor(jnp.asarray(blocks, jnp.int32), dp // 2)
        out, top = pl.pallas_call(
            functools.partial(grad_kernel, n_mp, per_shard, blk, window, n_windows),
            grid_spec=pltpu.PrefetchScalarGridSpec(
                num_scalar_prefetch=3,
                grid=(len(blocks),),
                in_specs=[ANY] * (2 * n_mp)
                + [pl.BlockSpec((dev_rows, tok_rows), lambda i, o, a, b: (o[i], 0))] * 2,
                out_specs=[
                    pl.BlockSpec((dev_rows, slots * blk), lambda i, o, a, b: (i, 0)),
                    pl.BlockSpec((8, 2 * blk), lambda i, o, a, b: (0, 0)),
                ],
                scratch_shapes=[
                    pltpu.VMEM((n_mp, 2 * tok_rows, shard_cols), BF),
                    pltpu.SemaphoreType.DMA((2 * n_mp,)),
                ],
            ),
            out_shape=[
                jax.ShapeDtypeStruct((len(blocks) * dev_rows, slots * blk), F32),
                jax.ShapeDtypeStruct((8, 2 * blk), F32),
            ],
            compiler_params=params(),
            cost_estimate=SMALL,
            name="pair_grad",
        )(
            order,
            window_starts.reshape(-1),
            pat_half,
            *shards,
            hid_own.reshape(half_rows, tok_rows).astype(hid_type),
            hid_got.reshape(half_rows, tok_rows).astype(hid_type),
        )
        out = out.reshape(len(blocks), dev_rows, slots * blk)
        top = jnp.max(top)
        return {block: (out[i], top) for i, block in enumerate(blocks)}

    def pack(part):
        value, top = part
        exponent = 13.0 - jnp.floor(jnp.log2(jnp.maximum(top, 1e-30)))
        below = jnp.broadcast_to(exponent, (16, value.shape[1]))
        return jnp.concatenate([value * jnp.exp2(exponent), below], axis=0).astype(F16)

    def unpack(message, first=0):
        below = lax.dynamic_slice(message, (dev_rows + first, 0), (8, message.shape[1]))
        exponent = below[:1].astype(F32)
        value = message[:dev_rows].astype(F32) * jnp.exp2(-exponent)
        return value, jnp.exp2(14.0 - jnp.max(exponent))

    def add(part, message, first=0):
        value, top = unpack(message, first)
        return part[0] + value, part[1] + top

    crossing = [i for i in range(outer) if i & 2][::-1]
    staying = [i for i in range(outer) if not i & 2][::-1]
    sums = pair_grad(crossing, own + y_group)
    sent = {i: pack(sums[i]) for i in crossing if i & 1}
    got_far, got_near, *before = lax.optimization_barrier((got_far, got_near, *sent.values()))
    sent = dict(zip(sent, before))
    got = {i: swap(sent[i], "dp", 2) for i in sent}
    far_half = (quarters[2] + got_far.astype(F32)).astype(F16)
    near_half = quarters[0] + got_near.astype(F32)
    far_half, near_half, y_group[3] = lax.optimization_barrier((far_half, near_half, y_group[3]))
    far_sum = swap(far_half, "mp", 2)
    sums.update(pair_grad(staying, own + y_group))
    sent = {i: pack(sums[i]) for i in staying if i & 1}
    got.update({i: swap(sent[i], "dp", 2) for i in staying if i & 1})
    far_sum, near_half, _ = lax.optimization_barrier((far_sum, near_half, list(sent.values())))

    quarter = near_half + far_sum.astype(F32)
    pieces = quarter.astype(F16).reshape(n_dp, per_shard * rank // n_dp, blk)
    if outer == 4:
        pieces, got[3] = lax.optimization_barrier((pieces, got[3]))
    pieces = lax.all_to_all(pieces, "dp", 0, 0)

    last = [got.pop(1)]
    level = 1
    while level < outer:
        if level > 1:
            got = {i: swap(pack(sums[i]), "dp", 2 * level) for i in sums if i & level}
        for i in got:
            sums[i ^ level] = add(sums[i ^ level], got[i])
        sums = {i: part for i, part in sums.items() if not i & level}
        if outer == 4:
            crossed, pieces = lax.optimization_barrier((pack(sums[2]), pieces))
            last.append(swap(crossed, "dp", 4))
            break
        level *= 2


    piece = jnp.sum(pieces.astype(F32), axis=0).astype(F16)
    quarter16 = over_dp(piece).reshape(per_shard, rank, blk)

    sk_own = after(sk_own, quarter)
    sk_far = swap(sk_own, "mp", 2)
    sk_parts = [sk_own, swap(sk_own, "mp", 1), sk_far, swap(sk_far, "mp", 1)]
    if width < blk:
        sk_abs = jnp.take(
            jnp.stack(sk_parts), jnp.bitwise_xor(jnp.arange(n_mp, dtype=jnp.int32), mp), axis=0
        )
        sk_abs = sk_abs.reshape(n_mp, col_blocks, blk // width // n_mp, rank, width)
        sk_abs = sk_abs.transpose(1, 3, 2, 0, 4).reshape(n_mp, per_shard, rank, blk)
        sk_parts = [
            lax.dynamic_index_in_dim(sk_abs, jnp.bitwise_xor(mp, i), 0, keepdims=False)
            for i in range(n_mp)
        ]
    oh, ol = split2_xla(sk_parts[0].astype(F32))
    sk_high, sk_low = split2_xla(jnp.concatenate(sk_parts, axis=0).astype(F32))

    sk_per = sk_high.shape[2] // blk
    sketch_gram = pl.pallas_call(
        sketch_gram_kernel,
        in_specs=[VMEM] * 2,
        out_specs=VMEM,
        out_shape=jax.ShapeDtypeStruct((rank, rank), F32),
        compiler_params=params(),
        cost_estimate=SMALL,
        name="sketch_gram",
    )(sk_high, sk_low)
    quarter16, sketch_gram, sk_high, sk_low, oh, ol = lax.optimization_barrier(
        (quarter16, sketch_gram, sk_high, sk_low, oh, ol)
    )
    qh, ql = split2_xla(quarter16.astype(F32))
    cross = pl.pallas_call(
        cross_gram_kernel,
        in_specs=[VMEM] * 4,
        out_specs=VMEM,
        out_shape=jax.ShapeDtypeStruct((rank, 2 * rank), F32),
        compiler_params=params(),
        cost_estimate=SMALL,
        name="cross_gram",
    )(qh, ql, oh, ol)
    cross = cross + swap(cross, "mp", 2)
    cross = cross + swap(cross, "mp", 1)
    input_grad = pl.pallas_call(
        functools.partial(input_grad_kernel, n_mp, per_shard, blk, per_step),
        grid_spec=pltpu.PrefetchScalarGridSpec(
            num_scalar_prefetch=1,
            grid=(block_rows // per_step,),
            in_specs=[ANY] * n_mp
            + [pl.BlockSpec((per_step * blk, slots * blk), lambda i, pat: (i, 0))],
            out_specs=pl.BlockSpec((tok_rows, per_step * blk), lambda i, pat: (0, i)),
            scratch_shapes=[
                pltpu.VMEM((n_mp, tok_rows, shard_cols), BF),
                pltpu.SemaphoreType.DMA((n_mp,)),
            ],
        ),
        out_shape=jax.ShapeDtypeStruct((tok_rows, mp_rows), BF),
        compiler_params=params(),
        cost_estimate=SMALL,
        name="input_grad",
    )(pat_all, *own, after(weights_2d, cross))
    cross, input_grad = lax.optimization_barrier((cross, input_grad))
    mixing = pl.pallas_call(
        mixing_kernel,
        in_specs=[VMEM] * 2,
        out_specs=VMEM,
        out_shape=jax.ShapeDtypeStruct((2 * rank, 2 * rank), F32),
        compiler_params=params(),
        cost_estimate=SMALL,
        name="mixing",
    )(sketch_gram, cross)

    quarter16 = after(quarter16, cross)
    far = swap(quarter16, "mp", 2)
    comp_parts = [quarter16, swap(quarter16, "mp", 1), far, swap(far, "mp", 1)]
    comp_parts = [split2_xla(part.astype(F32)) for part in comp_parts]
    comp_parts = [part[0] for part in comp_parts] + [part[1] for part in comp_parts]

    kept, mixing, first = lax.optimization_barrier((sums[0], mixing, jnp.int32(0)))
    for message in last:
        kept = add(kept, message, first)
    grad = kept[0] * (1.0 / all_tokens)
    _, my_starts, my_blocks = windows_of(dp * dev_rows, dev_rows, blk)
    my_pat = jnp.take(place(pattern), my_blocks, axis=0).reshape(-1)
    smem = pl.BlockSpec(memory_space=pltpu.SMEM)
    direction = pl.pallas_call(
        functools.partial(direction_kernel, sk_per, window, n_windows),
        in_specs=[smem] * 2 + [VMEM] * 4 + [ANY] * len(comp_parts),
        out_specs=VMEM,
        out_shape=jax.ShapeDtypeStruct((dev_rows, slots, blk), F32),
        scratch_shapes=[
            pltpu.VMEM((col_blocks, rank, blk), BF),
            pltpu.VMEM((col_blocks, rank, blk), BF),
            pltpu.SemaphoreType.DMA((len(comp_parts),)),
        ],
        compiler_params=params(),
        cost_estimate=SMALL,
        name="direction",
    )(my_starts, my_pat, grad, mixing, sk_high, sk_low, *comp_parts)
    return (input_grad, direction.reshape(1, dev_rows, slots, blk))


def solution(mesh):
    return jax.shard_map(
        per_device,
        mesh=mesh,
        in_specs=(
            P("mp", None, None),
            P("dp", "mp"),
            P("dp", "mp"),
            P(None, ("dp", "mp")),
            P(None, "mp", "dp"),
            P("mp", None),
        ),
        out_specs=(P("dp", "mp"), P("mp", "dp", None, None)),
        check_vma=False,
    )
```

```python
import functools
import math

import jax
import jax.numpy as jnp
from jax import lax
from jax.experimental import pallas as pl
from jax.experimental.pallas import tpu as pltpu
from jax.sharding import PartitionSpec as P

NS_STEPS = 5
SHIFT_EPS = 0.0001
PROJ_SCALE = 1024.0
SLOTS = 8

BF = jnp.bfloat16
F16 = jnp.float16
F32 = jnp.float32
HIGHEST = lax.Precision.HIGHEST
VMEM = pl.BlockSpec(memory_space=pltpu.VMEM)
ANY = pl.BlockSpec(memory_space=pl.ANY)


SMALL = pl.CostEstimate(flops=1, bytes_accessed=1, transcendentals=0)


def params(mib=48):
    return pltpu.CompilerParams(vmem_limit_bytes=mib * 1024 * 1024)


def dot(a, b):
    return jnp.dot(a, b, preferred_element_type=F32)


def dot_nt(a, b):
    return lax.dot_general(a, b, (((1,), (1,)), ((), ())), preferred_element_type=F32)


def split2(value):
    high = value.astype(BF)
    return high, (value - high.astype(F32)).astype(BF)


def split2_xla(value):
    high = lax.reduce_precision(value, exponent_bits=8, mantissa_bits=7)
    return high.astype(BF), (value - high).astype(BF)


def load_all(pairs, sems):
    copies = [pltpu.make_async_copy(src, dst, sems.at[i]) for i, (src, dst) in enumerate(pairs)]
    for copy in copies:
        copy.start()
    for copy in copies:
        copy.wait()


def column_block(held, block, per_shard, size):
    shard = block // per_shard
    offset = pl.multiple_of((block - shard * per_shard) * size, size)
    return held[shard, :, pl.ds(offset, size)]


def compress_kernel(n_shards, per_shard, scale, per_step, pat, pat_out, places, *refs):
    shards = refs[:n_shards]
    hid_ref, *proj_refs, out_ref, held, proj, sems = refs[n_shards:]
    blk = out_ref.shape[1]

    @pl.when(pl.program_id(0) == 0)
    def _():
        loads = [(ref, held.at[i]) for i, ref in enumerate(shards)]
        for ref in proj_refs:
            part_rows = ref.shape[1]
            for i in range(ref.shape[0]):
                place = places[len(loads) - n_shards]
                rows = pl.ds(pl.multiple_of(place * part_rows, 8), part_rows)
                loads.append((ref.at[i], proj.at[rows]))
        load_all(loads, sems)
        out_ref[...] = jnp.zeros_like(out_ref)

    first = pl.program_id(0) * per_step
    lefts = []
    for u in range(per_step):
        span = slice(u * blk, (u + 1) * blk)
        hid = hid_ref[span, :]
        rows = pl.ds(pl.multiple_of((first + u) * blk, blk), blk)
        ph, pl_ = split2(proj[rows, :].T)
        lefts.append(((dot(ph, hid) + dot(pl_, hid)) * scale).astype(BF))
    parts = []
    for u in range(per_step):
        cols = [pat[(first + u) * SLOTS + j] for j in range(SLOTS)]
        for j in range(0, SLOTS, 2):
            chosen = jnp.concatenate(
                [column_block(held, c, per_shard, blk) for c in cols[j : j + 2]], axis=1
            )
            parts.append(dot(lefts[u], chosen))
    for u in range(per_step):
        outs = [pat_out[(first + u) * SLOTS + j] for j in range(SLOTS)]
        sums = [
            out_ref[c] + parts[(u * SLOTS + j) // 2][:, (j % 2) * blk : (j % 2 + 1) * blk]
            for j, c in enumerate(outs)
        ]
        for c, total in zip(outs, sums):
            out_ref[c] = total


def grad_kernel(n_shards, per_shard, blk, window, n_windows, order, starts, pat, *refs):
    shards = refs[: 2 * n_shards]
    own_ref, got_ref, out_ref, top_ref, held, sems = refs[2 * n_shards :]
    toks = own_ref.shape[1]

    @pl.when(pl.program_id(0) == 0)
    def _():
        load_all(
            [
                (ref, held.at[i % n_shards, pl.ds(i // n_shards * toks, toks)])
                for i, ref in enumerate(shards)
            ],
            sems,
        )
        top_ref[...] = jnp.zeros_like(top_ref)

    top = top_ref[...]
    for w in range(n_windows):
        index = order[pl.program_id(0)] * n_windows + w
        rows = pl.ds(pl.multiple_of(starts[index], window // 2 if window >= 32 else 8), window)
        hid = jnp.concatenate([own_ref[rows, :], got_ref[rows, :]], axis=1).astype(BF)
        for j in range(0, SLOTS, 2):
            chosen = jnp.concatenate(
                [column_block(held, pat[index * SLOTS + j + i], per_shard, blk) for i in (0, 1)],
                axis=1,
            )
            part = dot(hid, chosen)
            out_ref[rows, j * blk : (j + 2) * blk] = part
            size = jnp.abs(part)
            for i in range(0, window, 8):
                top = jnp.maximum(top, size[i : i + 8])
    top_ref[...] = top


def input_grad_kernel(n_shards, per_shard, blk, per_step, pat, *refs):
    shards = refs[:n_shards]
    w_ref, out_ref, held, sems = refs[n_shards:]

    @pl.when(pl.program_id(0) == 0)
    def _():
        load_all([(ref, held.at[i]) for i, ref in enumerate(shards)], sems)

    for u in range(per_step):
        row = pl.program_id(0) * per_step + u
        chosen = jnp.concatenate(
            [column_block(held, pat[row * SLOTS + j], per_shard, blk) for j in range(SLOTS)], axis=1
        )
        span = slice(u * blk, (u + 1) * blk)
        out_ref[:, span] = dot_nt(chosen, w_ref[span, :]).astype(BF)


def sketch_gram_kernel(sh_ref, sl_ref, out_ref):
    out_ref[...] = jnp.zeros_like(out_ref)
    for s in range(sh_ref.shape[0]):
        high, low = sh_ref[s], sl_ref[s]
        out_ref[...] += dot_nt(high, high) + (dot_nt(high, low) + dot_nt(low, high))


def cross_gram_kernel(ch_ref, cl_ref, sh_ref, sl_ref, out_ref):
    rank = ch_ref.shape[1]
    per = ch_ref.shape[0] // sh_ref.shape[0]
    with_sketch = jnp.zeros((rank, rank), F32)
    with_self = jnp.zeros((rank, rank), F32)
    for s in range(sh_ref.shape[0]):
        high = jnp.concatenate([ch_ref[per * s + b] for b in range(per)], axis=1)
        low = jnp.concatenate([cl_ref[per * s + b] for b in range(per)], axis=1)
        sh, sl = sh_ref[s], sl_ref[s]
        with_sketch += dot_nt(high, sh) + (dot_nt(high, sl) + dot_nt(low, sh))
        with_self += dot_nt(high, high) + (dot_nt(high, low) + dot_nt(low, high))
    out_ref[:, :rank] = with_sketch
    out_ref[:, rank:] = with_self


def mixing_kernel(ss_ref, cross_ref, out_ref):
    rank = ss_ref.shape[0]
    size = 2 * rank
    sqrt_eps = math.sqrt(SHIFT_EPS)

    def mm(a, b):
        return jnp.dot(a, b, precision=HIGHEST, preferred_element_type=F32)

    cross = cross_ref[...]
    gram = jnp.concatenate(
        [jnp.concatenate([ss_ref[...], cross[:, :rank].T], axis=1), cross], axis=0
    )
    rows = lax.broadcasted_iota(jnp.int32, (size, size), 0)
    cols = lax.broadcasted_iota(jnp.int32, (size, size), 1)
    identity = jnp.where(rows == cols, 1.0, 0.0).astype(F32)
    shifted = gram + SHIFT_EPS * identity
    frobenius = jnp.sqrt(jnp.sum(shifted * shifted, keepdims=True))
    root = shifted / frobenius
    inverse = identity
    for step in range(NS_STEPS):
        product = root if step == 0 else mm(inverse, root)
        middle = 0.5 * (3.0 * identity - product)
        root = mm(root, middle)
        inverse = middle if step == 0 else mm(middle, inverse)
    sqrt_fro = jnp.sqrt(frobenius)
    half = 0.5 * sqrt_fro * (root + root.T) + sqrt_eps * identity
    guess = inverse / (sqrt_fro + sqrt_eps * 1.5**NS_STEPS)

    def residual(x):
        r = identity - mm(half, x)
        return r, jnp.max(jnp.abs(r))

    def keep_going(state):
        return jnp.logical_and(state[3] < 48, state[2] > 2e-6)

    def improve(state):
        x, r, _, count = state
        x = x + mm(x, r)
        r, size = residual(x)
        return x, r, size, count + 1

    r, top = residual(guess)
    x, r, _, _ = lax.while_loop(keep_going, improve, (guess, r, top, jnp.int32(0)))
    x = x + mm(x, r)
    out_ref[...] = -mm(inverse, x) / (sqrt_eps * sqrt_fro)


def direction_kernel(per, window, n_windows, starts, pat, *refs):
    g_ref, m_ref, skh, skl = refs[:4]
    parts, (out_ref, cph, cpl, sems) = refs[4:-4], refs[-4:]
    blk = cph.shape[2]
    half = len(parts) // 2
    pairs, at = [], 0
    for i in range(half):
        size = parts[i].shape[0]
        pairs += [(parts[i], cph.at[pl.ds(at, size)]), (parts[half + i], cpl.at[pl.ds(at, size)])]
        at += size
    load_all(pairs, sems)

    def gathered(sk, cp, c):
        shard = c // per
        offset = pl.multiple_of((c - shard * per) * blk, blk)
        return jnp.concatenate([sk[shard, :, pl.ds(offset, blk)], cp[c]], axis=0)

    for w in range(n_windows):
        rows = pl.ds(pl.multiple_of(starts[w], window // 2 if window >= 32 else 8), window)
        cols = [pat[w * SLOTS + k] for k in range(SLOTS)]
        g = g_ref[rows, :]
        g_high = g.astype(BF).astype(F32)
        g_both = jnp.concatenate([g_high, g - g_high], axis=0).astype(BF)
        high = [gathered(skh, cph, c) for c in cols]
        low = [gathered(skl, cpl, c) for c in cols]
        both = dot_nt(g_both, jnp.concatenate(high, axis=1))
        projected = both[:window] + both[window:]
        projected += dot_nt(g_high.astype(BF), jnp.concatenate(low, axis=1))
        mixed = jnp.dot(projected, m_ref[...], precision=HIGHEST, preferred_element_type=F32)
        mixed_high = mixed.astype(BF).astype(F32)
        mixed_both = jnp.concatenate([mixed_high, mixed - mixed_high], axis=0).astype(BF)
        for k in range(0, SLOTS, 2):
            both = dot(mixed_both, jnp.concatenate(high[k : k + 2], axis=1))
            corr = both[:window] + both[window:]
            corr += dot(mixed_high.astype(BF), jnp.concatenate(low[k : k + 2], axis=1))
            corr += g[:, k * blk : (k + 2) * blk] * (1.0 / math.sqrt(SHIFT_EPS))
            out_ref[rows, k, :] = corr[:, :blk]
            out_ref[rows, k + 1, :] = corr[:, blk:]


def windows_of(start, dev_rows, blk):
    group = math.gcd(dev_rows, blk)
    if dev_rows % blk == blk // 2 and dev_rows > blk:
        whole = dev_rows // blk
        odd = (start // group) % 2
        later = odd * group + blk * jnp.arange(whole, dtype=jnp.int32)
        first = jnp.where(odd == 1, 0, dev_rows - blk)
        first_row = jnp.where(odd == 1, start, start + dev_rows - group)
        starts = jnp.concatenate([first[None], later])
        inside = jnp.concatenate([first_row[None], start + later])
        return blk, starts.astype(jnp.int32), (inside // blk).astype(jnp.int32)
    starts = group * jnp.arange(dev_rows // group, dtype=jnp.int32)
    return group, starts, (start + starts) // blk


def per_device(weights, hidden, cotangent, sketch, projection, pattern):
    tok_rows = hidden.shape[0]
    mp_rows, slots, blk = weights.shape
    block_rows = mp_rows // blk
    n_dp, n_mp = lax.axis_size("dp"), lax.axis_size("mp")
    dev_rows = mp_rows // n_dp
    all_tokens = tok_rows * n_dp
    rank = sketch.shape[0]
    shard_cols = cotangent.shape[1]
    per_shard = shard_cols // blk
    col_blocks = per_shard * n_mp
    outer = n_dp // 2
    per_step = 4 if block_rows % 4 == 0 else 1
    dp, mp = lax.axis_index("dp"), lax.axis_index("mp")
    side = dp % 2

    def swap(x, axis, bit):
        size = lax.axis_size(axis)
        return lax.ppermute(x, axis, [(i, i ^ bit) for i in range(size)])

    def after(x, *others):
        return lax.optimization_barrier((x, *others))[0]

    def over_dp(x):
        return lax.all_to_all(jnp.broadcast_to(x[None], (n_dp, *x.shape)), "dp", 0, 0)

    width = sketch.shape[1]
    core_half = swap(cotangent, "mp", 1)
    proj_t = (projection.reshape(rank, dev_rows).T * PROJ_SCALE).astype(F16)
    if width < blk:
        sk_rows = sketch.reshape(width, rank)
    else:
        sk_rows = sketch.reshape(rank, width // blk, blk).swapaxes(0, 1).reshape(-1, blk)
    early = jnp.concatenate([proj_t, sk_rows.astype(F16)], axis=0)
    early, order = early[None], jnp.zeros((1,), jnp.int32)
    bits = [1 << i for i in range(1, n_dp.bit_length() - 1)]
    if n_dp > 8:
        early, order, bits = over_dp(early[0]), jnp.arange(n_dp, dtype=jnp.int32), []
    hidden_in, weights_in = hidden, weights
    x_part, y_part = swap(cotangent, "mp", 2), swap(cotangent, "dp", 1)
    for bit in bits:
        early = jnp.concatenate([early, swap(early, "dp", bit)], axis=0)
        order = jnp.concatenate([order, jnp.bitwise_xor(order, bit)])
        if bit == 2:
            early, hidden_in, weights_in = lax.optimization_barrier((early, hidden, weights))
    hid_t = hidden_in.T
    hid_parts = hid_t.reshape(outer, 2, dev_rows, tok_rows)
    hid_own = lax.dynamic_index_in_dim(hid_parts, side, 1, keepdims=False)
    hid_send = lax.dynamic_index_in_dim(hid_parts, 1 - side, 1, keepdims=False)
    weights_2d = weights_in.reshape(mp_rows, slots * blk)
    if n_dp <= 8:
        early, hid_own, hid_send, weights_2d, x_part, y_part = lax.optimization_barrier(
            (early, hid_own, hid_send, weights_2d, x_part, y_part)
        )
        early = [early, swap(early, "dp", 1)]
        order = jnp.concatenate([order, jnp.bitwise_xor(order, 1)])
        places = jnp.bitwise_xor(order, dp)
        sk_own = jnp.concatenate([part[:, dev_rows:] for part in early], axis=0)
        far = jnp.bitwise_xor(jnp.arange(n_dp, dtype=jnp.int32), dp)
        at = jnp.where(jnp.bitwise_and(far, 1) == 1, n_dp // 2, 0) + far // 2
        sk_own = jnp.take(sk_own, at, axis=0, mode="clip")
        proj_parts = [part[:, :dev_rows].astype(F32) for part in early]
        hid_send = after(hid_send, early[1])
    else:
        sk_own = early[:, dev_rows:]
        proj_parts = [early[:, :dev_rows].reshape(1, mp_rows, rank).astype(F32)]
        places = jnp.zeros((1,), jnp.int32)
    if width < blk:
        sk_own = sk_own.reshape(n_dp, rank, width)
    else:
        sk_own = sk_own.reshape(per_shard, rank, blk)
    x_half, y_own, core_half, hid_t, hid_own, weights_2d = (
        lax.optimization_barrier(
            (
                x_part,
                y_part,
                core_half,
                hid_t,
                hid_own,
                weights_2d,
            )
        )
    )
    own = [cotangent, core_half, x_half, swap(x_half, "mp", 1)]
    y_x = swap(y_own, "mp", 2)
    y_core = swap(y_own, "mp", 1)
    hid_got = swap(hid_send, "dp", 1)
    pattern_rel = jnp.bitwise_xor(pattern, mp * per_shard)

    def place(block):
        if width < blk:
            return jnp.bitwise_xor(block, mp * per_shard)
        per = width // blk
        shard, rest = block // per, block % per
        near_mp = jnp.bitwise_xor(shard % n_mp, mp)
        return (near_mp * n_dp + shard // n_mp) * per + rest

    pat_all = pattern_rel.reshape(-1)
    partial_c = pl.pallas_call(
        functools.partial(
            compress_kernel,
            n_mp,
            per_shard,
            1.0 / (PROJ_SCALE * all_tokens),
            per_step,
        ),
        grid_spec=pltpu.PrefetchScalarGridSpec(
            num_scalar_prefetch=3,
            grid=(block_rows // per_step,),
            in_specs=[ANY] * n_mp
            + [pl.BlockSpec((per_step * blk, tok_rows), lambda i, a, b, c: (i, 0))]
            + [ANY] * len(proj_parts),
            out_specs=pl.BlockSpec((col_blocks, rank, blk), lambda i, a, b, c: (0, 0, 0)),
            scratch_shapes=[
                pltpu.VMEM((n_mp, tok_rows, shard_cols), BF),
                pltpu.VMEM((mp_rows, rank), F32),
                pltpu.SemaphoreType.DMA((n_mp + len(places),)),
            ],
        ),
        out_shape=jax.ShapeDtypeStruct((col_blocks, rank, blk), F32),
        compiler_params=params(),
        cost_estimate=SMALL,
        name="compress",
    )(pat_all, place(pattern).reshape(-1), places, *own, hid_t, *proj_parts)

    partial_c, y_x, y_core, hid_got = lax.optimization_barrier((partial_c, y_x, y_core, hid_got))
    y_group = [y_own, y_core, y_x, swap(y_x, "mp", 1)]
    quarters = partial_c.reshape(n_mp, per_shard, rank, blk)
    to_far, to_near = quarters[3].astype(F16), quarters[1].astype(F16)
    got_far, got_near = swap(to_far, "mp", 1), swap(to_near, "mp", 1)
    y_group[3] = after(y_group[3], to_far, to_near)

    half_rows = outer * dev_rows
    devices = 2 * jnp.arange(outer, dtype=jnp.int32) + side
    window, _, _ = windows_of(dp * dev_rows, dev_rows, blk)
    window_starts, window_blocks = jax.vmap(lambda d: windows_of(d * dev_rows, dev_rows, blk)[1:])(
        devices
    )
    n_windows = window_starts.shape[1]
    pat_half = jnp.take(pattern_rel, window_blocks.reshape(-1), axis=0).reshape(-1)
    hid_type = BF if window % 32 == 0 else F32

    def pair_grad(blocks, shards):
        order = jnp.bitwise_xor(jnp.asarray(blocks, jnp.int32), dp // 2)
        out, top = pl.pallas_call(
            functools.partial(grad_kernel, n_mp, per_shard, blk, window, n_windows),
            grid_spec=pltpu.PrefetchScalarGridSpec(
                num_scalar_prefetch=3,
                grid=(len(blocks),),
                in_specs=[ANY] * (2 * n_mp)
                + [pl.BlockSpec((dev_rows, tok_rows), lambda i, o, a, b: (o[i], 0))] * 2,
                out_specs=[
                    pl.BlockSpec((dev_rows, slots * blk), lambda i, o, a, b: (i, 0)),
                    pl.BlockSpec((8, 2 * blk), lambda i, o, a, b: (0, 0)),
                ],
                scratch_shapes=[
                    pltpu.VMEM((n_mp, 2 * tok_rows, shard_cols), BF),
                    pltpu.SemaphoreType.DMA((2 * n_mp,)),
                ],
            ),
            out_shape=[
                jax.ShapeDtypeStruct((len(blocks) * dev_rows, slots * blk), F32),
                jax.ShapeDtypeStruct((8, 2 * blk), F32),
            ],
            compiler_params=params(),
            cost_estimate=SMALL,
            name="pair_grad",
        )(
            order,
            window_starts.reshape(-1),
            pat_half,
            *shards,
            hid_own.reshape(half_rows, tok_rows).astype(hid_type),
            hid_got.reshape(half_rows, tok_rows).astype(hid_type),
        )
        out = out.reshape(len(blocks), dev_rows, slots * blk)
        top = jnp.max(top)
        return {block: (out[i], top) for i, block in enumerate(blocks)}

    def pack(part):
        value, top = part
        exponent = 13.0 - jnp.floor(jnp.log2(jnp.maximum(top, 1e-30)))
        below = jnp.broadcast_to(exponent, (16, value.shape[1]))
        return jnp.concatenate([value * jnp.exp2(exponent), below], axis=0).astype(F16)

    def unpack(message, first=0):
        below = lax.dynamic_slice(message, (dev_rows + first, 0), (8, message.shape[1]))
        exponent = below[:1].astype(F32)
        value = message[:dev_rows].astype(F32) * jnp.exp2(-exponent)
        return value, jnp.exp2(14.0 - jnp.max(exponent))

    def add(part, message, first=0):
        value, top = unpack(message, first)
        return part[0] + value, part[1] + top

    crossing = [i for i in range(outer) if i & 2][::-1]
    staying = [i for i in range(outer) if not i & 2][::-1]
    sums = pair_grad(crossing, own + y_group)
    sent = {i: pack(sums[i]) for i in crossing if i & 1}
    got_far, got_near, *before = lax.optimization_barrier((got_far, got_near, *sent.values()))
    sent = dict(zip(sent, before))
    got = {i: swap(sent[i], "dp", 2) for i in sent}
    far_half = (quarters[2] + got_far.astype(F32)).astype(F16)
    near_half = quarters[0] + got_near.astype(F32)
    far_half, near_half, y_group[3] = lax.optimization_barrier((far_half, near_half, y_group[3]))
    far_sum = swap(far_half, "mp", 2)
    sums.update(pair_grad(staying, own + y_group))
    sent = {i: pack(sums[i]) for i in staying if i & 1}
    got.update({i: swap(sent[i], "dp", 2) for i in staying if i & 1})
    far_sum, near_half, _ = lax.optimization_barrier((far_sum, near_half, list(sent.values())))

    quarter = near_half + far_sum.astype(F32)
    pieces = quarter.astype(F16).reshape(n_dp, per_shard * rank // n_dp, blk)
    if outer == 4:
        pieces, got[3] = lax.optimization_barrier((pieces, got[3]))
    pieces = lax.all_to_all(pieces, "dp", 0, 0)

    last = [got.pop(1)]
    level = 1
    while level < outer:
        if level > 1:
            got = {i: swap(pack(sums[i]), "dp", 2 * level) for i in sums if i & level}
        for i in got:
            sums[i ^ level] = add(sums[i ^ level], got[i])
        sums = {i: part for i, part in sums.items() if not i & level}
        if outer == 4:
            crossed, pieces = lax.optimization_barrier((pack(sums[2]), pieces))
            last.append(swap(crossed, "dp", 4))
            break
        level *= 2


    piece = jnp.sum(pieces.astype(F32), axis=0).astype(F16)
    quarter16 = over_dp(piece).reshape(per_shard, rank, blk)

    sk_own = after(sk_own, quarter)
    sk_far = swap(sk_own, "mp", 2)
    sk_parts = [sk_own, swap(sk_own, "mp", 1), sk_far, swap(sk_far, "mp", 1)]
    if width < blk:
        sk_abs = jnp.take(
            jnp.stack(sk_parts), jnp.bitwise_xor(jnp.arange(n_mp, dtype=jnp.int32), mp), axis=0
        )
        sk_abs = sk_abs.reshape(n_mp, col_blocks, blk // width // n_mp, rank, width)
        sk_abs = sk_abs.transpose(1, 3, 2, 0, 4).reshape(n_mp, per_shard, rank, blk)
        sk_parts = [
            lax.dynamic_index_in_dim(sk_abs, jnp.bitwise_xor(mp, i), 0, keepdims=False)
            for i in range(n_mp)
        ]
    oh, ol = split2_xla(sk_parts[0].astype(F32))
    sk_high, sk_low = split2_xla(jnp.concatenate(sk_parts, axis=0).astype(F32))

    sk_per = sk_high.shape[2] // blk
    sketch_gram = pl.pallas_call(
        sketch_gram_kernel,
        in_specs=[VMEM] * 2,
        out_specs=VMEM,
        out_shape=jax.ShapeDtypeStruct((rank, rank), F32),
        compiler_params=params(),
        cost_estimate=SMALL,
        name="sketch_gram",
    )(sk_high, sk_low)
    quarter16, sketch_gram, sk_high, sk_low, oh, ol = lax.optimization_barrier(
        (quarter16, sketch_gram, sk_high, sk_low, oh, ol)
    )
    qh, ql = split2_xla(quarter16.astype(F32))
    cross = pl.pallas_call(
        cross_gram_kernel,
        in_specs=[VMEM] * 4,
        out_specs=VMEM,
        out_shape=jax.ShapeDtypeStruct((rank, 2 * rank), F32),
        compiler_params=params(),
        cost_estimate=SMALL,
        name="cross_gram",
    )(qh, ql, oh, ol)
    cross = cross + swap(cross, "mp", 2)
    cross = cross + swap(cross, "mp", 1)
    input_grad = pl.pallas_call(
        functools.partial(input_grad_kernel, n_mp, per_shard, blk, per_step),
        grid_spec=pltpu.PrefetchScalarGridSpec(
            num_scalar_prefetch=1,
            grid=(block_rows // per_step,),
            in_specs=[ANY] * n_mp
            + [pl.BlockSpec((per_step * blk, slots * blk), lambda i, pat: (i, 0))],
            out_specs=pl.BlockSpec((tok_rows, per_step * blk), lambda i, pat: (0, i)),
            scratch_shapes=[
                pltpu.VMEM((n_mp, tok_rows, shard_cols), BF),
                pltpu.SemaphoreType.DMA((n_mp,)),
            ],
        ),
        out_shape=jax.ShapeDtypeStruct((tok_rows, mp_rows), BF),
        compiler_params=params(),
        cost_estimate=SMALL,
        name="input_grad",
    )(pat_all, *own, after(weights_2d, cross))
    cross, input_grad = lax.optimization_barrier((cross, input_grad))
    mixing = pl.pallas_call(
        mixing_kernel,
        in_specs=[VMEM] * 2,
        out_specs=VMEM,
        out_shape=jax.ShapeDtypeStruct((2 * rank, 2 * rank), F32),
        compiler_params=params(),
        cost_estimate=SMALL,
        name="mixing",
    )(sketch_gram, cross)

    quarter16 = after(quarter16, cross)
    far = swap(quarter16, "mp", 2)
    comp_parts = [quarter16, swap(quarter16, "mp", 1), far, swap(far, "mp", 1)]
    comp_parts = [split2_xla(part.astype(F32)) for part in comp_parts]
    comp_parts = [part[0] for part in comp_parts] + [part[1] for part in comp_parts]

    kept, mixing, first = lax.optimization_barrier((sums[0], mixing, jnp.int32(0)))
    for message in last:
        kept = add(kept, message, first)
    grad = kept[0] * (1.0 / all_tokens)
    _, my_starts, my_blocks = windows_of(dp * dev_rows, dev_rows, blk)
    my_pat = jnp.take(place(pattern), my_blocks, axis=0).reshape(-1)
    smem = pl.BlockSpec(memory_space=pltpu.SMEM)
    direction = pl.pallas_call(
        functools.partial(direction_kernel, sk_per, window, n_windows),
        in_specs=[smem] * 2 + [VMEM] * 4 + [ANY] * len(comp_parts),
        out_specs=VMEM,
        out_shape=jax.ShapeDtypeStruct((dev_rows, slots, blk), F32),
        scratch_shapes=[
            pltpu.VMEM((col_blocks, rank, blk), BF),
            pltpu.VMEM((col_blocks, rank, blk), BF),
            pltpu.SemaphoreType.DMA((len(comp_parts),)),
        ],
        compiler_params=params(),
        cost_estimate=SMALL,
        name="direction",
    )(my_starts, my_pat, grad, mixing, sk_high, sk_low, *comp_parts)
    return (input_grad, direction.reshape(1, dev_rows, slots, blk))


def solution(mesh):
    return jax.shard_map(
        per_device,
        mesh=mesh,
        in_specs=(
            P("mp", None, None),
            P("dp", "mp"),
            P("dp", "mp"),
            P(None, ("dp", "mp")),
            P(None, "mp", "dp"),
            P("mp", None),
        ),
        out_specs=(P("dp", "mp"), P("mp", "dp", None, None)),
        check_vma=False,
    )
```

```python
import functools
import math

import jax
import jax.numpy as jnp
from jax import lax
from jax.experimental import pallas as pl
from jax.experimental.pallas import tpu as pltpu
from jax.sharding import PartitionSpec as P

NS_STEPS = 5
SHIFT_EPS = 0.0001
PROJ_SCALE = 1024.0
SLOTS = 8

BF = jnp.bfloat16
F16 = jnp.float16
F32 = jnp.float32
HIGHEST = lax.Precision.HIGHEST
VMEM = pl.BlockSpec(memory_space=pltpu.VMEM)
ANY = pl.BlockSpec(memory_space=pl.ANY)


SMALL = pl.CostEstimate(flops=1, bytes_accessed=1, transcendentals=0)


def params(mib=48):
    return pltpu.CompilerParams(vmem_limit_bytes=mib * 1024 * 1024)


def dot(a, b):
    return jnp.dot(a, b, preferred_element_type=F32)


def dot_nt(a, b):
    return lax.dot_general(a, b, (((1,), (1,)), ((), ())), preferred_element_type=F32)


def split2(value):
    high = value.astype(BF)
    return high, (value - high.astype(F32)).astype(BF)


def split2_xla(value):
    high = lax.reduce_precision(value, exponent_bits=8, mantissa_bits=7)
    return high.astype(BF), (value - high).astype(BF)


def load_all(pairs, sems):
    copies = [pltpu.make_async_copy(src, dst, sems.at[i]) for i, (src, dst) in enumerate(pairs)]
    for copy in copies:
        copy.start()
    for copy in copies:
        copy.wait()


def column_block(held, block, per_shard, size):
    shard = block // per_shard
    offset = pl.multiple_of((block - shard * per_shard) * size, size)
    return held[shard, :, pl.ds(offset, size)]


def compress_kernel(n_shards, per_shard, scale, per_step, pat, pat_out, places, *refs):
    shards = refs[:n_shards]
    hid_ref, *proj_refs, out_ref, held, proj, sems = refs[n_shards:]
    blk = out_ref.shape[1]

    @pl.when(pl.program_id(0) == 0)
    def _():
        loads = [(ref, held.at[i]) for i, ref in enumerate(shards)]
        for ref in proj_refs:
            part_rows = ref.shape[1]
            for i in range(ref.shape[0]):
                place = places[len(loads) - n_shards]
                rows = pl.ds(pl.multiple_of(place * part_rows, 8), part_rows)
                loads.append((ref.at[i], proj.at[rows]))
        load_all(loads, sems)
        out_ref[...] = jnp.zeros_like(out_ref)

    first = pl.program_id(0) * per_step
    lefts = []
    for u in range(per_step):
        span = slice(u * blk, (u + 1) * blk)
        hid = hid_ref[span, :]
        rows = pl.ds(pl.multiple_of((first + u) * blk, blk), blk)
        ph, pl_ = split2(proj[rows, :].T)
        lefts.append(((dot(ph, hid) + dot(pl_, hid)) * scale).astype(BF))
    parts = []
    for u in range(per_step):
        cols = [pat[(first + u) * SLOTS + j] for j in range(SLOTS)]
        for j in range(0, SLOTS, 2):
            chosen = jnp.concatenate(
                [column_block(held, c, per_shard, blk) for c in cols[j : j + 2]], axis=1
            )
            parts.append(dot(lefts[u], chosen))
    for u in range(per_step):
        outs = [pat_out[(first + u) * SLOTS + j] for j in range(SLOTS)]
        sums = [
            out_ref[c] + parts[(u * SLOTS + j) // 2][:, (j % 2) * blk : (j % 2 + 1) * blk]
            for j, c in enumerate(outs)
        ]
        for c, total in zip(outs, sums):
            out_ref[c] = total


def grad_kernel(n_shards, per_shard, blk, window, n_windows, order, starts, pat, *refs):
    shards = refs[: 2 * n_shards]
    own_ref, got_ref, out_ref, top_ref, held, sems = refs[2 * n_shards :]
    toks = own_ref.shape[1]

    @pl.when(pl.program_id(0) == 0)
    def _():
        load_all(
            [
                (ref, held.at[i % n_shards, pl.ds(i // n_shards * toks, toks)])
                for i, ref in enumerate(shards)
            ],
            sems,
        )
        top_ref[...] = jnp.zeros_like(top_ref)

    top = top_ref[...]
    for w in range(n_windows):
        index = order[pl.program_id(0)] * n_windows + w
        rows = pl.ds(pl.multiple_of(starts[index], window // 2 if window >= 32 else 8), window)
        hid = jnp.concatenate([own_ref[rows, :], got_ref[rows, :]], axis=1).astype(BF)
        for j in range(0, SLOTS, 2):
            chosen = jnp.concatenate(
                [column_block(held, pat[index * SLOTS + j + i], per_shard, blk) for i in (0, 1)],
                axis=1,
            )
            part = dot(hid, chosen)
            out_ref[rows, j * blk : (j + 2) * blk] = part
            size = jnp.abs(part)
            for i in range(0, window, 8):
                top = jnp.maximum(top, size[i : i + 8])
    top_ref[...] = top


def input_grad_kernel(n_shards, per_shard, blk, per_step, pat, *refs):
    shards = refs[:n_shards]
    w_ref, out_ref, held, sems = refs[n_shards:]

    @pl.when(pl.program_id(0) == 0)
    def _():
        load_all([(ref, held.at[i]) for i, ref in enumerate(shards)], sems)

    for u in range(per_step):
        row = pl.program_id(0) * per_step + u
        chosen = jnp.concatenate(
            [column_block(held, pat[row * SLOTS + j], per_shard, blk) for j in range(SLOTS)], axis=1
        )
        span = slice(u * blk, (u + 1) * blk)
        out_ref[:, span] = dot_nt(chosen, w_ref[span, :]).astype(BF)


def sketch_gram_kernel(sh_ref, sl_ref, out_ref):
    out_ref[...] = jnp.zeros_like(out_ref)
    for s in range(sh_ref.shape[0]):
        high, low = sh_ref[s], sl_ref[s]
        out_ref[...] += dot_nt(high, high) + (dot_nt(high, low) + dot_nt(low, high))


def cross_gram_kernel(ch_ref, cl_ref, sh_ref, sl_ref, out_ref):
    rank = ch_ref.shape[1]
    per = ch_ref.shape[0] // sh_ref.shape[0]
    with_sketch = jnp.zeros((rank, rank), F32)
    with_self = jnp.zeros((rank, rank), F32)
    for s in range(sh_ref.shape[0]):
        high = jnp.concatenate([ch_ref[per * s + b] for b in range(per)], axis=1)
        low = jnp.concatenate([cl_ref[per * s + b] for b in range(per)], axis=1)
        sh, sl = sh_ref[s], sl_ref[s]
        with_sketch += dot_nt(high, sh) + (dot_nt(high, sl) + dot_nt(low, sh))
        with_self += dot_nt(high, high) + (dot_nt(high, low) + dot_nt(low, high))
    out_ref[:, :rank] = with_sketch
    out_ref[:, rank:] = with_self


def mixing_kernel(ss_ref, cross_ref, out_ref):
    rank = ss_ref.shape[0]
    size = 2 * rank
    sqrt_eps = math.sqrt(SHIFT_EPS)

    def mm(a, b):
        return jnp.dot(a, b, precision=HIGHEST, preferred_element_type=F32)

    cross = cross_ref[...]
    gram = jnp.concatenate(
        [jnp.concatenate([ss_ref[...], cross[:, :rank].T], axis=1), cross], axis=0
    )
    rows = lax.broadcasted_iota(jnp.int32, (size, size), 0)
    cols = lax.broadcasted_iota(jnp.int32, (size, size), 1)
    identity = jnp.where(rows == cols, 1.0, 0.0).astype(F32)
    shifted = gram + SHIFT_EPS * identity
    frobenius = jnp.sqrt(jnp.sum(shifted * shifted, keepdims=True))
    root = shifted / frobenius
    inverse = identity
    for step in range(NS_STEPS):
        product = root if step == 0 else mm(inverse, root)
        middle = 0.5 * (3.0 * identity - product)
        root = mm(root, middle)
        inverse = middle if step == 0 else mm(middle, inverse)
    sqrt_fro = jnp.sqrt(frobenius)
    half = 0.5 * sqrt_fro * (root + root.T) + sqrt_eps * identity
    guess = inverse / (sqrt_fro + sqrt_eps * 1.5**NS_STEPS)

    def residual(x):
        r = identity - mm(half, x)
        return r, jnp.max(jnp.abs(r))

    def keep_going(state):
        return jnp.logical_and(state[3] < 48, state[2] > 2e-6)

    def improve(state):
        x, r, _, count = state
        x = x + mm(x, r)
        r, size = residual(x)
        return x, r, size, count + 1

    r, top = residual(guess)
    x, r, _, _ = lax.while_loop(keep_going, improve, (guess, r, top, jnp.int32(0)))
    x = x + mm(x, r)
    out_ref[...] = -mm(inverse, x) / (sqrt_eps * sqrt_fro)


def direction_kernel(per, window, n_windows, starts, pat, *refs):
    g_ref, m_ref, skh, skl = refs[:4]
    parts, (out_ref, cph, cpl, sems) = refs[4:-4], refs[-4:]
    blk = cph.shape[2]
    half = len(parts) // 2
    pairs, at = [], 0
    for i in range(half):
        size = parts[i].shape[0]
        pairs += [(parts[i], cph.at[pl.ds(at, size)]), (parts[half + i], cpl.at[pl.ds(at, size)])]
        at += size
    load_all(pairs, sems)

    def gathered(sk, cp, c):
        shard = c // per
        offset = pl.multiple_of((c - shard * per) * blk, blk)
        return jnp.concatenate([sk[shard, :, pl.ds(offset, blk)], cp[c]], axis=0)

    for w in range(n_windows):
        rows = pl.ds(pl.multiple_of(starts[w], window // 2 if window >= 32 else 8), window)
        cols = [pat[w * SLOTS + k] for k in range(SLOTS)]
        g = g_ref[rows, :]
        g_high = g.astype(BF).astype(F32)
        g_both = jnp.concatenate([g_high, g - g_high], axis=0).astype(BF)
        high = [gathered(skh, cph, c) for c in cols]
        low = [gathered(skl, cpl, c) for c in cols]
        both = dot_nt(g_both, jnp.concatenate(high, axis=1))
        projected = both[:window] + both[window:]
        projected += dot_nt(g_high.astype(BF), jnp.concatenate(low, axis=1))
        mixed = jnp.dot(projected, m_ref[...], precision=HIGHEST, preferred_element_type=F32)
        mixed_high = mixed.astype(BF).astype(F32)
        mixed_both = jnp.concatenate([mixed_high, mixed - mixed_high], axis=0).astype(BF)
        for k in range(0, SLOTS, 2):
            both = dot(mixed_both, jnp.concatenate(high[k : k + 2], axis=1))
            corr = both[:window] + both[window:]
            corr += dot(mixed_high.astype(BF), jnp.concatenate(low[k : k + 2], axis=1))
            corr += g[:, k * blk : (k + 2) * blk] * (1.0 / math.sqrt(SHIFT_EPS))
            out_ref[rows, k, :] = corr[:, :blk]
            out_ref[rows, k + 1, :] = corr[:, blk:]


def windows_of(start, dev_rows, blk):
    group = math.gcd(dev_rows, blk)
    if dev_rows % blk == blk // 2 and dev_rows > blk:
        whole = dev_rows // blk
        odd = (start // group) % 2
        later = odd * group + blk * jnp.arange(whole, dtype=jnp.int32)
        first = jnp.where(odd == 1, 0, dev_rows - blk)
        first_row = jnp.where(odd == 1, start, start + dev_rows - group)
        starts = jnp.concatenate([first[None], later])
        inside = jnp.concatenate([first_row[None], start + later])
        return blk, starts.astype(jnp.int32), (inside // blk).astype(jnp.int32)
    starts = group * jnp.arange(dev_rows // group, dtype=jnp.int32)
    return group, starts, (start + starts) // blk


def per_device(weights, hidden, cotangent, sketch, projection, pattern):
    tok_rows = hidden.shape[0]
    mp_rows, slots, blk = weights.shape
    block_rows = mp_rows // blk
    n_dp, n_mp = lax.axis_size("dp"), lax.axis_size("mp")
    dev_rows = mp_rows // n_dp
    all_tokens = tok_rows * n_dp
    rank = sketch.shape[0]
    shard_cols = cotangent.shape[1]
    per_shard = shard_cols // blk
    col_blocks = per_shard * n_mp
    outer = n_dp // 2
    per_step = 4 if block_rows % 4 == 0 else 1
    dp, mp = lax.axis_index("dp"), lax.axis_index("mp")
    side = dp % 2

    def swap(x, axis, bit):
        size = lax.axis_size(axis)
        return lax.ppermute(x, axis, [(i, i ^ bit) for i in range(size)])

    def after(x, *others):
        return lax.optimization_barrier((x, *others))[0]

    def over_dp(x):
        return lax.all_to_all(jnp.broadcast_to(x[None], (n_dp, *x.shape)), "dp", 0, 0)

    width = sketch.shape[1]
    core_half = swap(cotangent, "mp", 1)
    proj_t = (projection.reshape(rank, dev_rows).T * PROJ_SCALE).astype(F16)
    if width < blk:
        sk_rows = sketch.reshape(width, rank)
    else:
        sk_rows = sketch.reshape(rank, width // blk, blk).swapaxes(0, 1).reshape(-1, blk)
    early = jnp.concatenate([proj_t, sk_rows.astype(F16)], axis=0)
    early, order = early[None], jnp.zeros((1,), jnp.int32)
    bits = [1 << i for i in range(1, n_dp.bit_length() - 1)]
    if n_dp > 8:
        early, order, bits = over_dp(early[0]), jnp.arange(n_dp, dtype=jnp.int32), []
    hidden_in, weights_in = hidden, weights
    x_part, y_part = swap(cotangent, "mp", 2), swap(cotangent, "dp", 1)
    for bit in bits:
        early = jnp.concatenate([early, swap(early, "dp", bit)], axis=0)
        order = jnp.concatenate([order, jnp.bitwise_xor(order, bit)])
        if bit == 2:
            early, hidden_in, weights_in = lax.optimization_barrier((early, hidden, weights))
    hid_t = hidden_in.T
    hid_parts = hid_t.reshape(outer, 2, dev_rows, tok_rows)
    hid_own = lax.dynamic_index_in_dim(hid_parts, side, 1, keepdims=False)
    hid_send = lax.dynamic_index_in_dim(hid_parts, 1 - side, 1, keepdims=False)
    weights_2d = weights_in.reshape(mp_rows, slots * blk)
    if n_dp <= 8:
        early, hid_own, hid_send, weights_2d, x_part, y_part = lax.optimization_barrier(
            (early, hid_own, hid_send, weights_2d, x_part, y_part)
        )
        proj_near, sk_near = early[:, :dev_rows], early[:, dev_rows:]
        proj_far = swap(proj_near, "dp", 1)
        order = jnp.concatenate([order, jnp.bitwise_xor(order, 1)])
        places = jnp.bitwise_xor(order, dp)
        proj_parts = [proj_near.astype(F32), proj_far.astype(F32)]
        hid_send = after(hid_send, proj_far)
    else:
        sk_own = early[:, dev_rows:]
        proj_parts = [early[:, :dev_rows].reshape(1, mp_rows, rank).astype(F32)]
        places = jnp.zeros((1,), jnp.int32)
    x_half, y_own, core_half, hid_t, hid_own, weights_2d = (
        lax.optimization_barrier(
            (
                x_part,
                y_part,
                core_half,
                hid_t,
                hid_own,
                weights_2d,
            )
        )
    )
    own = [cotangent, core_half, x_half, swap(x_half, "mp", 1)]
    y_x = swap(y_own, "mp", 2)
    y_core = swap(y_own, "mp", 1)
    hid_got = swap(hid_send, "dp", 1)
    pattern_rel = jnp.bitwise_xor(pattern, mp * per_shard)

    def place(block):
        if width < blk:
            return jnp.bitwise_xor(block, mp * per_shard)
        per = width // blk
        shard, rest = block // per, block % per
        near_mp = jnp.bitwise_xor(shard % n_mp, mp)
        return (near_mp * n_dp + shard // n_mp) * per + rest

    pat_all = pattern_rel.reshape(-1)
    partial_c = pl.pallas_call(
        functools.partial(
            compress_kernel,
            n_mp,
            per_shard,
            1.0 / (PROJ_SCALE * all_tokens),
            per_step,
        ),
        grid_spec=pltpu.PrefetchScalarGridSpec(
            num_scalar_prefetch=3,
            grid=(block_rows // per_step,),
            in_specs=[ANY] * n_mp
            + [pl.BlockSpec((per_step * blk, tok_rows), lambda i, a, b, c: (i, 0))]
            + [ANY] * len(proj_parts),
            out_specs=pl.BlockSpec((col_blocks, rank, blk), lambda i, a, b, c: (0, 0, 0)),
            scratch_shapes=[
                pltpu.VMEM((n_mp, tok_rows, shard_cols), BF),
                pltpu.VMEM((mp_rows, rank), F32),
                pltpu.SemaphoreType.DMA((n_mp + len(places),)),
            ],
        ),
        out_shape=jax.ShapeDtypeStruct((col_blocks, rank, blk), F32),
        compiler_params=params(),
        cost_estimate=SMALL,
        name="compress",
    )(pat_all, place(pattern).reshape(-1), places, *own, hid_t, *proj_parts)

    partial_c, y_x, y_core, hid_got = lax.optimization_barrier((partial_c, y_x, y_core, hid_got))
    y_group = [y_own, y_core, y_x, swap(y_x, "mp", 1)]
    if n_dp <= 8:
        sk_own = jnp.concatenate([sk_near, swap(after(sk_near, hid_got), "dp", 1)], axis=0)
        far = jnp.bitwise_xor(jnp.arange(n_dp, dtype=jnp.int32), dp)
        at = jnp.where(jnp.bitwise_and(far, 1) == 1, n_dp // 2, 0) + far // 2
        sk_own = jnp.take(sk_own, at, axis=0, mode="clip")
    if width < blk:
        sk_own = sk_own.reshape(n_dp, rank, width)
    else:
        sk_own = sk_own.reshape(per_shard, rank, blk)
    quarters = partial_c.reshape(n_mp, per_shard, rank, blk)
    to_far, to_near = quarters[3].astype(F16), quarters[1].astype(F16)
    got_far, got_near = swap(to_far, "mp", 1), swap(to_near, "mp", 1)
    y_group[3] = after(y_group[3], to_far, to_near)

    half_rows = outer * dev_rows
    devices = 2 * jnp.arange(outer, dtype=jnp.int32) + side
    window, _, _ = windows_of(dp * dev_rows, dev_rows, blk)
    window_starts, window_blocks = jax.vmap(lambda d: windows_of(d * dev_rows, dev_rows, blk)[1:])(
        devices
    )
    n_windows = window_starts.shape[1]
    pat_half = jnp.take(pattern_rel, window_blocks.reshape(-1), axis=0).reshape(-1)
    hid_type = BF if window % 32 == 0 else F32

    def pair_grad(blocks, shards):
        order = jnp.bitwise_xor(jnp.asarray(blocks, jnp.int32), dp // 2)
        out, top = pl.pallas_call(
            functools.partial(grad_kernel, n_mp, per_shard, blk, window, n_windows),
            grid_spec=pltpu.PrefetchScalarGridSpec(
                num_scalar_prefetch=3,
                grid=(len(blocks),),
                in_specs=[ANY] * (2 * n_mp)
                + [pl.BlockSpec((dev_rows, tok_rows), lambda i, o, a, b: (o[i], 0))] * 2,
                out_specs=[
                    pl.BlockSpec((dev_rows, slots * blk), lambda i, o, a, b: (i, 0)),
                    pl.BlockSpec((8, 2 * blk), lambda i, o, a, b: (0, 0)),
                ],
                scratch_shapes=[
                    pltpu.VMEM((n_mp, 2 * tok_rows, shard_cols), BF),
                    pltpu.SemaphoreType.DMA((2 * n_mp,)),
                ],
            ),
            out_shape=[
                jax.ShapeDtypeStruct((len(blocks) * dev_rows, slots * blk), F32),
                jax.ShapeDtypeStruct((8, 2 * blk), F32),
            ],
            compiler_params=params(),
            cost_estimate=SMALL,
            name="pair_grad",
        )(
            order,
            window_starts.reshape(-1),
            pat_half,
            *shards,
            hid_own.reshape(half_rows, tok_rows).astype(hid_type),
            hid_got.reshape(half_rows, tok_rows).astype(hid_type),
        )
        out = out.reshape(len(blocks), dev_rows, slots * blk)
        top = jnp.max(top)
        return {block: (out[i], top) for i, block in enumerate(blocks)}

    def pack(part):
        value, top = part
        exponent = 13.0 - jnp.floor(jnp.log2(jnp.maximum(top, 1e-30)))
        below = jnp.broadcast_to(exponent, (16, value.shape[1]))
        return jnp.concatenate([value * jnp.exp2(exponent), below], axis=0).astype(F16)

    def unpack(message, first=0):
        below = lax.dynamic_slice(message, (dev_rows + first, 0), (8, message.shape[1]))
        exponent = below[:1].astype(F32)
        value = message[:dev_rows].astype(F32) * jnp.exp2(-exponent)
        return value, jnp.exp2(14.0 - jnp.max(exponent))

    def add(part, message, first=0):
        value, top = unpack(message, first)
        return part[0] + value, part[1] + top

    crossing = [i for i in range(outer) if i & 2][::-1]
    staying = [i for i in range(outer) if not i & 2][::-1]
    sums = pair_grad(crossing, own + y_group)
    sent = {i: pack(sums[i]) for i in crossing if i & 1}
    got_far, got_near, *before = lax.optimization_barrier((got_far, got_near, *sent.values()))
    sent = dict(zip(sent, before))
    got = {i: swap(sent[i], "dp", 2) for i in sent}
    far_half = (quarters[2] + got_far.astype(F32)).astype(F16)
    near_half = quarters[0] + got_near.astype(F32)
    far_half, near_half, y_group[3] = lax.optimization_barrier((far_half, near_half, y_group[3]))
    far_sum = swap(far_half, "mp", 2)
    sums.update(pair_grad(staying, own + y_group))
    sent = {i: pack(sums[i]) for i in staying if i & 1}
    got.update({i: swap(sent[i], "dp", 2) for i in staying if i & 1})
    far_sum, near_half, _ = lax.optimization_barrier((far_sum, near_half, list(sent.values())))

    quarter = near_half + far_sum.astype(F32)
    pieces = quarter.astype(F16).reshape(n_dp, per_shard * rank // n_dp, blk)
    if outer == 4:
        pieces, got[3] = lax.optimization_barrier((pieces, got[3]))
    pieces = lax.all_to_all(pieces, "dp", 0, 0)

    last = [got.pop(1)]
    level = 1
    while level < outer:
        if level > 1:
            got = {i: swap(pack(sums[i]), "dp", 2 * level) for i in sums if i & level}
        for i in got:
            sums[i ^ level] = add(sums[i ^ level], got[i])
        sums = {i: part for i, part in sums.items() if not i & level}
        if outer == 4:
            crossed, pieces = lax.optimization_barrier((pack(sums[2]), pieces))
            last.append(swap(crossed, "dp", 4))
            break
        level *= 2


    piece = jnp.sum(pieces.astype(F32), axis=0).astype(F16)
    quarter16 = over_dp(piece).reshape(per_shard, rank, blk)

    sk_own = after(sk_own, quarter)
    sk_far = swap(sk_own, "mp", 2)
    sk_parts = [sk_own, swap(sk_own, "mp", 1), sk_far, swap(sk_far, "mp", 1)]
    if width < blk:
        sk_abs = jnp.take(
            jnp.stack(sk_parts), jnp.bitwise_xor(jnp.arange(n_mp, dtype=jnp.int32), mp), axis=0
        )
        sk_abs = sk_abs.reshape(n_mp, col_blocks, blk // width // n_mp, rank, width)
        sk_abs = sk_abs.transpose(1, 3, 2, 0, 4).reshape(n_mp, per_shard, rank, blk)
        sk_parts = [
            lax.dynamic_index_in_dim(sk_abs, jnp.bitwise_xor(mp, i), 0, keepdims=False)
            for i in range(n_mp)
        ]
    oh, ol = split2_xla(sk_parts[0].astype(F32))
    sk_high, sk_low = split2_xla(jnp.concatenate(sk_parts, axis=0).astype(F32))

    sk_per = sk_high.shape[2] // blk
    sketch_gram = pl.pallas_call(
        sketch_gram_kernel,
        in_specs=[VMEM] * 2,
        out_specs=VMEM,
        out_shape=jax.ShapeDtypeStruct((rank, rank), F32),
        compiler_params=params(),
        cost_estimate=SMALL,
        name="sketch_gram",
    )(sk_high, sk_low)
    quarter16, sketch_gram, sk_high, sk_low, oh, ol = lax.optimization_barrier(
        (quarter16, sketch_gram, sk_high, sk_low, oh, ol)
    )
    qh, ql = split2_xla(quarter16.astype(F32))
    cross = pl.pallas_call(
        cross_gram_kernel,
        in_specs=[VMEM] * 4,
        out_specs=VMEM,
        out_shape=jax.ShapeDtypeStruct((rank, 2 * rank), F32),
        compiler_params=params(),
        cost_estimate=SMALL,
        name="cross_gram",
    )(qh, ql, oh, ol)
    cross = cross + swap(cross, "mp", 2)
    cross = cross + swap(cross, "mp", 1)
    input_grad = pl.pallas_call(
        functools.partial(input_grad_kernel, n_mp, per_shard, blk, per_step),
        grid_spec=pltpu.PrefetchScalarGridSpec(
            num_scalar_prefetch=1,
            grid=(block_rows // per_step,),
            in_specs=[ANY] * n_mp
            + [pl.BlockSpec((per_step * blk, slots * blk), lambda i, pat: (i, 0))],
            out_specs=pl.BlockSpec((tok_rows, per_step * blk), lambda i, pat: (0, i)),
            scratch_shapes=[
                pltpu.VMEM((n_mp, tok_rows, shard_cols), BF),
                pltpu.SemaphoreType.DMA((n_mp,)),
            ],
        ),
        out_shape=jax.ShapeDtypeStruct((tok_rows, mp_rows), BF),
        compiler_params=params(),
        cost_estimate=SMALL,
        name="input_grad",
    )(pat_all, *own, after(weights_2d, cross))
    cross, input_grad = lax.optimization_barrier((cross, input_grad))
    mixing = pl.pallas_call(
        mixing_kernel,
        in_specs=[VMEM] * 2,
        out_specs=VMEM,
        out_shape=jax.ShapeDtypeStruct((2 * rank, 2 * rank), F32),
        compiler_params=params(),
        cost_estimate=SMALL,
        name="mixing",
    )(sketch_gram, cross)

    quarter16 = after(quarter16, cross)
    far = swap(quarter16, "mp", 2)
    comp_parts = [quarter16, swap(quarter16, "mp", 1), far, swap(far, "mp", 1)]
    comp_parts = [split2_xla(part.astype(F32)) for part in comp_parts]
    comp_parts = [part[0] for part in comp_parts] + [part[1] for part in comp_parts]

    kept, mixing, first = lax.optimization_barrier((sums[0], mixing, jnp.int32(0)))
    for message in last:
        kept = add(kept, message, first)
    grad = kept[0] * (1.0 / all_tokens)
    _, my_starts, my_blocks = windows_of(dp * dev_rows, dev_rows, blk)
    my_pat = jnp.take(place(pattern), my_blocks, axis=0).reshape(-1)
    smem = pl.BlockSpec(memory_space=pltpu.SMEM)
    direction = pl.pallas_call(
        functools.partial(direction_kernel, sk_per, window, n_windows),
        in_specs=[smem] * 2 + [VMEM] * 4 + [ANY] * len(comp_parts),
        out_specs=VMEM,
        out_shape=jax.ShapeDtypeStruct((dev_rows, slots, blk), F32),
        scratch_shapes=[
            pltpu.VMEM((col_blocks, rank, blk), BF),
            pltpu.VMEM((col_blocks, rank, blk), BF),
            pltpu.SemaphoreType.DMA((len(comp_parts),)),
        ],
        compiler_params=params(),
        cost_estimate=SMALL,
        name="direction",
    )(my_starts, my_pat, grad, mixing, sk_high, sk_low, *comp_parts)
    return (input_grad, direction.reshape(1, dev_rows, slots, blk))


def solution(mesh):
    return jax.shard_map(
        per_device,
        mesh=mesh,
        in_specs=(
            P("mp", None, None),
            P("dp", "mp"),
            P("dp", "mp"),
            P(None, ("dp", "mp")),
            P(None, "mp", "dp"),
            P("mp", None),
        ),
        out_specs=(P("dp", "mp"), P("mp", "dp", None, None)),
        check_vma=False,
    )
```

```python
import functools
import math

import jax
import jax.numpy as jnp
from jax import lax
from jax.experimental import pallas as pl
from jax.experimental.pallas import tpu as pltpu
from jax.sharding import PartitionSpec as P

NS_STEPS = 5
SHIFT_EPS = 0.0001
PROJ_SCALE = 1024.0
SLOTS = 8

BF = jnp.bfloat16
F16 = jnp.float16
F32 = jnp.float32
HIGHEST = lax.Precision.HIGHEST
VMEM = pl.BlockSpec(memory_space=pltpu.VMEM)
ANY = pl.BlockSpec(memory_space=pl.ANY)


SMALL = pl.CostEstimate(flops=1, bytes_accessed=1, transcendentals=0)


def params(mib=48):
    return pltpu.CompilerParams(vmem_limit_bytes=mib * 1024 * 1024)


def dot(a, b):
    return jnp.dot(a, b, preferred_element_type=F32)


def dot_nt(a, b):
    return lax.dot_general(a, b, (((1,), (1,)), ((), ())), preferred_element_type=F32)


def split2(value):
    high = value.astype(BF)
    return high, (value - high.astype(F32)).astype(BF)


def split2_xla(value):
    high = lax.reduce_precision(value, exponent_bits=8, mantissa_bits=7)
    return high.astype(BF), (value - high).astype(BF)


def load_all(pairs, sems):
    copies = [pltpu.make_async_copy(src, dst, sems.at[i]) for i, (src, dst) in enumerate(pairs)]
    for copy in copies:
        copy.start()
    for copy in copies:
        copy.wait()


def column_block(held, block, per_shard, size):
    shard = block // per_shard
    offset = pl.multiple_of((block - shard * per_shard) * size, size)
    return held[shard, :, pl.ds(offset, size)]


def compress_kernel(n_shards, per_shard, scale, per_step, pat, pat_out, places, *refs):
    shards = refs[:n_shards]
    hid_ref, *proj_refs, out_ref, held, proj, sems = refs[n_shards:]
    blk = out_ref.shape[1]

    @pl.when(pl.program_id(0) == 0)
    def _():
        loads = [(ref, held.at[i]) for i, ref in enumerate(shards)]
        for ref in proj_refs:
            part_rows = ref.shape[1]
            for i in range(ref.shape[0]):
                place = places[len(loads) - n_shards]
                rows = pl.ds(pl.multiple_of(place * part_rows, 8), part_rows)
                loads.append((ref.at[i], proj.at[rows]))
        load_all(loads, sems)
        out_ref[...] = jnp.zeros_like(out_ref)

    first = pl.program_id(0) * per_step
    lefts = []
    for u in range(per_step):
        span = slice(u * blk, (u + 1) * blk)
        hid = hid_ref[span, :]
        rows = pl.ds(pl.multiple_of((first + u) * blk, blk), blk)
        ph, pl_ = split2(proj[rows, :].T)
        lefts.append(((dot(ph, hid) + dot(pl_, hid)) * scale).astype(BF))
    parts = []
    for u in range(per_step):
        cols = [pat[(first + u) * SLOTS + j] for j in range(SLOTS)]
        for j in range(0, SLOTS, 2):
            chosen = jnp.concatenate(
                [column_block(held, c, per_shard, blk) for c in cols[j : j + 2]], axis=1
            )
            parts.append(dot(lefts[u], chosen))
    for u in range(per_step):
        outs = [pat_out[(first + u) * SLOTS + j] for j in range(SLOTS)]
        sums = [
            out_ref[c] + parts[(u * SLOTS + j) // 2][:, (j % 2) * blk : (j % 2 + 1) * blk]
            for j, c in enumerate(outs)
        ]
        for c, total in zip(outs, sums):
            out_ref[c] = total


def grad_kernel(n_shards, per_shard, blk, window, n_windows, order, starts, pat, *refs):
    shards = refs[: 2 * n_shards]
    own_ref, got_ref, out_ref, top_ref, held, sems = refs[2 * n_shards :]
    toks = own_ref.shape[1]

    @pl.when(pl.program_id(0) == 0)
    def _():
        load_all(
            [
                (ref, held.at[i % n_shards, pl.ds(i // n_shards * toks, toks)])
                for i, ref in enumerate(shards)
            ],
            sems,
        )
        top_ref[...] = jnp.zeros_like(top_ref)

    top = top_ref[...]
    for w in range(n_windows):
        index = order[pl.program_id(0)] * n_windows + w
        rows = pl.ds(pl.multiple_of(starts[index], window // 2 if window >= 32 else 8), window)
        hid = jnp.concatenate([own_ref[rows, :], got_ref[rows, :]], axis=1).astype(BF)
        for j in range(0, SLOTS, 2):
            chosen = jnp.concatenate(
                [column_block(held, pat[index * SLOTS + j + i], per_shard, blk) for i in (0, 1)],
                axis=1,
            )
            part = dot(hid, chosen)
            out_ref[rows, j * blk : (j + 2) * blk] = part
            size = jnp.abs(part)
            for i in range(0, window, 8):
                top = jnp.maximum(top, size[i : i + 8])
    top_ref[...] = top


def input_grad_kernel(n_shards, per_shard, blk, per_step, pat, *refs):
    shards = refs[:n_shards]
    w_ref, out_ref, held, sems = refs[n_shards:]

    @pl.when(pl.program_id(0) == 0)
    def _():
        load_all([(ref, held.at[i]) for i, ref in enumerate(shards)], sems)

    for u in range(per_step):
        row = pl.program_id(0) * per_step + u
        chosen = jnp.concatenate(
            [column_block(held, pat[row * SLOTS + j], per_shard, blk) for j in range(SLOTS)], axis=1
        )
        span = slice(u * blk, (u + 1) * blk)
        out_ref[:, span] = dot_nt(chosen, w_ref[span, :]).astype(BF)


def sketch_gram_kernel(sh_ref, sl_ref, out_ref):
    out_ref[...] = jnp.zeros_like(out_ref)
    for s in range(sh_ref.shape[0]):
        high, low = sh_ref[s], sl_ref[s]
        out_ref[...] += dot_nt(high, high) + (dot_nt(high, low) + dot_nt(low, high))


def cross_gram_kernel(ch_ref, cl_ref, sh_ref, sl_ref, out_ref):
    rank = ch_ref.shape[1]
    per = ch_ref.shape[0] // sh_ref.shape[0]
    with_sketch = jnp.zeros((rank, rank), F32)
    with_self = jnp.zeros((rank, rank), F32)
    for s in range(sh_ref.shape[0]):
        high = jnp.concatenate([ch_ref[per * s + b] for b in range(per)], axis=1)
        low = jnp.concatenate([cl_ref[per * s + b] for b in range(per)], axis=1)
        sh, sl = sh_ref[s], sl_ref[s]
        with_sketch += dot_nt(high, sh) + (dot_nt(high, sl) + dot_nt(low, sh))
        with_self += dot_nt(high, high) + (dot_nt(high, low) + dot_nt(low, high))
    out_ref[:, :rank] = with_sketch
    out_ref[:, rank:] = with_self


def mixing_kernel(ss_ref, cross_ref, out_ref):
    rank = ss_ref.shape[0]
    size = 2 * rank
    sqrt_eps = math.sqrt(SHIFT_EPS)

    def mm(a, b):
        return jnp.dot(a, b, precision=HIGHEST, preferred_element_type=F32)

    cross = cross_ref[...]
    gram = jnp.concatenate(
        [jnp.concatenate([ss_ref[...], cross[:, :rank].T], axis=1), cross], axis=0
    )
    rows = lax.broadcasted_iota(jnp.int32, (size, size), 0)
    cols = lax.broadcasted_iota(jnp.int32, (size, size), 1)
    identity = jnp.where(rows == cols, 1.0, 0.0).astype(F32)
    shifted = gram + SHIFT_EPS * identity
    frobenius = jnp.sqrt(jnp.sum(shifted * shifted, keepdims=True))
    root = shifted / frobenius
    inverse = identity
    for step in range(NS_STEPS):
        product = root if step == 0 else mm(inverse, root)
        middle = 0.5 * (3.0 * identity - product)
        root = mm(root, middle)
        inverse = middle if step == 0 else mm(middle, inverse)
    sqrt_fro = jnp.sqrt(frobenius)
    half = 0.5 * sqrt_fro * (root + root.T) + sqrt_eps * identity
    guess = inverse / (sqrt_fro + sqrt_eps * 1.5**NS_STEPS)

    def residual(x):
        r = identity - mm(half, x)
        return r, jnp.max(jnp.abs(r))

    def keep_going(state):
        return jnp.logical_and(state[3] < 48, state[2] > 2e-6)

    def improve(state):
        x, r, _, count = state
        x = x + mm(x, r)
        r, size = residual(x)
        return x, r, size, count + 1

    r, top = residual(guess)
    x, r, _, _ = lax.while_loop(keep_going, improve, (guess, r, top, jnp.int32(0)))
    x = x + mm(x, r)
    out_ref[...] = -mm(inverse, x) / (sqrt_eps * sqrt_fro)


def direction_kernel(per, window, n_windows, starts, pat, *refs):
    g_ref, m_ref, skh, skl = refs[:4]
    parts, (out_ref, cph, cpl, sems) = refs[4:-4], refs[-4:]
    blk = cph.shape[2]
    half = len(parts) // 2
    pairs, at = [], 0
    for i in range(half):
        size = parts[i].shape[0]
        pairs += [(parts[i], cph.at[pl.ds(at, size)]), (parts[half + i], cpl.at[pl.ds(at, size)])]
        at += size
    load_all(pairs, sems)

    def gathered(sk, cp, c):
        shard = c // per
        offset = pl.multiple_of((c - shard * per) * blk, blk)
        return jnp.concatenate([sk[shard, :, pl.ds(offset, blk)], cp[c]], axis=0)

    for w in range(n_windows):
        rows = pl.ds(pl.multiple_of(starts[w], window // 2 if window >= 32 else 8), window)
        cols = [pat[w * SLOTS + k] for k in range(SLOTS)]
        g = g_ref[rows, :]
        g_high = g.astype(BF).astype(F32)
        g_both = jnp.concatenate([g_high, g - g_high], axis=0).astype(BF)
        high = [gathered(skh, cph, c) for c in cols]
        low = [gathered(skl, cpl, c) for c in cols]
        both = dot_nt(g_both, jnp.concatenate(high, axis=1))
        projected = both[:window] + both[window:]
        projected += dot_nt(g_high.astype(BF), jnp.concatenate(low, axis=1))
        mixed = jnp.dot(projected, m_ref[...], precision=HIGHEST, preferred_element_type=F32)
        mixed_high = mixed.astype(BF).astype(F32)
        mixed_both = jnp.concatenate([mixed_high, mixed - mixed_high], axis=0).astype(BF)
        for k in range(0, SLOTS, 2):
            both = dot(mixed_both, jnp.concatenate(high[k : k + 2], axis=1))
            corr = both[:window] + both[window:]
            corr += dot(mixed_high.astype(BF), jnp.concatenate(low[k : k + 2], axis=1))
            corr += g[:, k * blk : (k + 2) * blk] * (1.0 / math.sqrt(SHIFT_EPS))
            out_ref[rows, k, :] = corr[:, :blk]
            out_ref[rows, k + 1, :] = corr[:, blk:]


def windows_of(start, dev_rows, blk):
    group = math.gcd(dev_rows, blk)
    if dev_rows % blk == blk // 2 and dev_rows > blk:
        whole = dev_rows // blk
        odd = (start // group) % 2
        later = odd * group + blk * jnp.arange(whole, dtype=jnp.int32)
        first = jnp.where(odd == 1, 0, dev_rows - blk)
        first_row = jnp.where(odd == 1, start, start + dev_rows - group)
        starts = jnp.concatenate([first[None], later])
        inside = jnp.concatenate([first_row[None], start + later])
        return blk, starts.astype(jnp.int32), (inside // blk).astype(jnp.int32)
    starts = group * jnp.arange(dev_rows // group, dtype=jnp.int32)
    return group, starts, (start + starts) // blk


def per_device(weights, hidden, cotangent, sketch, projection, pattern):
    tok_rows = hidden.shape[0]
    mp_rows, slots, blk = weights.shape
    block_rows = mp_rows // blk
    n_dp, n_mp = lax.axis_size("dp"), lax.axis_size("mp")
    dev_rows = mp_rows // n_dp
    all_tokens = tok_rows * n_dp
    rank = sketch.shape[0]
    shard_cols = cotangent.shape[1]
    per_shard = shard_cols // blk
    col_blocks = per_shard * n_mp
    outer = n_dp // 2
    per_step = 7 if block_rows % 7 == 0 else 1
    dp, mp = lax.axis_index("dp"), lax.axis_index("mp")
    side = dp % 2

    def swap(x, axis, bit):
        size = lax.axis_size(axis)
        return lax.ppermute(x, axis, [(i, i ^ bit) for i in range(size)])

    def after(x, *others):
        return lax.optimization_barrier((x, *others))[0]

    def over_dp(x):
        return lax.all_to_all(jnp.broadcast_to(x[None], (n_dp, *x.shape)), "dp", 0, 0)

    width = sketch.shape[1]
    core_half = swap(cotangent, "mp", 1)
    proj_t = (projection.reshape(rank, dev_rows).T * PROJ_SCALE).astype(F16)
    if width < blk:
        sk_rows = sketch.reshape(width, rank)
    else:
        sk_rows = sketch.reshape(rank, width // blk, blk).swapaxes(0, 1).reshape(-1, blk)
    early = jnp.concatenate([proj_t, sk_rows.astype(F16)], axis=0)
    early, order = early[None], jnp.zeros((1,), jnp.int32)
    bits = [1 << i for i in range(1, n_dp.bit_length() - 1)]
    if n_dp > 8:
        early, order, bits = over_dp(early[0]), jnp.arange(n_dp, dtype=jnp.int32), []
    hidden_in, weights_in = hidden, weights
    x_part, y_part = swap(cotangent, "mp", 2), swap(cotangent, "dp", 1)
    for bit in bits:
        early = jnp.concatenate([early, swap(early, "dp", bit)], axis=0)
        order = jnp.concatenate([order, jnp.bitwise_xor(order, bit)])
        if bit == 2:
            early, hidden_in, weights_in = lax.optimization_barrier((early, hidden, weights))
    hid_t = hidden_in.T
    hid_parts = hid_t.reshape(outer, 2, dev_rows, tok_rows)
    hid_own = lax.dynamic_index_in_dim(hid_parts, side, 1, keepdims=False)
    hid_send = lax.dynamic_index_in_dim(hid_parts, 1 - side, 1, keepdims=False)
    weights_2d = weights_in.reshape(mp_rows, slots * blk)
    if n_dp <= 8:
        early, hid_own, hid_send, weights_2d, x_part, y_part = lax.optimization_barrier(
            (early, hid_own, hid_send, weights_2d, x_part, y_part)
        )
        proj_near, sk_near = early[:, :dev_rows], early[:, dev_rows:]
        proj_far = swap(proj_near, "dp", 1)
        order = jnp.concatenate([order, jnp.bitwise_xor(order, 1)])
        places = jnp.bitwise_xor(order, dp)
        proj_parts = [proj_near.astype(F32), proj_far.astype(F32)]
        hid_send = after(hid_send, proj_far)
    else:
        sk_own = early[:, dev_rows:]
        proj_parts = [early[:, :dev_rows].reshape(1, mp_rows, rank).astype(F32)]
        places = jnp.zeros((1,), jnp.int32)
    x_half, y_own, core_half, hid_t, hid_own, weights_2d = (
        lax.optimization_barrier(
            (
                x_part,
                y_part,
                core_half,
                hid_t,
                hid_own,
                weights_2d,
            )
        )
    )
    own = [cotangent, core_half, x_half, swap(x_half, "mp", 1)]
    y_x = swap(y_own, "mp", 2)
    y_core = swap(y_own, "mp", 1)
    hid_got = swap(hid_send, "dp", 1)
    pattern_rel = jnp.bitwise_xor(pattern, mp * per_shard)

    def place(block):
        if width < blk:
            return jnp.bitwise_xor(block, mp * per_shard)
        per = width // blk
        shard, rest = block // per, block % per
        near_mp = jnp.bitwise_xor(shard % n_mp, mp)
        return (near_mp * n_dp + shard // n_mp) * per + rest

    pat_all = pattern_rel.reshape(-1)
    partial_c = pl.pallas_call(
        functools.partial(
            compress_kernel,
            n_mp,
            per_shard,
            1.0 / (PROJ_SCALE * all_tokens),
            per_step,
        ),
        grid_spec=pltpu.PrefetchScalarGridSpec(
            num_scalar_prefetch=3,
            grid=(block_rows // per_step,),
            in_specs=[ANY] * n_mp
            + [pl.BlockSpec((per_step * blk, tok_rows), lambda i, a, b, c: (i, 0))]
            + [ANY] * len(proj_parts),
            out_specs=pl.BlockSpec((col_blocks, rank, blk), lambda i, a, b, c: (0, 0, 0)),
            scratch_shapes=[
                pltpu.VMEM((n_mp, tok_rows, shard_cols), BF),
                pltpu.VMEM((mp_rows, rank), F32),
                pltpu.SemaphoreType.DMA((n_mp + len(places),)),
            ],
        ),
        out_shape=jax.ShapeDtypeStruct((col_blocks, rank, blk), F32),
        compiler_params=params(),
        cost_estimate=SMALL,
        name="compress",
    )(pat_all, place(pattern).reshape(-1), places, *own, hid_t, *proj_parts)

    partial_c, y_x, y_core, hid_got = lax.optimization_barrier((partial_c, y_x, y_core, hid_got))
    y_group = [y_own, y_core, y_x, swap(y_x, "mp", 1)]
    if n_dp <= 8:
        sk_own = jnp.concatenate([sk_near, swap(after(sk_near, hid_got), "dp", 1)], axis=0)
        far = jnp.bitwise_xor(jnp.arange(n_dp, dtype=jnp.int32), dp)
        at = jnp.where(jnp.bitwise_and(far, 1) == 1, n_dp // 2, 0) + far // 2
        sk_own = jnp.take(sk_own, at, axis=0, mode="clip")
    if width < blk:
        sk_own = sk_own.reshape(n_dp, rank, width)
    else:
        sk_own = sk_own.reshape(per_shard, rank, blk)
    quarters = partial_c.reshape(n_mp, per_shard, rank, blk)
    to_far, to_near = quarters[3].astype(F16), quarters[1].astype(F16)
    got_far, got_near = swap(to_far, "mp", 1), swap(to_near, "mp", 1)
    y_group[3] = after(y_group[3], to_far, to_near)

    half_rows = outer * dev_rows
    devices = 2 * jnp.arange(outer, dtype=jnp.int32) + side
    window, _, _ = windows_of(dp * dev_rows, dev_rows, blk)
    window_starts, window_blocks = jax.vmap(lambda d: windows_of(d * dev_rows, dev_rows, blk)[1:])(
        devices
    )
    n_windows = window_starts.shape[1]
    pat_half = jnp.take(pattern_rel, window_blocks.reshape(-1), axis=0).reshape(-1)
    hid_type = BF if window % 32 == 0 else F32

    def pair_grad(blocks, shards):
        order = jnp.bitwise_xor(jnp.asarray(blocks, jnp.int32), dp // 2)
        out, top = pl.pallas_call(
            functools.partial(grad_kernel, n_mp, per_shard, blk, window, n_windows),
            grid_spec=pltpu.PrefetchScalarGridSpec(
                num_scalar_prefetch=3,
                grid=(len(blocks),),
                in_specs=[ANY] * (2 * n_mp)
                + [pl.BlockSpec((dev_rows, tok_rows), lambda i, o, a, b: (o[i], 0))] * 2,
                out_specs=[
                    pl.BlockSpec((dev_rows, slots * blk), lambda i, o, a, b: (i, 0)),
                    pl.BlockSpec((8, 2 * blk), lambda i, o, a, b: (0, 0)),
                ],
                scratch_shapes=[
                    pltpu.VMEM((n_mp, 2 * tok_rows, shard_cols), BF),
                    pltpu.SemaphoreType.DMA((2 * n_mp,)),
                ],
            ),
            out_shape=[
                jax.ShapeDtypeStruct((len(blocks) * dev_rows, slots * blk), F32),
                jax.ShapeDtypeStruct((8, 2 * blk), F32),
            ],
            compiler_params=params(),
            cost_estimate=SMALL,
            name="pair_grad",
        )(
            order,
            window_starts.reshape(-1),
            pat_half,
            *shards,
            hid_own.reshape(half_rows, tok_rows).astype(hid_type),
            hid_got.reshape(half_rows, tok_rows).astype(hid_type),
        )
        out = out.reshape(len(blocks), dev_rows, slots * blk)
        top = jnp.max(top)
        return {block: (out[i], top) for i, block in enumerate(blocks)}

    def pack(part):
        value, top = part
        exponent = 13.0 - jnp.floor(jnp.log2(jnp.maximum(top, 1e-30)))
        below = jnp.broadcast_to(exponent, (16, value.shape[1]))
        return jnp.concatenate([value * jnp.exp2(exponent), below], axis=0).astype(F16)

    def unpack(message, first=0):
        below = lax.dynamic_slice(message, (dev_rows + first, 0), (8, message.shape[1]))
        exponent = below[:1].astype(F32)
        value = message[:dev_rows].astype(F32) * jnp.exp2(-exponent)
        return value, jnp.exp2(14.0 - jnp.max(exponent))

    def add(part, message, first=0):
        value, top = unpack(message, first)
        return part[0] + value, part[1] + top

    crossing = [i for i in range(outer) if i & 2][::-1]
    staying = [i for i in range(outer) if not i & 2][::-1]
    sums = pair_grad(crossing, own + y_group)
    sent = {i: pack(sums[i]) for i in crossing if i & 1}
    got_far, got_near, *before = lax.optimization_barrier((got_far, got_near, *sent.values()))
    sent = dict(zip(sent, before))
    got = {i: swap(sent[i], "dp", 2) for i in sent}
    far_half = (quarters[2] + got_far.astype(F32)).astype(F16)
    near_half = quarters[0] + got_near.astype(F32)
    far_half, near_half, y_group[3] = lax.optimization_barrier((far_half, near_half, y_group[3]))
    far_sum = swap(far_half, "mp", 2)
    sums.update(pair_grad(staying, own + y_group))
    sent = {i: pack(sums[i]) for i in staying if i & 1}
    got.update({i: swap(sent[i], "dp", 2) for i in staying if i & 1})
    far_sum, near_half, _ = lax.optimization_barrier((far_sum, near_half, list(sent.values())))

    quarter = near_half + far_sum.astype(F32)
    pieces = quarter.astype(F16).reshape(n_dp, per_shard * rank // n_dp, blk)
    if outer == 4:
        pieces, got[3] = lax.optimization_barrier((pieces, got[3]))
    pieces = lax.all_to_all(pieces, "dp", 0, 0)

    last = [got.pop(1)]
    level = 1
    while level < outer:
        if level > 1:
            got = {i: swap(pack(sums[i]), "dp", 2 * level) for i in sums if i & level}
        for i in got:
            sums[i ^ level] = add(sums[i ^ level], got[i])
        sums = {i: part for i, part in sums.items() if not i & level}
        if outer == 4:
            crossed, pieces = lax.optimization_barrier((pack(sums[2]), pieces))
            last.append(swap(crossed, "dp", 4))
            break
        level *= 2


    piece = jnp.sum(pieces.astype(F32), axis=0).astype(F16)
    quarter16 = over_dp(piece).reshape(per_shard, rank, blk)

    sk_own = after(sk_own, quarter)
    sk_far = swap(sk_own, "mp", 2)
    sk_parts = [sk_own, swap(sk_own, "mp", 1), sk_far, swap(sk_far, "mp", 1)]
    if width < blk:
        sk_abs = jnp.take(
            jnp.stack(sk_parts), jnp.bitwise_xor(jnp.arange(n_mp, dtype=jnp.int32), mp), axis=0
        )
        sk_abs = sk_abs.reshape(n_mp, col_blocks, blk // width // n_mp, rank, width)
        sk_abs = sk_abs.transpose(1, 3, 2, 0, 4).reshape(n_mp, per_shard, rank, blk)
        sk_parts = [
            lax.dynamic_index_in_dim(sk_abs, jnp.bitwise_xor(mp, i), 0, keepdims=False)
            for i in range(n_mp)
        ]
    oh, ol = split2_xla(sk_parts[0].astype(F32))
    sk_high, sk_low = split2_xla(jnp.concatenate(sk_parts, axis=0).astype(F32))

    sk_per = sk_high.shape[2] // blk
    sketch_gram = pl.pallas_call(
        sketch_gram_kernel,
        in_specs=[VMEM] * 2,
        out_specs=VMEM,
        out_shape=jax.ShapeDtypeStruct((rank, rank), F32),
        compiler_params=params(),
        cost_estimate=SMALL,
        name="sketch_gram",
    )(sk_high, sk_low)
    quarter16, sketch_gram, sk_high, sk_low, oh, ol = lax.optimization_barrier(
        (quarter16, sketch_gram, sk_high, sk_low, oh, ol)
    )
    qh, ql = split2_xla(quarter16.astype(F32))
    cross = pl.pallas_call(
        cross_gram_kernel,
        in_specs=[VMEM] * 4,
        out_specs=VMEM,
        out_shape=jax.ShapeDtypeStruct((rank, 2 * rank), F32),
        compiler_params=params(),
        cost_estimate=SMALL,
        name="cross_gram",
    )(qh, ql, oh, ol)
    cross = cross + swap(cross, "mp", 2)
    cross = cross + swap(cross, "mp", 1)
    input_grad = pl.pallas_call(
        functools.partial(input_grad_kernel, n_mp, per_shard, blk, per_step),
        grid_spec=pltpu.PrefetchScalarGridSpec(
            num_scalar_prefetch=1,
            grid=(block_rows // per_step,),
            in_specs=[ANY] * n_mp
            + [pl.BlockSpec((per_step * blk, slots * blk), lambda i, pat: (i, 0))],
            out_specs=pl.BlockSpec((tok_rows, per_step * blk), lambda i, pat: (0, i)),
            scratch_shapes=[
                pltpu.VMEM((n_mp, tok_rows, shard_cols), BF),
                pltpu.SemaphoreType.DMA((n_mp,)),
            ],
        ),
        out_shape=jax.ShapeDtypeStruct((tok_rows, mp_rows), BF),
        compiler_params=params(),
        cost_estimate=SMALL,
        name="input_grad",
    )(pat_all, *own, after(weights_2d, cross))
    cross, input_grad = lax.optimization_barrier((cross, input_grad))
    mixing = pl.pallas_call(
        mixing_kernel,
        in_specs=[VMEM] * 2,
        out_specs=VMEM,
        out_shape=jax.ShapeDtypeStruct((2 * rank, 2 * rank), F32),
        compiler_params=params(),
        cost_estimate=SMALL,
        name="mixing",
    )(sketch_gram, cross)

    quarter16 = after(quarter16, cross)
    far = swap(quarter16, "mp", 2)
    comp_parts = [quarter16, swap(quarter16, "mp", 1), far, swap(far, "mp", 1)]
    comp_parts = [split2_xla(part.astype(F32)) for part in comp_parts]
    comp_parts = [part[0] for part in comp_parts] + [part[1] for part in comp_parts]

    kept, mixing, first = lax.optimization_barrier((sums[0], mixing, jnp.int32(0)))
    for message in last:
        kept = add(kept, message, first)
    grad = kept[0] * (1.0 / all_tokens)
    _, my_starts, my_blocks = windows_of(dp * dev_rows, dev_rows, blk)
    my_pat = jnp.take(place(pattern), my_blocks, axis=0).reshape(-1)
    smem = pl.BlockSpec(memory_space=pltpu.SMEM)
    direction = pl.pallas_call(
        functools.partial(direction_kernel, sk_per, window, n_windows),
        in_specs=[smem] * 2 + [VMEM] * 4 + [ANY] * len(comp_parts),
        out_specs=VMEM,
        out_shape=jax.ShapeDtypeStruct((dev_rows, slots, blk), F32),
        scratch_shapes=[
            pltpu.VMEM((col_blocks, rank, blk), BF),
            pltpu.VMEM((col_blocks, rank, blk), BF),
            pltpu.SemaphoreType.DMA((len(comp_parts),)),
        ],
        compiler_params=params(),
        cost_estimate=SMALL,
        name="direction",
    )(my_starts, my_pat, grad, mixing, sk_high, sk_low, *comp_parts)
    return (input_grad, direction.reshape(1, dev_rows, slots, blk))


def solution(mesh):
    return jax.shard_map(
        per_device,
        mesh=mesh,
        in_specs=(
            P("mp", None, None),
            P("dp", "mp"),
            P("dp", "mp"),
            P(None, ("dp", "mp")),
            P(None, "mp", "dp"),
            P("mp", None),
        ),
        out_specs=(P("dp", "mp"), P("mp", "dp", None, None)),
        check_vma=False,
    )
```
